32 devices in a mesh: gx: 4 (over y, x), gy: 4 (over z), gz: 2 (over core).
Axes of the slice: x: 2, y: 2, z: 4, core: 2. Of those that a mesh axis runs over, the one named last changes fastest.
Arguments:
- velocity: float32 [3, 8, 4, 8, 512], P(None, 'gx', 'gy', 'gz'), may hold values from -4 to 4
- reaction: float32 [8, 4, 8, 512], P('gx', 'gy', 'gz'), may hold values from 10 to 100
Outputs:
- velocity_out: float32 [3, 8, 4, 8, 512], P(None, 'gx', 'gy', 'gz')
- pressure: float32 [8, 4, 8, 512], P('gx', 'gy', 'gz')
- residual: float32 [8, 4, 8, 512], P('gx', 'gy', 'gz')
The draws below stay inside these ranges and needn't reach their ends.
All inputs are finite; a program needn't handle non-finite values.
Results may differ from the reference program's by a relative error of at most 0.007.
Values sent between devices are 32-bit elements; how exact they have to be, the bound alone decides.
No kernel may reach another device: no remote copies, remote signals or barrier semaphores. Data moves between devices by JAX's collectives and lax.ppermute only.
A program may use at most 64 MiB of HBM per device.

```python
import math
import jax
import jax.numpy as jnp
import numpy as np
from jax import lax

ELEMENT_NODES = 512
SUBSTEPS = 2
ITERS = 4
ELEMENTS_AXIAL = 8
ELEMENTS_CROSS = 4
ELEMENTS_DEPTH = 8


def level_of(stream_key, dims, pieces, low, largest):
    def one(dim, parts):
        steps = jax.random.uniform(jax.random.fold_in(jax.random.fold_in(stream_key, 6), dim), (parts,), jnp.float32, low / len(pieces), largest / len(pieces))
        return jnp.repeat(jnp.exp(steps), dims[dim] // parts).reshape((-1,) + (1,) * (len(dims) - dim - 1))

    level = one(*pieces[0])
    for cut in pieces[1:]:
        level = level * one(*cut)
    return level


def centred(rng, extent, width, reach, cuts=(), dtype=jnp.bfloat16):
    factor_of = level_of(rng, extent, cuts, -0.22, 0.18) if cuts else 1.0
    values = jax.random.normal(rng, extent, jnp.float32) * width * factor_of
    return jnp.minimum(jnp.maximum(values, -reach), reach).astype(dtype)


def setup_inputs(seed: int = 0) -> dict:
    key_of = jax.random.split(jax.random.key(seed), 3)
    return {
        "velocity": centred(key_of[0], (3, ELEMENTS_AXIAL, ELEMENTS_CROSS, ELEMENTS_DEPTH, ELEMENT_NODES), 1.0, 4.0, ((1, 4), (2, 4), (3, 2)), jnp.float32),
        "reaction": jnp.clip(jnp.exp(math.log(100.0) - 2.3025851 * jax.random.uniform(key_of[1], (ELEMENTS_AXIAL, ELEMENTS_CROSS, ELEMENTS_DEPTH, ELEMENT_NODES), jnp.float32) ** level_of(key_of[1], (ELEMENTS_AXIAL, ELEMENTS_CROSS, ELEMENTS_DEPTH, ELEMENT_NODES), ((0, 4), (1, 4), (2, 2)), -0.2, 0.2)), 10.0, 100.0),
    }


step_size = 0.02


def legendre_seven(points):
    earlier = points * 0.0 + 1.0
    current = points
    for degree in range(1, 7):
        earlier, current = current, ((2 * degree + 1) * points * current - degree * earlier) / (degree + 1)
    return current


def tables():
    half = np.array([0.2092992179024788687, 0.5917001814331423022, 0.8717401485096066153, 1.0])
    points = np.concatenate([-half[::-1], half])
    legendre = legendre_seven(points)
    weights = 2.0 / (56.0 * legendre ** 2)
    spacing = points[:, None] - points[None, :] + np.eye(8)
    derivative = (legendre[:, None] / legendre[None, :]) / spacing * (1.0 - np.eye(8))
    derivative[0, 0] = -14.0
    derivative[7, 7] = 14.0
    return jnp.asarray(weights, jnp.float32), jnp.asarray(derivative, jnp.float32)


def derive(values, derivative, along_dim, transposed):
    matrix = derivative.T if transposed else derivative
    layout = values.shape
    blocks = values.reshape(-1, 8, 8, 8)
    patterns = ("aq,nqbc->nabc", "bq,naqc->nabc", "cq,nabq->nabc")
    result = jnp.einsum(patterns[along_dim], matrix, blocks, precision=lax.Precision.HIGHEST)
    return result.reshape(layout)


def place_face(values, target_axis, position, update):
    selector = tuple(position if place == target_axis else slice(None) for place in range(values.ndim))
    return values.at[selector].set(update)


def join_faces(values, along_dim, periodic):
    lower_face = jnp.moveaxis(jnp.take(values, 0, axis=4 + along_dim), 1 + along_dim, 0)
    upper_face = jnp.moveaxis(jnp.take(values, 7, axis=4 + along_dim), 1 + along_dim, 0)
    elements = lower_face.shape[0]
    face_shape = lower_face.shape
    sequence = jnp.stack([lower_face, upper_face], axis=1).reshape(2 * elements, -1)
    if periodic:
        leading = sequence[-1:]
        trailing = sequence[:1]
    else:
        leading = jnp.zeros_like(sequence[:1])
        trailing = jnp.zeros_like(sequence[:1])
    padded = jnp.concatenate([leading, sequence, trailing], axis=0)
    paired = padded.reshape(elements + 1, 2, -1)
    totals = paired[:, 0] + paired[:, 1]
    new_lower = jnp.moveaxis(totals[:-1].reshape(face_shape), 0, 1 + along_dim)
    new_upper = jnp.moveaxis(totals[1:].reshape(face_shape), 0, 1 + along_dim)
    values = place_face(values, 4 + along_dim, 0, new_lower)
    return place_face(values, 4 + along_dim, 7, new_upper)


def assemble(values):
    values = join_faces(values, 0, True)
    values = join_faces(values, 1, False)
    return join_faces(values, 2, False)


def dim_factors(local_count, offset, total_count, bounded_by_walls):
    element_ids = offset + jnp.arange(local_count)
    node_ids = jnp.arange(8)
    at_end = (node_ids[None, :] == 0) | (node_ids[None, :] == 7)
    low_wall = (element_ids[:, None] == 0) & (node_ids[None, :] == 0)
    high_wall = (element_ids[:, None] == total_count - 1) & (node_ids[None, :] == 7)
    on_wall = (low_wall | high_wall) & bounded_by_walls
    shared = at_end & jnp.logical_not(on_wall)
    return jnp.where(shared, 2.0, 1.0).astype(jnp.float32), on_wall.astype(jnp.float32)


def reference(velocity, reaction):
    weights, derivative = tables()
    count_x, count_y, count_z = reaction.shape[0], reaction.shape[1], reaction.shape[2]
    speed = velocity.reshape(3, count_x, count_y, count_z, 8, 8, 8)
    react = reaction.reshape(1, count_x, count_y, count_z, 8, 8, 8)
    mass_matrix = weights[:, None, None] * weights[None, :, None] * weights[None, None, :]
    factor_x, wall_x = dim_factors(count_x, 0, count_x, False)
    factor_y, wall_y = dim_factors(count_y, 0, count_y, True)
    factor_z, wall_z = dim_factors(count_z, 0, count_z, True)
    multiplicity = (factor_x[None, :, None, None, :, None, None] * factor_y[None, None, :, None, None, :, None]
                    * factor_z[None, None, None, :, None, None, :])
    interior = ((1.0 - wall_y[None, None, :, None, None, :, None]) * (1.0 - wall_z[None, None, None, :, None, None, :]))
    speed = assemble(speed) / multiplicity
    for substep in range(SUBSTEPS):
        gradient_fields = [derive(speed, derivative, along_dim, False) for along_dim in range(3)]
        transport = speed[0:1] * gradient_fields[0] + speed[1:2] * gradient_fields[1] + speed[2:3] * gradient_fields[2]
        tendency = assemble(mass_matrix * transport) / (mass_matrix * multiplicity)
        speed = interior * (speed - step_size * tendency)
    spread = (derive(speed[0:1], derivative, 0, False) + derive(speed[1:2], derivative, 1, False)
              + derive(speed[2:3], derivative, 2, False))
    source = -assemble(mass_matrix * spread)
    stiff_sum = jnp.sum(weights[:, None] * derivative * derivative, axis=0)
    diag_local = (stiff_sum[:, None, None] * weights[None, :, None] * weights[None, None, :]
                  + weights[:, None, None] * stiff_sum[None, :, None] * weights[None, None, :]
                  + weights[:, None, None] * weights[None, :, None] * stiff_sum[None, None, :])
    diagonal = assemble(diag_local + react * mass_matrix)

    def apply_operator(search_vec):
        local_sum = react * mass_matrix * search_vec
        for along_dim in range(3):
            local_sum = local_sum + derive(mass_matrix * derive(search_vec, derivative, along_dim, False), derivative, along_dim, True)
        return assemble(local_sum)

    def inner_product(first, second):
        return jnp.sum(first * second / multiplicity)

    pressure = jnp.zeros_like(source)
    residual = source
    precond = residual / diagonal
    search = precond
    progress = inner_product(residual, precond)
    for sweep_index in range(ITERS):
        applied = apply_operator(search)
        step_length = progress / inner_product(search, applied)
        pressure = pressure + step_length * search
        residual = residual - step_length * applied
        precond = residual / diagonal
        progress_next = inner_product(residual, precond)
        search = precond + (progress_next / progress) * search
        progress = progress_next
    return (speed.reshape(3, count_x, count_y, count_z, 512),
            pressure.reshape(count_x, count_y, count_z, 512),
            residual.reshape(count_x, count_y, count_z, 512))
```

```python
import functools

import jax
import jax.numpy as jnp
import numpy as np
from jax import lax
from jax.experimental import pallas as pl
from jax.experimental.pallas import tpu as pltpu
from jax.sharding import PartitionSpec as P

SUBSTEPS = 2
ITERS = 4
step_size = 0.02

F32 = jnp.float32
BF16 = jnp.bfloat16

WHOLE_NODES = 1 << 17


def legendre_seven(points):
    earlier = points * 0.0 + 1.0
    current = points
    for degree in range(1, 7):
        earlier, current = (
            current,
            ((2 * degree + 1) * points * current - degree * earlier) / (degree + 1),
        )
    return current


def host_tables():
    half = np.array([0.20929921790247888, 0.5917001814331423, 0.8717401485096066, 1.0])
    points = np.concatenate([-half[::-1], half])
    legendre = legendre_seven(points)
    weights = 2.0 / (56.0 * legendre**2)
    spacing = points[:, None] - points[None, :] + np.eye(8)
    derivative = legendre[:, None] / legendre[None, :] / spacing * (1.0 - np.eye(8))
    derivative[0, 0] = -14.0
    derivative[7, 7] = 14.0
    return weights, derivative


def tables():
    weights, derivative = host_tables()
    return (jnp.asarray(weights, F32), jnp.asarray(derivative, F32))


def split_matrix(matrix):
    matrix = matrix.astype(np.float32)
    high = matrix.astype(jnp.bfloat16)
    low = (matrix - high.astype(np.float32)).astype(jnp.bfloat16)
    return np.concatenate([high, high, low], axis=1)


def split_rows(values):
    high = values.astype(BF16)
    low = (values - high.astype(F32)).astype(BF16)
    return high, low


def lane_plan(devices, local):
    counts = [d * l for d, l in zip(devices, local)]
    lanes = int(np.prod(counts))
    grid = np.indices(tuple(devices) + tuple(local)).reshape(6, -1)
    place = [grid[i] * local[i] + grid[3 + i] for i in range(3)]
    lane_of = np.zeros(counts, np.int64)
    lane_of[place[0], place[1], place[2]] = np.arange(lanes)
    rows, plan = [], []

    def row(values):
        rows.append(np.asarray(values, np.float32))
        return len(rows) - 1

    for direction in range(3):
        moved = [p.copy() for p in place]
        moved[direction] += 1
        joined = moved[direction] < counts[direction]
        if direction == 0:
            joined[:] = True
        moved[direction] %= counts[direction]
        following = lane_of[moved[0], moved[1], moved[2]]
        delta = (following - np.arange(lanes)) % lanes
        behind = np.zeros(lanes, bool)
        behind[following[joined]] = True
        entry = {"classes": [], "keep": {}}
        for shift in np.unique(delta[joined]):
            here = joined & (delta == shift)
            there = np.zeros(lanes, bool)
            there[following[here]] = True
            entry["classes"].append(
                (
                    int(shift),
                    {s: row(here * s) for s in (1.0, 0.5)},
                    {s: row(there * s) for s in (1.0, 0.5)},
                )
            )
        entry["keep"]["avg"] = (
            row(np.where(joined, 0.5, 1.0)),
            row(np.where(behind, 0.5, 1.0)),
        )
        entry["keep"]["wall"] = (
            row(np.where(joined, 0.5, 0.0)),
            row(np.where(behind, 0.5, 0.0)),
        )
        plan.append(entry)
    return plan, np.stack(rows)


def face_slices(direction, end):
    if direction == 0:
        return [pl.ds(448 * end, 64)]
    if direction == 1:
        return [pl.ds(64 * a + 56 * end, 8) for a in range(8)]
    return [pl.ds(7 * end, 64, stride=8)]


def get(ref, rows):
    return jnp.concatenate([ref[h, rows, :] for h in range(ref.shape[0])], axis=1)


def put(ref, rows, values):
    for h in range(ref.shape[0]):
        ref[h, rows, :] = values[:, 128 * h : 128 * (h + 1)]


def load_face(ref, direction, end):
    parts = [get(ref, s) for s in face_slices(direction, end)]
    return parts[0] if len(parts) == 1 else jnp.concatenate(parts, axis=0)


def store_face(ref, direction, end, values):
    picks = face_slices(direction, end)
    size = 64 // len(picks)
    for i, s in enumerate(picks):
        put(ref, s, values[i * size : (i + 1) * size])


def join(ref, tab, plan, lanes, mode):
    scale = 1.0 if mode == "sum" else 0.5
    for direction in range(3):
        entry = plan[direction]
        lower = load_face(ref, direction, 0)
        upper = load_face(ref, direction, 1)
        if mode == "sum":
            new_upper, new_lower = upper, lower
        else:
            up, low = entry["keep"][mode]
            new_upper = upper * tab[up : up + 1, :]
            new_lower = lower * tab[low : low + 1, :]
        for shift, here, there in entry["classes"]:
            h, t = here[scale], there[scale]
            new_upper += pltpu.roll(lower, lanes - shift, 1) * tab[h : h + 1, :]
            new_lower += pltpu.roll(upper, shift, 1) * tab[t : t + 1, :]
        store_face(ref, direction, 0, new_lower)
        store_face(ref, direction, 1, new_upper)


def along_first(values, matrix, odd):
    total = [values[j] + values[7 - j] for j in range(4)]
    gap = [values[j] - values[7 - j] for j in range(4)]
    plus = 0.5 * (matrix[:4, :4] + matrix[:4, :3:-1])
    minus = 0.5 * (matrix[:4, :4] - matrix[:4, :3:-1])
    out = [None] * 8
    for i in range(4):
        from_total = total[0] * float(plus[i, 0])
        from_gap = gap[0] * float(minus[i, 0])
        for j in range(1, 4):
            from_total += total[j] * float(plus[i, j])
            from_gap += gap[j] * float(minus[i, j])
        out[i] = from_total + from_gap
        out[7 - i] = from_gap - from_total if odd else from_total - from_gap
    return out


def whole_kernel(
    plan, devices, weights, derivative, stiffness,
    me_ref, vel_ref, rea_ref, tab, grad_ref, op_ref, mass_ref, diag_ref, cross_ref,
    vel_out, pre_out, res_out,
    u, v, xs, g, rm, w, dinv, p, x, r, y, flip,
):
    halves = u.shape[1]
    lanes = 128 * halves
    per_half = 128 // 8
    fields = vel_ref.shape[1]

    def to_lanes(source, target):
        for half in range(halves):
            for chunk in range(4):
                cols = pl.ds(128 * chunk, 128)
                block = jnp.concatenate(
                    [source(half * per_half + d, cols) for d in range(per_half)], axis=0
                )
                target[half, cols, :] = block.T

    def split_to(slot, a, values):
        high, low = split_rows(values)
        rows = 64 * (a % 4)
        xs[slot, a // 4, pl.ds(rows, 64), :] = high
        xs[slot, a // 4, pl.ds(256 + rows, 64), :] = low
        xs[slot, a // 4, pl.ds(512 + rows, 64), :] = high

    def total(acc):
        return jnp.sum(jnp.sum(acc, axis=0, keepdims=True), axis=1, keepdims=True)

    for k in range(fields):
        to_lanes(lambda d, cols: vel_ref[d, k, :, cols], u.at[k])
        join(u.at[k], tab, plan, lanes, "avg")
    to_lanes(lambda d, cols: rea_ref[d, :, cols], rm)

    for a in range(8):
        rows = pl.ds(64 * a, 64)
        mass = jnp.concatenate([mass_ref[rows, :]] * halves, axis=1)
        diag = jnp.concatenate([diag_ref[rows, :]] * halves, axis=1)
        react = get(rm, rows) * mass
        put(rm, rows, react)
        put(dinv, rows, react + diag)
    join(dinv, tab, plan, lanes, "sum")
    for a in range(8):
        rows = pl.ds(64 * a, 64)
        inverse = 1.0 / get(dinv, rows)
        put(dinv, rows, inverse)
        put(w, rows, inverse)
    for direction in range(3):
        up, low = plan[direction]["keep"]["avg"]
        store_face(w, direction, 0, load_face(w, direction, 0) * tab[low : low + 1, :])
        store_face(w, direction, 1, load_face(w, direction, 1) * tab[up : up + 1, :])

    now, after = u, v
    for _ in range(SUBSTEPS):
        for k in range(fields):
            for a in range(8):
                split_to(k, a, get(now.at[k], pl.ds(64 * a, 64)))
            for half in range(2):
                g[k, half] = jnp.dot(grad_ref[...], xs[k, half], preferred_element_type=F32)
        for b in range(8):
            rows = [pl.ds(64 * a + 8 * b, 8) for a in range(8)]
            speed = [[get(now.at[j], rows[a]) for a in range(8)] for j in range(3)]
            for k in range(fields):
                first = along_first(speed[k], derivative, True)
                for a in range(8):
                    at = 64 * (a % 4) + 8 * b
                    transport = (
                        speed[0][a] * first[a]
                        + speed[1][a] * g[k, a // 4, pl.ds(at, 8), :]
                        + speed[2][a] * g[k, a // 4, pl.ds(256 + at, 8), :]
                    )
                    put(after.at[k], rows[a], speed[k][a] - step_size * transport)
        for k in range(fields):
            join(after.at[k], tab, plan, lanes, "wall")
        now, after = after, now

    for k in (1, 2):
        for a in range(8):
            split_to(k, a, get(now.at[k], pl.ds(64 * a, 64)))
    for half in range(2):
        second = jnp.dot(grad_ref[pl.ds(0, 256), :], xs[1, half], preferred_element_type=F32)
        third = jnp.dot(grad_ref[pl.ds(256, 256), :], xs[2, half], preferred_element_type=F32)
        put(y, pl.ds(256 * half, 256), second + third)
    for b in range(8):
        rows = [pl.ds(64 * a + 8 * b, 8) for a in range(8)]
        first = along_first([get(now.at[0], rows[a]) for a in range(8)], derivative, True)
        for a in range(8):
            mass = jnp.concatenate([mass_ref[rows[a], :]] * halves, axis=1)
            put(r, rows[a], -mass * (first[a] + get(y, rows[a])))
    join(r, tab, plan, lanes, "sum")

    acc = jnp.zeros((64, lanes), F32)
    for a in range(8):
        rows = pl.ds(64 * a, 64)
        res = get(r, rows)
        search = res * get(dinv, rows)
        put(p, rows, search)
        put(x, rows, jnp.zeros_like(res))
        split_to(0, a, search)
        acc += res * res * get(w, rows)
    progress = total(acc)
    for sweep in range(ITERS):
        for half in range(2):
            image = jnp.dot(op_ref[half], xs[0, half], preferred_element_type=F32)
            put(y, pl.ds(256 * half, 256), image)
        acc = jnp.zeros((8, lanes), F32)
        for b in range(8):
            rows = [pl.ds(64 * a + 8 * b, 8) for a in range(8)]
            search = [get(p, rows[a]) for a in range(8)]
            first = along_first(search, stiffness, False)
            cross = jnp.concatenate([cross_ref[pl.ds(8 * b, 8), :]] * halves, axis=1)
            for a in range(8):
                image = get(y, rows[a]) + cross * first[a] + get(rm, rows[a]) * search[a]
                put(y, rows[a], image)
                acc += image * search[a]
        alpha = progress / total(acc)
        join(y, tab, plan, lanes, "sum")
        acc = jnp.zeros((64, lanes), F32)
        for a in range(8):
            rows = pl.ds(64 * a, 64)
            put(x, rows, get(x, rows) + alpha * get(p, rows))
            res = get(r, rows) - alpha * get(y, rows)
            put(r, rows, res)
            acc += res * res * get(w, rows)
        if sweep < ITERS - 1:
            following = total(acc)
            beta = following / progress
            progress = following
            for a in range(8):
                rows = pl.ds(64 * a, 64)
                search = get(r, rows) * get(dinv, rows) + beta * get(p, rows)
                put(p, rows, search)
                split_to(0, a, search)

    me = me_ref[0]
    half = me // per_half
    block = pl.multiple_of((me % per_half) * 8, 8)
    for source, target in (
        [(now.at[k], vel_out.at[k]) for k in range(fields)] + [(x, pre_out), (r, res_out)]
    ):
        flip[...] = source[half].T
        target[...] = flip[pl.ds(block, 8), :]


def whole_body(devices, velocity, reaction):
    fields = velocity.shape[0]
    local = reaction.shape[:3]
    weights, derivative = host_tables()
    plan, tab = lane_plan(devices, local)
    lanes = tab.shape[1]
    eye = np.eye(8)
    grad = np.concatenate(
        [np.kron(np.eye(4), np.kron(derivative, eye)), np.kron(np.eye(4), np.kron(eye, derivative))]
    )
    stiffness = derivative.T @ (weights[:, None] * derivative)
    across = np.kron(stiffness, np.diag(weights)) + np.kron(np.diag(weights), stiffness)
    op = np.stack(
        [split_matrix(np.kron(np.diag(weights[4 * h : 4 * h + 4]), across)) for h in range(2)]
    )
    cube = weights[:, None, None] * weights[None, :, None] * weights[None, None, :]
    stiff_sum = np.sum(weights[:, None] * derivative * derivative, axis=0)
    diag = (
        stiff_sum[:, None, None] * weights[None, :, None] * weights[None, None, :]
        + weights[:, None, None] * stiff_sum[None, :, None] * weights[None, None, :]
        + weights[:, None, None] * weights[None, :, None] * stiff_sum[None, None, :]
    )

    def column(values):
        return np.broadcast_to(values.reshape(-1, 1), (values.size, 128)).astype(np.float32)

    cross = weights[:, None] * weights[None, :]
    axes = ("gx", "gy", "gz")
    everyone = lax.all_gather(velocity.reshape(fields, 8, 512), axes)
    react = lax.all_gather(reaction.reshape(8, 512), axes)
    me = lax.axis_index(axes).astype(jnp.int32).reshape(1)
    kernel = functools.partial(whole_kernel, plan, devices, weights, derivative, stiffness)
    vmem = pl.BlockSpec(memory_space=pltpu.VMEM)
    field = pltpu.VMEM((lanes // 128, 512, 128), F32)
    vel_out, pre_out, res_out = pl.pallas_call(
        kernel,
        out_shape=(
            jax.ShapeDtypeStruct((fields, 8, 512), F32),
            jax.ShapeDtypeStruct((8, 512), F32),
            jax.ShapeDtypeStruct((8, 512), F32),
        ),
        in_specs=[pl.BlockSpec(memory_space=pltpu.SMEM)] + [vmem] * 8,
        out_specs=(vmem, vmem, vmem),
        scratch_shapes=[
            pltpu.VMEM((fields, lanes // 128, 512, 128), F32),
            pltpu.VMEM((fields, lanes // 128, 512, 128), F32),
            pltpu.VMEM((fields, 2, 768, lanes), BF16),
            pltpu.VMEM((fields, 2, 512, lanes), F32),
        ]
        + [field] * 7
        + [pltpu.VMEM((128, 512), F32)],
        compiler_params=pltpu.CompilerParams(vmem_limit_bytes=40 << 20),
    )(
        me, everyone, react, jnp.asarray(tab), jnp.asarray(split_matrix(grad)), jnp.asarray(op),
        jnp.asarray(column(cube)), jnp.asarray(column(diag)), jnp.asarray(column(cross)),
    )
    return (
        vel_out.reshape(velocity.shape),
        pre_out.reshape(reaction.shape),
        res_out.reshape(reaction.shape),
    )


def extended(block, sides, width, periodic):
    for axis, dim in sides:
        count = lax.axis_size(axis)
        forward = [(i, i + 1) for i in range(count - 1)]
        if periodic:
            forward.append((count - 1, 0))
        backward = [(target, source) for source, target in forward]
        low = lax.ppermute(
            lax.slice_in_dim(block, block.shape[dim] - width, None, axis=dim), axis, forward
        )
        high = lax.ppermute(lax.slice_in_dim(block, 0, width, axis=dim), axis, backward)
        block = jnp.concatenate([low, block, high], axis=dim)
    return block


def derive(values, derivative, along_dim, transposed):
    layout = values.shape
    matrix = derivative.T if transposed else derivative
    blocks = values.reshape(-1, 8, 8, 8)
    patterns = ("aq,nqbc->nabc", "bq,naqc->nabc", "cq,nabq->nabc")
    result = jnp.einsum(patterns[along_dim], matrix, blocks, precision=lax.Precision.HIGHEST)
    return result.reshape(layout)


def place_face(values, target_axis, position, update):
    selector = tuple(
        (position if place == target_axis else slice(None) for place in range(values.ndim))
    )
    return values.at[selector].set(update)


def faces_along_x(sequence):
    return extended(sequence, (("gx", 0),), 1, True)


def faces_along_y(sequence):
    return extended(sequence, (("gy", 0),), 1, False)


def faces_along_z(sequence):
    return extended(sequence, (("gz", 0),), 1, False)


def join_faces(values, along_dim, exchanger):
    lower_face = jnp.moveaxis(jnp.take(values, 0, axis=4 + along_dim), 1 + along_dim, 0)
    upper_face = jnp.moveaxis(jnp.take(values, 7, axis=4 + along_dim), 1 + along_dim, 0)
    elements = lower_face.shape[0]
    face_shape = lower_face.shape
    sequence = jnp.stack([lower_face, upper_face], axis=1).reshape(2 * elements, -1)
    padded = exchanger(sequence)
    paired = padded.reshape(elements + 1, 2, -1)
    totals = paired[:, 0] + paired[:, 1]
    new_lower = jnp.moveaxis(totals[:-1].reshape(face_shape), 0, 1 + along_dim)
    new_upper = jnp.moveaxis(totals[1:].reshape(face_shape), 0, 1 + along_dim)
    values = place_face(values, 4 + along_dim, 0, new_lower)
    return place_face(values, 4 + along_dim, 7, new_upper)


def assemble(values):
    exchangers = (faces_along_x, faces_along_y, faces_along_z)
    dim_order = (0, 1, 2)
    for along_dim in dim_order:
        values = join_faces(values, along_dim, exchangers[along_dim])
    return values


def dim_factors(local_count, offset, total_count, bounded_by_walls):
    element_ids = offset + jnp.arange(local_count)
    node_ids = jnp.arange(8)
    at_end = (node_ids[None, :] == 0) | (node_ids[None, :] == 7)
    low_wall = (element_ids[:, None] == 0) & (node_ids[None, :] == 0)
    high_wall = (element_ids[:, None] == total_count - 1) & (node_ids[None, :] == 7)
    on_wall = (low_wall | high_wall) & bounded_by_walls
    shared = at_end & jnp.logical_not(on_wall)
    return (jnp.where(shared, 2.0, 1.0).astype(jnp.float32), on_wall.astype(jnp.float32))


def spread_body(velocity, reaction):
    weights, derivative = tables()
    count_x, count_y, count_z = (reaction.shape[0], reaction.shape[1], reaction.shape[2])
    speed = velocity.reshape(3, count_x, count_y, count_z, 8, 8, 8)
    react = reaction.reshape(1, count_x, count_y, count_z, 8, 8, 8)
    mass_matrix = weights[:, None, None] * weights[None, :, None] * weights[None, None, :]
    factor_x, wall_x = dim_factors(
        count_x, lax.axis_index("gx") * count_x, lax.axis_size("gx") * count_x, False
    )
    factor_y, wall_y = dim_factors(
        count_y, lax.axis_index("gy") * count_y, lax.axis_size("gy") * count_y, True
    )
    factor_z, wall_z = dim_factors(
        count_z, lax.axis_index("gz") * count_z, lax.axis_size("gz") * count_z, True
    )
    multiplicity = (
        factor_x[None, :, None, None, :, None, None]
        * factor_y[None, None, :, None, None, :, None]
        * factor_z[None, None, None, :, None, None, :]
    )
    interior = (1.0 - wall_y[None, None, :, None, None, :, None]) * (
        1.0 - wall_z[None, None, None, :, None, None, :]
    )
    stiff_sum = jnp.sum(weights[:, None] * derivative * derivative, axis=0)
    diag_local = (
        stiff_sum[:, None, None] * weights[None, :, None] * weights[None, None, :]
        + weights[:, None, None] * stiff_sum[None, :, None] * weights[None, None, :]
        + weights[:, None, None] * weights[None, :, None] * stiff_sum[None, None, :]
    )
    diag_terms = diag_local + react * mass_matrix
    speed = assemble(speed) / multiplicity
    diagonal = None
    for substep in range(SUBSTEPS):
        gradient_fields = [derive(speed, derivative, along_dim, False) for along_dim in range(3)]
        transport = (
            speed[0:1] * gradient_fields[0]
            + speed[1:2] * gradient_fields[1]
            + speed[2:3] * gradient_fields[2]
        )
        tendency = assemble(mass_matrix * transport) / (mass_matrix * multiplicity)
        speed = interior * (speed - step_size * tendency)
    spread = (
        derive(speed[0:1], derivative, 0, False)
        + derive(speed[1:2], derivative, 1, False)
        + derive(speed[2:3], derivative, 2, False)
    )
    source = -assemble(mass_matrix * spread)
    diagonal = assemble(diag_terms)

    def local_inner(first, second):
        return jnp.sum(first * second / multiplicity)

    def norm_weighted_mass(residual_vec, precond_vec):
        return lax.psum(local_inner(residual_vec, precond_vec), ("gx", "gy", "gz"))

    pressure = jnp.zeros_like(source)
    residual = source
    precond = residual / diagonal
    search = precond
    progress = norm_weighted_mass(residual, precond)
    for sweep_index in range(ITERS):
        local_sum = react * mass_matrix * search
        for apply_along_dim in range(3):
            local_sum = local_sum + derive(
                mass_matrix * derive(search, derivative, apply_along_dim, False),
                derivative,
                apply_along_dim,
                True,
            )
        applied = assemble(local_sum)
        step_length = progress / lax.psum(local_inner(search, applied), ("gx", "gy", "gz"))
        pressure = pressure + step_length * search
        residual = residual - step_length * applied
        precond = residual / diagonal
        progress_next = norm_weighted_mass(residual, precond)
        search = precond + progress_next / progress * search
        progress = progress_next
    return (
        speed.reshape(3, count_x, count_y, count_z, 512),
        pressure.reshape(count_x, count_y, count_z, 512),
        residual.reshape(count_x, count_y, count_z, 512),
    )


def solution(mesh):
    in_specs = (P(None, "gx", "gy", "gz", None), P("gx", "gy", "gz", None))
    out_specs = (
        P(None, "gx", "gy", "gz", None),
        P("gx", "gy", "gz", None),
        P("gx", "gy", "gz", None),
    )
    devices = tuple(mesh.shape[axis] for axis in ("gx", "gy", "gz"))

    def body(velocity, reaction):
        count = int(np.prod(reaction.shape[:3]))
        lanes = count * int(np.prod(devices))
        if count == 8 and lanes % 128 == 0 and lanes * reaction.shape[3] <= WHOLE_NODES:
            return whole_body(devices, velocity, reaction)
        return spread_body(velocity, reaction)

    return jax.shard_map(body, mesh=mesh, in_specs=in_specs, out_specs=out_specs, check_vma=False)
```

```python
import functools

import jax
import jax.numpy as jnp
import numpy as np
from jax import lax
from jax.experimental import pallas as pl
from jax.experimental.pallas import tpu as pltpu
from jax.sharding import PartitionSpec as P

SUBSTEPS = 2
ITERS = 4
step_size = 0.02

F32 = jnp.float32
BF16 = jnp.bfloat16

WHOLE_NODES = 1 << 17


def legendre_seven(points):
    earlier = points * 0.0 + 1.0
    current = points
    for degree in range(1, 7):
        earlier, current = (
            current,
            ((2 * degree + 1) * points * current - degree * earlier) / (degree + 1),
        )
    return current


def host_tables():
    half = np.array([0.20929921790247888, 0.5917001814331423, 0.8717401485096066, 1.0])
    points = np.concatenate([-half[::-1], half])
    legendre = legendre_seven(points)
    weights = 2.0 / (56.0 * legendre**2)
    spacing = points[:, None] - points[None, :] + np.eye(8)
    derivative = legendre[:, None] / legendre[None, :] / spacing * (1.0 - np.eye(8))
    derivative[0, 0] = -14.0
    derivative[7, 7] = 14.0
    return weights, derivative


def tables():
    weights, derivative = host_tables()
    return (jnp.asarray(weights, F32), jnp.asarray(derivative, F32))


def split_matrix(matrix):
    matrix = matrix.astype(np.float32)
    high = matrix.astype(jnp.bfloat16)
    low = (matrix - high.astype(np.float32)).astype(jnp.bfloat16)
    return np.concatenate([high, high, low], axis=1)


def split_rows(values):
    high = values.astype(BF16)
    low = (values - high.astype(F32)).astype(BF16)
    return high, low


def lane_plan(devices, local):
    counts = [d * l for d, l in zip(devices, local)]
    lanes = int(np.prod(counts))
    grid = np.indices(tuple(devices) + tuple(local)).reshape(6, -1)
    place = [grid[i] * local[i] + grid[3 + i] for i in range(3)]
    lane_of = np.zeros(counts, np.int64)
    lane_of[place[0], place[1], place[2]] = np.arange(lanes)
    rows, plan = [], []

    def row(values):
        rows.append(np.asarray(values, np.float32))
        return len(rows) - 1

    for direction in range(3):
        moved = [p.copy() for p in place]
        moved[direction] += 1
        joined = moved[direction] < counts[direction]
        if direction == 0:
            joined[:] = True
        moved[direction] %= counts[direction]
        following = lane_of[moved[0], moved[1], moved[2]]
        delta = (following - np.arange(lanes)) % lanes
        behind = np.zeros(lanes, bool)
        behind[following[joined]] = True
        entry = {"classes": [], "keep": {}}
        for shift in np.unique(delta[joined]):
            here = joined & (delta == shift)
            there = np.zeros(lanes, bool)
            there[following[here]] = True
            entry["classes"].append(
                (
                    int(shift),
                    {s: row(here * s) for s in (1.0, 0.5)},
                    {s: row(there * s) for s in (1.0, 0.5)},
                )
            )
        entry["keep"]["avg"] = (
            row(np.where(joined, 0.5, 1.0)),
            row(np.where(behind, 0.5, 1.0)),
        )
        entry["keep"]["wall"] = (
            row(np.where(joined, 0.5, 0.0)),
            row(np.where(behind, 0.5, 0.0)),
        )
        plan.append(entry)
    return plan, np.stack(rows)


def face_slices(direction, end):
    if direction == 0:
        return [pl.ds(448 * end, 64)]
    if direction == 1:
        return [pl.ds(64 * a + 56 * end, 8) for a in range(8)]
    return [pl.ds(7 * end, 64, stride=8)]


def get(ref, rows):
    return jnp.concatenate([ref[h, rows, :] for h in range(ref.shape[0])], axis=1)


def put(ref, rows, values):
    for h in range(ref.shape[0]):
        ref[h, rows, :] = values[:, 128 * h : 128 * (h + 1)]


def load_face(ref, direction, end):
    parts = [get(ref, s) for s in face_slices(direction, end)]
    return parts[0] if len(parts) == 1 else jnp.concatenate(parts, axis=0)


def store_face(ref, direction, end, values):
    picks = face_slices(direction, end)
    size = 64 // len(picks)
    for i, s in enumerate(picks):
        put(ref, s, values[i * size : (i + 1) * size])


def join(ref, tab, plan, lanes, mode):
    scale = 1.0 if mode == "sum" else 0.5
    for direction in range(3):
        entry = plan[direction]
        lower = load_face(ref, direction, 0)
        upper = load_face(ref, direction, 1)
        if mode == "sum":
            new_upper, new_lower = upper, lower
        else:
            up, low = entry["keep"][mode]
            new_upper = upper * tab[up : up + 1, :]
            new_lower = lower * tab[low : low + 1, :]
        for shift, here, there in entry["classes"]:
            h, t = here[scale], there[scale]
            new_upper += pltpu.roll(lower, lanes - shift, 1) * tab[h : h + 1, :]
            new_lower += pltpu.roll(upper, shift, 1) * tab[t : t + 1, :]
        store_face(ref, direction, 0, new_lower)
        store_face(ref, direction, 1, new_upper)


def along_first(values, matrix, odd):
    total = [values[j] + values[7 - j] for j in range(4)]
    gap = [values[j] - values[7 - j] for j in range(4)]
    plus = 0.5 * (matrix[:4, :4] + matrix[:4, :3:-1])
    minus = 0.5 * (matrix[:4, :4] - matrix[:4, :3:-1])
    out = [None] * 8
    for i in range(4):
        from_total = total[0] * float(plus[i, 0])
        from_gap = gap[0] * float(minus[i, 0])
        for j in range(1, 4):
            from_total += total[j] * float(plus[i, j])
            from_gap += gap[j] * float(minus[i, j])
        out[i] = from_total + from_gap
        out[7 - i] = from_gap - from_total if odd else from_total - from_gap
    return out


def pack_kernel(velocity, reaction, out, held, sems):
    fields = velocity.shape[0]
    copies = [
        pltpu.make_async_copy(velocity, held.at[pl.ds(0, fields)], sems.at[0]),
        pltpu.make_async_copy(reaction, held.at[fields], sems.at[1]),
    ]
    for copy in copies:
        copy.start()
    for copy in copies:
        copy.wait()
    for k in range(fields + 1):
        out[k] = jnp.concatenate([held[k, i, 0] for i in range(held.shape[1])], axis=0)


def whole_kernel(
    plan, devices, derivative, stiffness, fields,
    me_ref, *refs,
):
    pieces = 2 * devices[0]
    mine, others = refs[: devices[0]], refs[devices[0] : pieces]
    hbm = refs[pieces : pieces + 6]
    vel_out, pre_out, res_out = refs[pieces + 6 : pieces + 9]
    (
        tab, grad_ref, op_ref, mass_ref, diag_ref, cross_ref,
        u, v, xs, g, rm, w, dinv, p, x, r, y, flip, vel_own, pre_own, res_own, sems,
    ) = refs[pieces + 9 :]
    constants = [
        pltpu.make_async_copy(source, target, sems.at[i])
        for i, (source, target) in enumerate(
            zip(hbm, (tab, grad_ref, op_ref, mass_ref, diag_ref, cross_ref))
        )
    ]
    for copy in constants:
        copy.start()
    my_y, my_z = me_ref[0], me_ref[1]
    halves = u.shape[1]
    lanes = 128 * halves
    per_half = 128 // (8 * devices[1] * devices[2])
    is_low = my_z == 0

    def to_lanes(k, target):
        for half in range(halves):
            for chunk in range(4):
                cols = pl.ds(128 * chunk, 128)
                blocks = []
                for i in range(per_half):
                    s = -(half * per_half + i) % devices[0]
                    for j in range(devices[1]):
                        at = (my_y + (devices[1] - j)) % devices[1]
                        here = mine[s][at, k, :, cols]
                        there = others[s][at, k, :, cols]
                        blocks.append(jnp.where(is_low, here, there))
                        blocks.append(jnp.where(is_low, there, here))
                target[half, cols, :] = jnp.concatenate(blocks, axis=0).T

    def split_to(slot, a, values):
        high, low = split_rows(values)
        rows = 64 * (a % 4)
        xs[slot, a // 4, pl.ds(rows, 64), :] = high
        xs[slot, a // 4, pl.ds(256 + rows, 64), :] = low
        xs[slot, a // 4, pl.ds(512 + rows, 64), :] = high

    def total(acc):
        return jnp.sum(jnp.sum(acc, axis=0, keepdims=True), axis=1, keepdims=True)

    for k in range(fields):
        to_lanes(k, u.at[k])
    to_lanes(fields, rm)
    for copy in constants:
        copy.wait()
    for k in range(fields):
        join(u.at[k], tab, plan, lanes, "avg")

    for a in range(8):
        rows = pl.ds(64 * a, 64)
        mass = jnp.concatenate([mass_ref[rows, :]] * halves, axis=1)
        diag = jnp.concatenate([diag_ref[rows, :]] * halves, axis=1)
        react = get(rm, rows) * mass
        put(rm, rows, react)
        put(dinv, rows, react + diag)
    join(dinv, tab, plan, lanes, "sum")
    for a in range(8):
        rows = pl.ds(64 * a, 64)
        inverse = 1.0 / get(dinv, rows)
        put(dinv, rows, inverse)
        put(w, rows, inverse)
    for direction in range(3):
        up, low = plan[direction]["keep"]["avg"]
        store_face(w, direction, 0, load_face(w, direction, 0) * tab[low : low + 1, :])
        store_face(w, direction, 1, load_face(w, direction, 1) * tab[up : up + 1, :])

    now, after = u, v
    for _ in range(SUBSTEPS):
        for k in range(fields):
            for a in range(8):
                split_to(k, a, get(now.at[k], pl.ds(64 * a, 64)))
            for half in range(2):
                g[k, half] = jnp.dot(grad_ref[...], xs[k, half], preferred_element_type=F32)
        for b in range(8):
            rows = [pl.ds(64 * a + 8 * b, 8) for a in range(8)]
            speed = [[get(now.at[j], rows[a]) for a in range(8)] for j in range(3)]
            for k in range(fields):
                first = along_first(speed[k], derivative, True)
                for a in range(8):
                    at = 64 * (a % 4) + 8 * b
                    transport = (
                        speed[0][a] * first[a]
                        + speed[1][a] * g[k, a // 4, pl.ds(at, 8), :]
                        + speed[2][a] * g[k, a // 4, pl.ds(256 + at, 8), :]
                    )
                    put(after.at[k], rows[a], speed[k][a] - step_size * transport)
        for k in range(fields):
            join(after.at[k], tab, plan, lanes, "wall")
        now, after = after, now

    def own_block(source, own):
        flip[...] = source[0].T
        block = flip[pl.ds(pl.multiple_of((my_y * devices[2] + my_z) * 8, 8), 8), :]
        size = own.shape[2]
        for i in range(own.shape[0]):
            own[i, 0] = block[i * size : (i + 1) * size]

    for k in range(fields):
        own_block(now.at[k], vel_own.at[k])
    send_velocity = pltpu.make_async_copy(vel_own, vel_out, sems.at[6])
    send_velocity.start()

    for k in (1, 2):
        for a in range(8):
            split_to(k, a, get(now.at[k], pl.ds(64 * a, 64)))
    for half in range(2):
        second = jnp.dot(grad_ref[pl.ds(0, 256), :], xs[1, half], preferred_element_type=F32)
        third = jnp.dot(grad_ref[pl.ds(256, 256), :], xs[2, half], preferred_element_type=F32)
        put(y, pl.ds(256 * half, 256), second + third)
    for b in range(8):
        rows = [pl.ds(64 * a + 8 * b, 8) for a in range(8)]
        first = along_first([get(now.at[0], rows[a]) for a in range(8)], derivative, True)
        for a in range(8):
            mass = jnp.concatenate([mass_ref[rows[a], :]] * halves, axis=1)
            put(r, rows[a], -mass * (first[a] + get(y, rows[a])))
    join(r, tab, plan, lanes, "sum")

    acc = jnp.zeros((64, lanes), F32)
    for a in range(8):
        rows = pl.ds(64 * a, 64)
        res = get(r, rows)
        search = res * get(dinv, rows)
        put(p, rows, search)
        put(x, rows, jnp.zeros_like(res))
        split_to(0, a, search)
        acc += res * res * get(w, rows)
    progress = total(acc)
    for sweep in range(ITERS):
        for half in range(2):
            image = jnp.dot(op_ref[half], xs[0, half], preferred_element_type=F32)
            put(y, pl.ds(256 * half, 256), image)
        acc = jnp.zeros((8, lanes), F32)
        for b in range(8):
            rows = [pl.ds(64 * a + 8 * b, 8) for a in range(8)]
            search = [get(p, rows[a]) for a in range(8)]
            first = along_first(search, stiffness, False)
            cross = jnp.concatenate([cross_ref[pl.ds(8 * b, 8), :]] * halves, axis=1)
            for a in range(8):
                image = get(y, rows[a]) + cross * first[a] + get(rm, rows[a]) * search[a]
                put(y, rows[a], image)
                acc += image * search[a]
        alpha = progress / total(acc)
        join(y, tab, plan, lanes, "sum")
        acc = jnp.zeros((64, lanes), F32)
        for a in range(8):
            rows = pl.ds(64 * a, 64)
            put(x, rows, get(x, rows) + alpha * get(p, rows))
            res = get(r, rows) - alpha * get(y, rows)
            put(r, rows, res)
            acc += res * res * get(w, rows)
        if sweep < ITERS - 1:
            following = total(acc)
            beta = following / progress
            progress = following
            for a in range(8):
                rows = pl.ds(64 * a, 64)
                search = get(r, rows) * get(dinv, rows) + beta * get(p, rows)
                put(p, rows, search)
                split_to(0, a, search)

    for source, own in ((x, pre_own), (r, res_own)):
        own_block(source, own)
    for copy in (
        pltpu.make_async_copy(pre_own, pre_out, sems.at[7]),
        pltpu.make_async_copy(res_own, res_out, sems.at[8]),
    ):
        copy.start()
    send_velocity.wait()
    pltpu.make_async_copy(pre_own, pre_out, sems.at[7]).wait()
    pltpu.make_async_copy(res_own, res_out, sems.at[8]).wait()


def whole_body(devices, velocity, reaction):
    fields = velocity.shape[0]
    local = reaction.shape[:3]
    weights, derivative = host_tables()
    plan, tab = lane_plan(devices, local)
    lanes = tab.shape[1]
    eye = np.eye(8)
    grad = np.concatenate(
        [np.kron(np.eye(4), np.kron(derivative, eye)), np.kron(np.eye(4), np.kron(eye, derivative))]
    )
    stiffness = derivative.T @ (weights[:, None] * derivative)
    across = np.kron(stiffness, np.diag(weights)) + np.kron(np.diag(weights), stiffness)
    op = np.stack(
        [split_matrix(np.kron(np.diag(weights[4 * h : 4 * h + 4]), across)) for h in range(2)]
    )
    cube = weights[:, None, None] * weights[None, :, None] * weights[None, None, :]
    stiff_sum = np.sum(weights[:, None] * derivative * derivative, axis=0)
    diag = (
        stiff_sum[:, None, None] * weights[None, :, None] * weights[None, None, :]
        + weights[:, None, None] * stiff_sum[None, :, None] * weights[None, None, :]
        + weights[:, None, None] * weights[None, :, None] * stiff_sum[None, None, :]
    )

    def column(values):
        return np.broadcast_to(values.reshape(-1, 1), (values.size, 128)).astype(np.float32)

    cross = weights[:, None] * weights[None, :]
    vmem = pl.BlockSpec(memory_space=pltpu.VMEM)
    hbm = pl.BlockSpec(memory_space=pltpu.HBM)
    packed = pl.pallas_call(
        pack_kernel,
        out_shape=jax.ShapeDtypeStruct((fields + 1, 8, 512), F32),
        in_specs=[hbm, hbm],
        out_specs=vmem,
        scratch_shapes=[
            pltpu.VMEM((fields + 1,) + reaction.shape, F32),
            pltpu.SemaphoreType.DMA((2,)),
        ],
    )(velocity, reaction)

    def shifted(block, axis, step):
        count = lax.axis_size(axis)
        return lax.ppermute(block, axis, [(i, (i + step) % count) for i in range(count)])

    column_block = jnp.stack(
        [packed] + [shifted(packed, "gy", step) for step in range(1, devices[1])]
    )
    mine = [column_block] + [shifted(column_block, "gx", step) for step in range(1, devices[0])]
    others = [shifted(block, "gz", 1) for block in mine]
    me = jnp.stack([lax.axis_index("gy"), lax.axis_index("gz")]).astype(jnp.int32)
    constants = (
        tab, split_matrix(grad), op, column(cube), column(diag), column(cross),
    )
    field = pltpu.VMEM((lanes // 128, 512, 128), F32)
    own = pltpu.VMEM(reaction.shape, F32)
    return pl.pallas_call(
        functools.partial(whole_kernel, plan, devices, derivative, stiffness, fields),
        out_shape=(
            jax.ShapeDtypeStruct(velocity.shape, F32),
            jax.ShapeDtypeStruct(reaction.shape, F32),
            jax.ShapeDtypeStruct(reaction.shape, F32),
        ),
        in_specs=[pl.BlockSpec(memory_space=pltpu.SMEM)]
        + [vmem] * (2 * devices[0])
        + [hbm] * len(constants),
        out_specs=(hbm, hbm, hbm),
        scratch_shapes=[pltpu.VMEM(c.shape, c.dtype) for c in constants]
        + [
            pltpu.VMEM((fields, lanes // 128, 512, 128), F32),
            pltpu.VMEM((fields, lanes // 128, 512, 128), F32),
            pltpu.VMEM((fields, 2, 768, lanes), BF16),
            pltpu.VMEM((fields, 2, 512, lanes), F32),
        ]
        + [field] * 7
        + [
            pltpu.VMEM((128, 512), F32),
            pltpu.VMEM(velocity.shape, F32),
            own,
            own,
            pltpu.SemaphoreType.DMA((9,)),
        ],
        compiler_params=pltpu.CompilerParams(vmem_limit_bytes=40 << 20),
    )(me, *mine, *others, *(jnp.asarray(c) for c in constants))


def extended(block, sides, width, periodic):
    for axis, dim in sides:
        count = lax.axis_size(axis)
        forward = [(i, i + 1) for i in range(count - 1)]
        if periodic:
            forward.append((count - 1, 0))
        backward = [(target, source) for source, target in forward]
        low = lax.ppermute(
            lax.slice_in_dim(block, block.shape[dim] - width, None, axis=dim), axis, forward
        )
        high = lax.ppermute(lax.slice_in_dim(block, 0, width, axis=dim), axis, backward)
        block = jnp.concatenate([low, block, high], axis=dim)
    return block


def derive(values, derivative, along_dim, transposed):
    layout = values.shape
    matrix = derivative.T if transposed else derivative
    blocks = values.reshape(-1, 8, 8, 8)
    patterns = ("aq,nqbc->nabc", "bq,naqc->nabc", "cq,nabq->nabc")
    result = jnp.einsum(patterns[along_dim], matrix, blocks, precision=lax.Precision.HIGHEST)
    return result.reshape(layout)


def place_face(values, target_axis, position, update):
    selector = tuple(
        (position if place == target_axis else slice(None) for place in range(values.ndim))
    )
    return values.at[selector].set(update)


def faces_along_x(sequence):
    return extended(sequence, (("gx", 0),), 1, True)


def faces_along_y(sequence):
    return extended(sequence, (("gy", 0),), 1, False)


def faces_along_z(sequence):
    return extended(sequence, (("gz", 0),), 1, False)


def join_faces(values, along_dim, exchanger):
    lower_face = jnp.moveaxis(jnp.take(values, 0, axis=4 + along_dim), 1 + along_dim, 0)
    upper_face = jnp.moveaxis(jnp.take(values, 7, axis=4 + along_dim), 1 + along_dim, 0)
    elements = lower_face.shape[0]
    face_shape = lower_face.shape
    sequence = jnp.stack([lower_face, upper_face], axis=1).reshape(2 * elements, -1)
    padded = exchanger(sequence)
    paired = padded.reshape(elements + 1, 2, -1)
    totals = paired[:, 0] + paired[:, 1]
    new_lower = jnp.moveaxis(totals[:-1].reshape(face_shape), 0, 1 + along_dim)
    new_upper = jnp.moveaxis(totals[1:].reshape(face_shape), 0, 1 + along_dim)
    values = place_face(values, 4 + along_dim, 0, new_lower)
    return place_face(values, 4 + along_dim, 7, new_upper)


def assemble(values):
    exchangers = (faces_along_x, faces_along_y, faces_along_z)
    dim_order = (0, 1, 2)
    for along_dim in dim_order:
        values = join_faces(values, along_dim, exchangers[along_dim])
    return values


def dim_factors(local_count, offset, total_count, bounded_by_walls):
    element_ids = offset + jnp.arange(local_count)
    node_ids = jnp.arange(8)
    at_end = (node_ids[None, :] == 0) | (node_ids[None, :] == 7)
    low_wall = (element_ids[:, None] == 0) & (node_ids[None, :] == 0)
    high_wall = (element_ids[:, None] == total_count - 1) & (node_ids[None, :] == 7)
    on_wall = (low_wall | high_wall) & bounded_by_walls
    shared = at_end & jnp.logical_not(on_wall)
    return (jnp.where(shared, 2.0, 1.0).astype(jnp.float32), on_wall.astype(jnp.float32))


def spread_body(velocity, reaction):
    weights, derivative = tables()
    count_x, count_y, count_z = (reaction.shape[0], reaction.shape[1], reaction.shape[2])
    speed = velocity.reshape(3, count_x, count_y, count_z, 8, 8, 8)
    react = reaction.reshape(1, count_x, count_y, count_z, 8, 8, 8)
    mass_matrix = weights[:, None, None] * weights[None, :, None] * weights[None, None, :]
    factor_x, wall_x = dim_factors(
        count_x, lax.axis_index("gx") * count_x, lax.axis_size("gx") * count_x, False
    )
    factor_y, wall_y = dim_factors(
        count_y, lax.axis_index("gy") * count_y, lax.axis_size("gy") * count_y, True
    )
    factor_z, wall_z = dim_factors(
        count_z, lax.axis_index("gz") * count_z, lax.axis_size("gz") * count_z, True
    )
    multiplicity = (
        factor_x[None, :, None, None, :, None, None]
        * factor_y[None, None, :, None, None, :, None]
        * factor_z[None, None, None, :, None, None, :]
    )
    interior = (1.0 - wall_y[None, None, :, None, None, :, None]) * (
        1.0 - wall_z[None, None, None, :, None, None, :]
    )
    stiff_sum = jnp.sum(weights[:, None] * derivative * derivative, axis=0)
    diag_local = (
        stiff_sum[:, None, None] * weights[None, :, None] * weights[None, None, :]
        + weights[:, None, None] * stiff_sum[None, :, None] * weights[None, None, :]
        + weights[:, None, None] * weights[None, :, None] * stiff_sum[None, None, :]
    )
    diag_terms = diag_local + react * mass_matrix
    speed = assemble(speed) / multiplicity
    diagonal = None
    for substep in range(SUBSTEPS):
        gradient_fields = [derive(speed, derivative, along_dim, False) for along_dim in range(3)]
        transport = (
            speed[0:1] * gradient_fields[0]
            + speed[1:2] * gradient_fields[1]
            + speed[2:3] * gradient_fields[2]
        )
        tendency = assemble(mass_matrix * transport) / (mass_matrix * multiplicity)
        speed = interior * (speed - step_size * tendency)
    spread = (
        derive(speed[0:1], derivative, 0, False)
        + derive(speed[1:2], derivative, 1, False)
        + derive(speed[2:3], derivative, 2, False)
    )
    source = -assemble(mass_matrix * spread)
    diagonal = assemble(diag_terms)

    def local_inner(first, second):
        return jnp.sum(first * second / multiplicity)

    def norm_weighted_mass(residual_vec, precond_vec):
        return lax.psum(local_inner(residual_vec, precond_vec), ("gx", "gy", "gz"))

    pressure = jnp.zeros_like(source)
    residual = source
    precond = residual / diagonal
    search = precond
    progress = norm_weighted_mass(residual, precond)
    for sweep_index in range(ITERS):
        local_sum = react * mass_matrix * search
        for apply_along_dim in range(3):
            local_sum = local_sum + derive(
                mass_matrix * derive(search, derivative, apply_along_dim, False),
                derivative,
                apply_along_dim,
                True,
            )
        applied = assemble(local_sum)
        step_length = progress / lax.psum(local_inner(search, applied), ("gx", "gy", "gz"))
        pressure = pressure + step_length * search
        residual = residual - step_length * applied
        precond = residual / diagonal
        progress_next = norm_weighted_mass(residual, precond)
        search = precond + progress_next / progress * search
        progress = progress_next
    return (
        speed.reshape(3, count_x, count_y, count_z, 512),
        pressure.reshape(count_x, count_y, count_z, 512),
        residual.reshape(count_x, count_y, count_z, 512),
    )


def solution(mesh):
    in_specs = (P(None, "gx", "gy", "gz", None), P("gx", "gy", "gz", None))
    out_specs = (
        P(None, "gx", "gy", "gz", None),
        P("gx", "gy", "gz", None),
        P("gx", "gy", "gz", None),
    )
    devices = tuple(mesh.shape[axis] for axis in ("gx", "gy", "gz"))

    def body(velocity, reaction):
        count = int(np.prod(reaction.shape[:3]))
        lanes = count * int(np.prod(devices))
        fits = lanes % 128 == 0 and lanes * reaction.shape[3] <= WHOLE_NODES
        if count == 8 and reaction.shape[1] == 1 and devices[2] == 2 and fits:
            return whole_body(devices, velocity, reaction)
        return spread_body(velocity, reaction)

    return jax.shard_map(body, mesh=mesh, in_specs=in_specs, out_specs=out_specs, check_vma=False)
```

```python
import functools

import jax
import jax.numpy as jnp
import numpy as np
from jax import lax
from jax.experimental import pallas as pl
from jax.experimental.pallas import tpu as pltpu
from jax.sharding import PartitionSpec as P

SUBSTEPS = 2
ITERS = 4
step_size = 0.02

F32 = jnp.float32
BF16 = jnp.bfloat16


def legendre_seven(points):
    earlier = points * 0.0 + 1.0
    current = points
    for degree in range(1, 7):
        earlier, current = (
            current,
            ((2 * degree + 1) * points * current - degree * earlier) / (degree + 1),
        )
    return current


def host_tables():
    half = np.array([0.20929921790247888, 0.5917001814331423, 0.8717401485096066, 1.0])
    points = np.concatenate([-half[::-1], half])
    legendre = legendre_seven(points)
    weights = 2.0 / (56.0 * legendre**2)
    spacing = points[:, None] - points[None, :] + np.eye(8)
    derivative = legendre[:, None] / legendre[None, :] / spacing * (1.0 - np.eye(8))
    derivative[0, 0] = -14.0
    derivative[7, 7] = 14.0
    return weights, derivative


def tables():
    weights, derivative = host_tables()
    return (jnp.asarray(weights, F32), jnp.asarray(derivative, F32))


def split_matrix(matrix):
    matrix = matrix.astype(np.float32)
    high = matrix.astype(jnp.bfloat16)
    low = (matrix - high.astype(np.float32)).astype(jnp.bfloat16)
    return np.concatenate([high, high, low, low], axis=1)


def split_rows(values):
    high = values.astype(BF16)
    low = (values - high.astype(F32)).astype(BF16)
    return jnp.concatenate([high, low, high, low], axis=0)


def face_slices(direction, end):
    if direction == 0:
        return [pl.ds(448 * end, 64)]
    if direction == 1:
        return [pl.ds(64 * a + 56 * end, 8) for a in range(8)]
    return [pl.ds(7 * end, 64, stride=8)]


def load_face(ref, half, direction, end):
    parts = [ref[half, s, :] for s in face_slices(direction, end)]
    return parts[0] if len(parts) == 1 else jnp.concatenate(parts, axis=0)


def store_face(ref, half, direction, end, values):
    picks = face_slices(direction, end)
    size = 64 // len(picks)
    for i, s in enumerate(picks):
        ref[half, s, :] = values[i * size : (i + 1) * size]


def roll_lanes(parts, shift):
    turned = [pltpu.roll(part, shift, 1) for part in parts]
    lane = lax.broadcasted_iota(jnp.int32, parts[0].shape, 1)
    return [jnp.where(lane < shift, turned[i - 1], turned[i]) for i in range(len(parts))]


def roll_lanes_back(parts, shift):
    turned = [pltpu.roll(part, 128 - shift, 1) for part in parts]
    lane = lax.broadcasted_iota(jnp.int32, parts[0].shape, 1)
    count = len(parts)
    return [
        jnp.where(lane < 128 - shift, turned[i], turned[(i + 1) % count]) for i in range(count)
    ]


class Lanes:
    def __init__(self, counts):
        self.strides = (counts[1] * counts[2], counts[2], 1)
        lane = lax.broadcasted_iota(jnp.int32, (1, 128), 1)
        place = {1: (lane // counts[2]) % counts[1], 2: lane % counts[2]}
        self.has_next = {d: place[d] < counts[d] - 1 for d in (1, 2)}
        self.has_prev = {d: place[d] > 0 for d in (1, 2)}

    def factors(self, direction, mode):
        n, p = self.has_next[direction], self.has_prev[direction]
        if mode == "sum":
            return None, None, jnp.where(n, 1.0, 0.0), jnp.where(p, 1.0, 0.0)
        alone = 1.0 if mode == "avg" else 0.0
        return (
            jnp.where(n, 0.5, alone),
            jnp.where(p, 0.5, alone),
            jnp.where(n, 0.5, 0.0),
            jnp.where(p, 0.5, 0.0),
        )


def join(jobs, lanes):
    for direction in range(3):
        stride = lanes.strides[direction]
        for ref, mode in jobs:
            halves = range(ref.shape[0])
            lower = [load_face(ref, h, direction, 0) for h in halves]
            upper = [load_face(ref, h, direction, 1) for h in halves]
            if direction == 0:
                new_upper = [a + b for a, b in zip(upper, roll_lanes_back(lower, stride))]
                new_lower = [a + b for a, b in zip(lower, roll_lanes(upper, stride))]
                if mode != "sum":
                    new_upper = [0.5 * a for a in new_upper]
                    new_lower = [0.5 * a for a in new_lower]
            else:
                own_up, own_low, from_next, from_prev = lanes.factors(direction, mode)
                new_upper, new_lower = [], []
                for h in halves:
                    up, low = upper[h], lower[h]
                    if own_up is not None:
                        up, low = up * own_up, low * own_low
                    new_upper.append(up + pltpu.roll(lower[h], 128 - stride, 1) * from_next)
                    new_lower.append(low + pltpu.roll(upper[h], stride, 1) * from_prev)
            for h in halves:
                store_face(ref, h, direction, 0, new_lower[h])
                store_face(ref, h, direction, 1, new_upper[h])


def along_first(values, matrix, odd):
    total = [values[j] + values[7 - j] for j in range(4)]
    gap = [values[j] - values[7 - j] for j in range(4)]
    plus = 0.5 * (matrix[:4, :4] + matrix[:4, :3:-1])
    minus = 0.5 * (matrix[:4, :4] - matrix[:4, :3:-1])
    out = [None] * 8
    for i in range(4):
        from_total = total[0] * float(plus[i, 0])
        from_gap = gap[0] * float(minus[i, 0])
        for j in range(1, 4):
            from_total += total[j] * float(plus[i, j])
            from_gap += gap[j] * float(minus[i, j])
        out[i] = from_total + from_gap
        out[7 - i] = from_gap - from_total if odd else from_total - from_gap
    return out


def pack_kernel(me, velocity, reaction, vel_out, rea_out, vel_held, rea_held, sems):
    copies = [
        pltpu.make_async_copy(velocity, vel_held, sems.at[0]),
        pltpu.make_async_copy(reaction, rea_held, sems.at[1]),
    ]
    for copy in copies:
        copy.start()
    for copy in copies:
        copy.wait()
    is_low = me[1] == 0

    def rows(held):
        low, high = held[0, 0], held[1, 0]
        straight = jnp.concatenate([low, high], axis=0)
        turned = jnp.concatenate([high, low], axis=0)
        return jnp.where(is_low, straight, turned)

    for k in range(vel_held.shape[0]):
        vel_out[k] = rows(vel_held.at[k])
    rea_out[...] = rows(rea_held)


def stack_kernel(*refs):
    out = refs[-1]
    for i, ref in enumerate(refs[:-1]):
        out[i] = ref[...]


def stacked(blocks):
    vmem = pl.BlockSpec(memory_space=pltpu.VMEM)
    return pl.pallas_call(
        stack_kernel,
        out_shape=jax.ShapeDtypeStruct((len(blocks),) + blocks[0].shape, F32),
        in_specs=[vmem] * len(blocks),
        out_specs=vmem,
    )(*blocks)


def whole_kernel(devices, weights, derivative, me_ref, *refs):
    count_x = devices[0]
    mine, others = refs[:count_x], refs[count_x : 2 * count_x]
    (
        react_mine, react_others, cross_ref, matrix_ref,
        vel_out, pre_out, res_out,
        u, v, rm, w, dinv, p, r, y, x, flip, vel_own, pre_own, res_own, sems,
    ) = refs[2 * count_x :]
    my_y, my_z = me_ref[0], me_ref[1]
    halves = range(u.shape[1])
    per_half = count_x // len(halves)
    fields = u.shape[0]
    lanes = Lanes((2 * devices[0], devices[1], 8))
    stiffness = derivative.T @ (weights[:, None] * derivative)
    stiff_sum = np.sum(weights[:, None] * derivative * derivative, axis=0)
    slabs = [pl.ds(64 * a, 64) for a in range(8)]
    columns = [[pl.ds(64 * a + 8 * b, 8) for a in range(8)] for b in range(8)]

    sublane = lax.broadcasted_iota(jnp.int32, (8, 128), 0)
    own_rows = (sublane < 4) == (my_z == 0)
    below = [(my_y + (devices[1] - j)) % devices[1] for j in range(devices[1])]

    def to_lanes(here_of, there_of, target):
        for half in halves:
            for chunk in range(4):
                cols = pl.ds(128 * chunk, 128)
                blocks = []
                for i in range(per_half):
                    s = -(half * per_half + i) % count_x
                    first, second = [], []
                    for at in below:
                        here, there = here_of(s, at, cols), there_of(s, at, cols)
                        first.append(jnp.where(own_rows, here, there))
                        second.append(pltpu.roll(jnp.where(own_rows, there, here), 4, 0))
                    blocks += first + second
                target[half, cols, :] = jnp.concatenate(blocks, axis=0).T

    for k in range(fields):
        to_lanes(
            lambda s, at, cols: mine[s][at, k, :, cols],
            lambda s, at, cols: others[s][at, k, :, cols],
            u.at[k],
        )
    to_lanes(
        lambda s, at, cols: react_mine[at, s, :, cols],
        lambda s, at, cols: react_others[at, s, :, cols],
        rm,
    )

    for a in range(8):
        mass = cross_ref[pl.ds(0, 64), :] * float(weights[a])
        diag = cross_ref[pl.ds(0, 64), :] * float(stiff_sum[a])
        diag += cross_ref[pl.ds(64, 64), :] * float(weights[a])
        for h in halves:
            react = rm[h, slabs[a], :] * mass
            rm[h, slabs[a], :] = react
            dinv[h, slabs[a], :] = react + diag
    join([(u.at[k], "avg") for k in range(fields)] + [(dinv, "sum")], lanes)

    up, low, _, _ = lanes.factors(2, "avg")
    share_z = jnp.where(sublane == 7, up, jnp.where(sublane == 0, low, 1.0))
    up, low, _, _ = lanes.factors(1, "avg")
    for b in range(8):
        share = share_z * (low if b == 0 else up) if b in (0, 7) else share_z
        for a in range(8):
            for h in halves:
                inverse = 1.0 / dinv[h, columns[b][a], :]
                dinv[h, columns[b][a], :] = inverse
                w[h, columns[b][a], :] = inverse * (share * 0.5 if a in (0, 7) else share)

    def slab(ref, a):
        return split_rows(jnp.concatenate([ref[h, slabs[a], :] for h in halves], axis=1))

    now, after = u, v
    for _ in range(SUBSTEPS):
        for b in range(8):
            for h in halves:
                along = [now[0, h, columns[b][a], :] for a in range(8)]
                for k in range(fields):
                    values = [now[k, h, columns[b][a], :] for a in range(8)] if k else along
                    first = along_first(values, step_size * derivative, True)
                    for a in range(8):
                        after[k, h, columns[b][a], :] = values[a] - along[a] * first[a]
        for a in range(8):
            for k in range(fields):
                g = jnp.dot(
                    matrix_ref[pl.ds(0, 128), :], slab(now.at[k], a), preferred_element_type=F32
                )
                for h in halves:
                    cols = slice(128 * h, 128 * (h + 1))
                    after[k, h, slabs[a], :] -= (
                        now[1, h, slabs[a], :] * g[:64, cols] + now[2, h, slabs[a], :] * g[64:, cols]
                    )
        join([(after.at[k], "wall") for k in range(fields)], lanes)
        now, after = after, now

    def own_block(source, own):
        flip[...] = source.T
        size = own.shape[2]
        for i in range(own.shape[0]):
            start = i * lanes.strides[0] + my_y * lanes.strides[1]
            block = flip[pl.ds(pl.multiple_of(start, 8), 8), :]
            own[i, 0] = jnp.where(my_z == 0, block[:size], block[size:])

    for b in range(8):
        for h in halves:
            first = along_first(
                [now[0, h, columns[b][a], :] for a in range(8)], step_size * derivative, True
            )
            for a in range(8):
                r[h, columns[b][a], :] = first[a]
    for a in range(8):
        g = jnp.dot(matrix_ref[pl.ds(0, 64), :], slab(now.at[1], a), preferred_element_type=F32)
        g += jnp.dot(matrix_ref[pl.ds(64, 64), :], slab(now.at[2], a), preferred_element_type=F32)
        mass = cross_ref[pl.ds(0, 64), :] * float(-weights[a] / step_size)
        for h in halves:
            r[h, slabs[a], :] = mass * (r[h, slabs[a], :] + g[:, 128 * h : 128 * (h + 1)])
    join([(r, "sum")], lanes)

    for k in range(fields):
        own_block(now[k, 0], vel_own.at[k])
    send_velocity = pltpu.make_async_copy(vel_own, vel_out, sems.at[0])
    send_velocity.start()

    def total(acc):
        return jnp.sum(jnp.sum(acc, axis=0, keepdims=True), axis=1, keepdims=True)

    progress = beta = None
    for sweep in range(ITERS):
        acc = jnp.zeros((8, 128), F32)
        for b in range(8):
            cross = cross_ref[pl.ds(8 * b, 8), :]
            for h in halves:
                search = []
                for a in range(8):
                    res = r[h, columns[b][a], :]
                    here = res * dinv[h, columns[b][a], :]
                    if sweep:
                        here += beta * p[h, columns[b][a], :]
                    else:
                        acc += res * res * w[h, columns[b][a], :]
                    p[h, columns[b][a], :] = here
                    search.append(here)
                first = along_first(search, stiffness, False)
                for a in range(8):
                    y[h, columns[b][a], :] = cross * first[a] + rm[h, columns[b][a], :] * search[a]
        if not sweep:
            progress = total(acc)
        acc = jnp.zeros((64, 128), F32)
        for a in range(8):
            at = 128 + 64 * min(a, 7 - a)
            g = jnp.dot(matrix_ref[pl.ds(at, 64), :], slab(p, a), preferred_element_type=F32)
            for h in halves:
                image = y[h, slabs[a], :] + g[:, 128 * h : 128 * (h + 1)]
                y[h, slabs[a], :] = image
                acc += image * p[h, slabs[a], :]
        alpha = progress / total(acc)
        join([(y, "sum")], lanes)
        last = sweep == ITERS - 1
        acc = jnp.zeros((64, 128), F32)
        for a in range(8):
            step = alpha * p[0, slabs[a], :]
            x[slabs[a], :] = x[slabs[a], :] + step if sweep else step
            for h in halves[:1] if last else halves:
                res = r[h, slabs[a], :] - alpha * y[h, slabs[a], :]
                r[h, slabs[a], :] = res
                if not last:
                    acc += res * res * w[h, slabs[a], :]
        if not last:
            following = total(acc)
            beta = following / progress
            progress = following

    own_block(x[...], pre_own)
    send_pressure = pltpu.make_async_copy(pre_own, pre_out, sems.at[1])
    send_pressure.start()
    own_block(r[0], res_own)
    send_residual = pltpu.make_async_copy(res_own, res_out, sems.at[2])
    send_residual.start()
    send_velocity.wait()
    send_pressure.wait()
    send_residual.wait()


def whole_body(devices, velocity, reaction):
    fields = velocity.shape[0]
    lanes = int(np.prod(devices)) * 8
    weights, derivative = host_tables()
    eye = np.eye(8)
    stiffness = derivative.T @ (weights[:, None] * derivative)
    stiff_sum = np.sum(weights[:, None] * derivative * derivative, axis=0)
    across = np.kron(stiffness, np.diag(weights)) + np.kron(np.diag(weights), stiffness)
    matrices = np.concatenate(
        [
            split_matrix(step_size * np.kron(derivative, eye)),
            split_matrix(step_size * np.kron(eye, derivative)),
        ]
        + [split_matrix(weights[a] * across) for a in range(4)]
    )
    cross = np.outer(weights, weights).reshape(-1)
    sides = np.outer(stiff_sum, weights).reshape(-1) + np.outer(weights, stiff_sum).reshape(-1)
    cross = np.broadcast_to(np.concatenate([cross, sides])[:, None], (128, 128))

    vmem = pl.BlockSpec(memory_space=pltpu.VMEM)
    smem = pl.BlockSpec(memory_space=pltpu.SMEM)
    hbm = pl.BlockSpec(memory_space=pltpu.HBM)
    me = jnp.stack([lax.axis_index("gy"), lax.axis_index("gz")]).astype(jnp.int32)
    speed, react = pl.pallas_call(
        pack_kernel,
        out_shape=(
            jax.ShapeDtypeStruct((fields, 8, 512), F32),
            jax.ShapeDtypeStruct((8, 512), F32),
        ),
        in_specs=[smem, hbm, hbm],
        out_specs=(vmem, vmem),
        scratch_shapes=[
            pltpu.VMEM(velocity.shape, F32),
            pltpu.VMEM(reaction.shape, F32),
            pltpu.SemaphoreType.DMA((2,)),
        ],
    )(me, velocity, reaction)

    def shifted(block, axis, step):
        count = lax.axis_size(axis)
        return lax.ppermute(block, axis, [(i, (i + step) % count) for i in range(count)])

    def around(block, axis):
        return [block] + [shifted(block, axis, step) for step in range(1, lax.axis_size(axis))]

    mine = around(stacked(around(speed, "gy")), "gx")
    others = [shifted(block, "gz", 1) for block in mine]
    react_mine = stacked(around(stacked(around(react, "gx")), "gy"))
    react_others = shifted(react_mine, "gz", 1)

    field = pltpu.VMEM((lanes // 128, 512, 128), F32)
    three = pltpu.VMEM((fields, lanes // 128, 512, 128), F32)
    own = pltpu.VMEM(reaction.shape, F32)
    return pl.pallas_call(
        functools.partial(whole_kernel, devices, weights, derivative),
        out_shape=(
            jax.ShapeDtypeStruct(velocity.shape, F32),
            jax.ShapeDtypeStruct(reaction.shape, F32),
            jax.ShapeDtypeStruct(reaction.shape, F32),
        ),
        in_specs=[smem] + [vmem] * (2 * devices[0] + 4),
        out_specs=(hbm, hbm, hbm),
        scratch_shapes=[three, three]
        + [field] * 6
        + [
            pltpu.VMEM((512, 128), F32),
            pltpu.VMEM((128, 512), F32),
            pltpu.VMEM(velocity.shape, F32),
            own,
            own,
            pltpu.SemaphoreType.DMA((3,)),
        ],
        compiler_params=pltpu.CompilerParams(vmem_limit_bytes=40 << 20),
    )(
        me, *mine, *others, react_mine, react_others,
        jnp.asarray(cross, F32), jnp.asarray(matrices),
    )


def extended(block, sides, width, periodic):
    for axis, dim in sides:
        count = lax.axis_size(axis)
        forward = [(i, i + 1) for i in range(count - 1)]
        if periodic:
            forward.append((count - 1, 0))
        backward = [(target, source) for source, target in forward]
        low = lax.ppermute(
            lax.slice_in_dim(block, block.shape[dim] - width, None, axis=dim), axis, forward
        )
        high = lax.ppermute(lax.slice_in_dim(block, 0, width, axis=dim), axis, backward)
        block = jnp.concatenate([low, block, high], axis=dim)
    return block


def derive(values, derivative, along_dim, transposed):
    layout = values.shape
    matrix = derivative.T if transposed else derivative
    blocks = values.reshape(-1, 8, 8, 8)
    patterns = ("aq,nqbc->nabc", "bq,naqc->nabc", "cq,nabq->nabc")
    result = jnp.einsum(patterns[along_dim], matrix, blocks, precision=lax.Precision.HIGHEST)
    return result.reshape(layout)


def place_face(values, target_axis, position, update):
    selector = tuple(
        (position if place == target_axis else slice(None) for place in range(values.ndim))
    )
    return values.at[selector].set(update)


def faces_along_x(sequence):
    return extended(sequence, (("gx", 0),), 1, True)


def faces_along_y(sequence):
    return extended(sequence, (("gy", 0),), 1, False)


def faces_along_z(sequence):
    return extended(sequence, (("gz", 0),), 1, False)


def join_faces(values, along_dim, exchanger):
    lower_face = jnp.moveaxis(jnp.take(values, 0, axis=4 + along_dim), 1 + along_dim, 0)
    upper_face = jnp.moveaxis(jnp.take(values, 7, axis=4 + along_dim), 1 + along_dim, 0)
    elements = lower_face.shape[0]
    face_shape = lower_face.shape
    sequence = jnp.stack([lower_face, upper_face], axis=1).reshape(2 * elements, -1)
    padded = exchanger(sequence)
    paired = padded.reshape(elements + 1, 2, -1)
    totals = paired[:, 0] + paired[:, 1]
    new_lower = jnp.moveaxis(totals[:-1].reshape(face_shape), 0, 1 + along_dim)
    new_upper = jnp.moveaxis(totals[1:].reshape(face_shape), 0, 1 + along_dim)
    values = place_face(values, 4 + along_dim, 0, new_lower)
    return place_face(values, 4 + along_dim, 7, new_upper)


def assemble(values):
    exchangers = (faces_along_x, faces_along_y, faces_along_z)
    dim_order = (0, 1, 2)
    for along_dim in dim_order:
        values = join_faces(values, along_dim, exchangers[along_dim])
    return values


def dim_factors(local_count, offset, total_count, bounded_by_walls):
    element_ids = offset + jnp.arange(local_count)
    node_ids = jnp.arange(8)
    at_end = (node_ids[None, :] == 0) | (node_ids[None, :] == 7)
    low_wall = (element_ids[:, None] == 0) & (node_ids[None, :] == 0)
    high_wall = (element_ids[:, None] == total_count - 1) & (node_ids[None, :] == 7)
    on_wall = (low_wall | high_wall) & bounded_by_walls
    shared = at_end & jnp.logical_not(on_wall)
    return (jnp.where(shared, 2.0, 1.0).astype(jnp.float32), on_wall.astype(jnp.float32))


def spread_body(velocity, reaction):
    weights, derivative = tables()
    count_x, count_y, count_z = (reaction.shape[0], reaction.shape[1], reaction.shape[2])
    speed = velocity.reshape(3, count_x, count_y, count_z, 8, 8, 8)
    react = reaction.reshape(1, count_x, count_y, count_z, 8, 8, 8)
    mass_matrix = weights[:, None, None] * weights[None, :, None] * weights[None, None, :]
    factor_x, wall_x = dim_factors(
        count_x, lax.axis_index("gx") * count_x, lax.axis_size("gx") * count_x, False
    )
    factor_y, wall_y = dim_factors(
        count_y, lax.axis_index("gy") * count_y, lax.axis_size("gy") * count_y, True
    )
    factor_z, wall_z = dim_factors(
        count_z, lax.axis_index("gz") * count_z, lax.axis_size("gz") * count_z, True
    )
    multiplicity = (
        factor_x[None, :, None, None, :, None, None]
        * factor_y[None, None, :, None, None, :, None]
        * factor_z[None, None, None, :, None, None, :]
    )
    interior = (1.0 - wall_y[None, None, :, None, None, :, None]) * (
        1.0 - wall_z[None, None, None, :, None, None, :]
    )
    stiff_sum = jnp.sum(weights[:, None] * derivative * derivative, axis=0)
    diag_local = (
        stiff_sum[:, None, None] * weights[None, :, None] * weights[None, None, :]
        + weights[:, None, None] * stiff_sum[None, :, None] * weights[None, None, :]
        + weights[:, None, None] * weights[None, :, None] * stiff_sum[None, None, :]
    )
    diag_terms = diag_local + react * mass_matrix
    speed = assemble(speed) / multiplicity
    diagonal = None
    for substep in range(SUBSTEPS):
        gradient_fields = [derive(speed, derivative, along_dim, False) for along_dim in range(3)]
        transport = (
            speed[0:1] * gradient_fields[0]
            + speed[1:2] * gradient_fields[1]
            + speed[2:3] * gradient_fields[2]
        )
        tendency = assemble(mass_matrix * transport) / (mass_matrix * multiplicity)
        speed = interior * (speed - step_size * tendency)
    spread = (
        derive(speed[0:1], derivative, 0, False)
        + derive(speed[1:2], derivative, 1, False)
        + derive(speed[2:3], derivative, 2, False)
    )
    source = -assemble(mass_matrix * spread)
    diagonal = assemble(diag_terms)

    def local_inner(first, second):
        return jnp.sum(first * second / multiplicity)

    def norm_weighted_mass(residual_vec, precond_vec):
        return lax.psum(local_inner(residual_vec, precond_vec), ("gx", "gy", "gz"))

    pressure = jnp.zeros_like(source)
    residual = source
    precond = residual / diagonal
    search = precond
    progress = norm_weighted_mass(residual, precond)
    for sweep_index in range(ITERS):
        local_sum = react * mass_matrix * search
        for apply_along_dim in range(3):
            local_sum = local_sum + derive(
                mass_matrix * derive(search, derivative, apply_along_dim, False),
                derivative,
                apply_along_dim,
                True,
            )
        applied = assemble(local_sum)
        step_length = progress / lax.psum(local_inner(search, applied), ("gx", "gy", "gz"))
        pressure = pressure + step_length * search
        residual = residual - step_length * applied
        precond = residual / diagonal
        progress_next = norm_weighted_mass(residual, precond)
        search = precond + progress_next / progress * search
        progress = progress_next
    return (
        speed.reshape(3, count_x, count_y, count_z, 512),
        pressure.reshape(count_x, count_y, count_z, 512),
        residual.reshape(count_x, count_y, count_z, 512),
    )


def solution(mesh):
    in_specs = (P(None, "gx", "gy", "gz", None), P("gx", "gy", "gz", None))
    out_specs = (
        P(None, "gx", "gy", "gz", None),
        P("gx", "gy", "gz", None),
        P("gx", "gy", "gz", None),
    )
    devices = tuple(mesh.shape[axis] for axis in ("gx", "gy", "gz"))

    def body(velocity, reaction):
        lanes = int(np.prod(reaction.shape[:3])) * int(np.prod(devices))
        blocks = reaction.shape[:3] == (2, 1, 4) and devices[0] % 2 == 0 and devices[2] == 2
        section = 8 * devices[1]
        if blocks and 128 % section == 0 and lanes == 256:
            return whole_body(devices, velocity, reaction)
        return spread_body(velocity, reaction)

    return jax.shard_map(body, mesh=mesh, in_specs=in_specs, out_specs=out_specs, check_vma=False)
```

```python
import functools

import jax
import jax.numpy as jnp
import numpy as np
from jax import lax
from jax.experimental import pallas as pl
from jax.experimental.pallas import tpu as pltpu
from jax.sharding import PartitionSpec as P

SUBSTEPS = 2
ITERS = 4
step_size = 0.02

F32 = jnp.float32
BF16 = jnp.bfloat16


def legendre_seven(points):
    earlier = points * 0.0 + 1.0
    current = points
    for degree in range(1, 7):
        earlier, current = (
            current,
            ((2 * degree + 1) * points * current - degree * earlier) / (degree + 1),
        )
    return current


def host_tables():
    half = np.array([0.20929921790247888, 0.5917001814331423, 0.8717401485096066, 1.0])
    points = np.concatenate([-half[::-1], half])
    legendre = legendre_seven(points)
    weights = 2.0 / (56.0 * legendre**2)
    spacing = points[:, None] - points[None, :] + np.eye(8)
    derivative = legendre[:, None] / legendre[None, :] / spacing * (1.0 - np.eye(8))
    derivative[0, 0] = -14.0
    derivative[7, 7] = 14.0
    return weights, derivative


def tables():
    weights, derivative = host_tables()
    return (jnp.asarray(weights, F32), jnp.asarray(derivative, F32))


def split_matrix(matrix):
    matrix = matrix.astype(np.float32)
    high = matrix.astype(jnp.bfloat16)
    low = (matrix - high.astype(np.float32)).astype(jnp.bfloat16)
    return np.concatenate([high, high, low, low], axis=1)


def split_rows(values):
    high = values.astype(BF16)
    low = (values - high.astype(F32)).astype(BF16)
    return jnp.concatenate([high, low, high, low], axis=0)


def face_slices(direction, end):
    if direction == 0:
        return [pl.ds(448 * end, 64)]
    if direction == 1:
        return [pl.ds(64 * a + 56 * end, 8) for a in range(8)]
    return [pl.ds(7 * end, 64, stride=8)]


def load_face(ref, half, direction, end):
    parts = [ref[half, s, :] for s in face_slices(direction, end)]
    return parts[0] if len(parts) == 1 else jnp.concatenate(parts, axis=0)


def store_face(ref, half, direction, end, values):
    picks = face_slices(direction, end)
    size = 64 // len(picks)
    for i, s in enumerate(picks):
        ref[half, s, :] = values[i * size : (i + 1) * size]


def roll_lanes(parts, shift):
    turned = [pltpu.roll(part, shift, 1) for part in parts]
    lane = lax.broadcasted_iota(jnp.int32, parts[0].shape, 1)
    return [jnp.where(lane < shift, turned[i - 1], turned[i]) for i in range(len(parts))]


def roll_lanes_back(parts, shift):
    turned = [pltpu.roll(part, 128 - shift, 1) for part in parts]
    lane = lax.broadcasted_iota(jnp.int32, parts[0].shape, 1)
    count = len(parts)
    return [
        jnp.where(lane < 128 - shift, turned[i], turned[(i + 1) % count]) for i in range(count)
    ]


class Lanes:
    def __init__(self, counts):
        self.strides = (counts[1] * counts[2], counts[2], 1)
        lane = lax.broadcasted_iota(jnp.int32, (1, 128), 1)
        place = {1: (lane // counts[2]) % counts[1], 2: lane % counts[2]}
        self.has_next = {d: place[d] < counts[d] - 1 for d in (1, 2)}
        self.has_prev = {d: place[d] > 0 for d in (1, 2)}

    def factors(self, direction, mode):
        n, p = self.has_next[direction], self.has_prev[direction]
        if mode == "sum":
            return None, None, jnp.where(n, 1.0, 0.0), jnp.where(p, 1.0, 0.0)
        alone = 1.0 if mode == "avg" else 0.0
        return (
            jnp.where(n, 0.5, alone),
            jnp.where(p, 0.5, alone),
            jnp.where(n, 0.5, 0.0),
            jnp.where(p, 0.5, 0.0),
        )


def join(jobs, lanes):
    for direction in range(3):
        stride = lanes.strides[direction]
        for ref, mode in jobs:
            halves = range(ref.shape[0])
            lower = [load_face(ref, h, direction, 0) for h in halves]
            upper = [load_face(ref, h, direction, 1) for h in halves]
            if direction == 0:
                new_upper = [a + b for a, b in zip(upper, roll_lanes_back(lower, stride))]
                new_lower = [a + b for a, b in zip(lower, roll_lanes(upper, stride))]
                if mode != "sum":
                    new_upper = [0.5 * a for a in new_upper]
                    new_lower = [0.5 * a for a in new_lower]
            else:
                own_up, own_low, from_next, from_prev = lanes.factors(direction, mode)
                new_upper, new_lower = [], []
                for h in halves:
                    up, low = upper[h], lower[h]
                    if own_up is not None:
                        up, low = up * own_up, low * own_low
                    new_upper.append(up + pltpu.roll(lower[h], 128 - stride, 1) * from_next)
                    new_lower.append(low + pltpu.roll(upper[h], stride, 1) * from_prev)
            for h in halves:
                store_face(ref, h, direction, 0, new_lower[h])
                store_face(ref, h, direction, 1, new_upper[h])


def along_first(values, matrix, odd):
    total = [values[j] + values[7 - j] for j in range(4)]
    gap = [values[j] - values[7 - j] for j in range(4)]
    plus = 0.5 * (matrix[:4, :4] + matrix[:4, :3:-1])
    minus = 0.5 * (matrix[:4, :4] - matrix[:4, :3:-1])
    out = [None] * 8
    for i in range(4):
        from_total = total[0] * float(plus[i, 0])
        from_gap = gap[0] * float(minus[i, 0])
        for j in range(1, 4):
            from_total += total[j] * float(plus[i, j])
            from_gap += gap[j] * float(minus[i, j])
        out[i] = from_total + from_gap
        out[7 - i] = from_gap - from_total if odd else from_total - from_gap
    return out


def pack_kernel(velocity, reaction, out, held, sems):
    fields = velocity.shape[0]
    copies = [
        pltpu.make_async_copy(velocity, held.at[pl.ds(0, fields)], sems.at[0]),
        pltpu.make_async_copy(reaction, held.at[fields], sems.at[1]),
    ]
    for copy in copies:
        copy.start()
    is_low = lax.axis_index("gz") == 0
    for copy in copies:
        copy.wait()
    for k in range(fields + 1):
        low, high = held[k, 0, 0], held[k, 1, 0]
        straight = jnp.concatenate([low, high], axis=0)
        turned = jnp.concatenate([high, low], axis=0)
        block = jnp.where(is_low, straight, turned)
        for i in range(out.shape[0]):
            out[i, k] = block


def whole_kernel(devices, weights, derivative, *refs):
    count_x = devices[0]
    mine, others = refs[:count_x], refs[count_x : 2 * count_x]
    (
        cross_ref, matrix_ref,
        vel_out, pre_out, res_out,
        u, rm, w, dinv, p, r, y, x, flip, vel_own, pre_own, res_own, sems,
    ) = refs[2 * count_x :]
    my_y, my_z = lax.axis_index("gy"), lax.axis_index("gz")
    fields = u.shape[1]
    halves = range(u.shape[2])
    per_half = count_x // len(halves)
    lanes = Lanes((2 * devices[0], devices[1], 8))
    stiffness = derivative.T @ (weights[:, None] * derivative)
    stiff_sum = np.sum(weights[:, None] * derivative * derivative, axis=0)
    slabs = [pl.ds(64 * a, 64) for a in range(8)]
    columns = [[pl.ds(64 * a + 8 * b, 8) for a in range(8)] for b in range(8)]

    sublane = lax.broadcasted_iota(jnp.int32, (8, 128), 0)
    own_rows = (sublane < 4) == (my_z == 0)

    def to_lanes(k, target):
        for half in halves:
            for chunk in range(4):
                cols = pl.ds(128 * chunk, 128)
                blocks = []
                for i in range(per_half):
                    s = -(half * per_half + i) % count_x
                    first, second = [], []
                    for j in range(devices[1]):
                        here, there = mine[s][j, k, :, cols], others[s][j, k, :, cols]
                        first.append(jnp.where(own_rows, here, there))
                        second.append(pltpu.roll(jnp.where(own_rows, there, here), 4, 0))
                    blocks += first + second
                target[half, cols, :] = jnp.concatenate(blocks, axis=0).T

    for k in range(fields):
        to_lanes(k, u.at[0, k])
    to_lanes(fields, rm)

    for a in range(8):
        mass = cross_ref[pl.ds(0, 64), :] * float(weights[a])
        diag = cross_ref[pl.ds(0, 64), :] * float(stiff_sum[a])
        diag += cross_ref[pl.ds(64, 64), :] * float(weights[a])
        for h in halves:
            react = rm[h, slabs[a], :] * mass
            rm[h, slabs[a], :] = react
            dinv[h, slabs[a], :] = react + diag
    join([(u.at[0, k], "avg") for k in range(fields)] + [(dinv, "sum")], lanes)

    up, low, _, _ = lanes.factors(2, "avg")
    share_z = jnp.where(sublane == 7, up, jnp.where(sublane == 0, low, 1.0))
    up, low, _, _ = lanes.factors(1, "avg")
    for b in range(8):
        share = share_z * (low if b == 0 else up) if b in (0, 7) else share_z
        for a in range(8):
            for h in halves:
                inverse = 1.0 / dinv[h, columns[b][a], :]
                dinv[h, columns[b][a], :] = inverse
                w[h, columns[b][a], :] = inverse * (share * 0.5 if a in (0, 7) else share)

    def slab(ref, a):
        return split_rows(jnp.concatenate([ref[h, slabs[a], :] for h in halves], axis=1))

    def substep(step, carry):
        now, after = u.at[step % 2], u.at[1 - step % 2]
        for b in range(8):
            for h in halves:
                along = [now[0, h, columns[b][a], :] for a in range(8)]
                for k in range(fields):
                    values = [now[k, h, columns[b][a], :] for a in range(8)] if k else along
                    first = along_first(values, step_size * derivative, True)
                    for a in range(8):
                        after[k, h, columns[b][a], :] = values[a] - along[a] * first[a]
        for a in range(8):
            for k in range(fields):
                g = jnp.dot(
                    matrix_ref[pl.ds(0, 128), :], slab(now.at[k], a), preferred_element_type=F32
                )
                for h in halves:
                    cols = slice(128 * h, 128 * (h + 1))
                    after[k, h, slabs[a], :] -= (
                        now[1, h, slabs[a], :] * g[:64, cols] + now[2, h, slabs[a], :] * g[64:, cols]
                    )
        join([(after.at[k], "wall") for k in range(fields)], lanes)
        return carry

    lax.fori_loop(0, SUBSTEPS, substep, 0)
    now = u.at[SUBSTEPS % 2]

    def own_block(source, own):
        flip[...] = source.T
        size = own.shape[2]
        for i in range(own.shape[0]):
            start = i * lanes.strides[0] + my_y * lanes.strides[1]
            block = flip[pl.ds(pl.multiple_of(start, 8), 8), :]
            own[i, 0] = jnp.where(my_z == 0, block[:size], block[size:])

    for b in range(8):
        for h in halves:
            first = along_first(
                [now[0, h, columns[b][a], :] for a in range(8)], step_size * derivative, True
            )
            for a in range(8):
                r[h, columns[b][a], :] = first[a]
    for a in range(8):
        g = jnp.dot(matrix_ref[pl.ds(0, 64), :], slab(now.at[1], a), preferred_element_type=F32)
        g += jnp.dot(matrix_ref[pl.ds(64, 64), :], slab(now.at[2], a), preferred_element_type=F32)
        mass = cross_ref[pl.ds(0, 64), :] * float(-weights[a] / step_size)
        for h in halves:
            r[h, slabs[a], :] = mass * (r[h, slabs[a], :] + g[:, 128 * h : 128 * (h + 1)])
    join([(r, "sum")], lanes)

    for k in range(fields):
        own_block(now[k, 0], vel_own.at[k])
    send_velocity = pltpu.make_async_copy(vel_own, vel_out, sems.at[0])
    send_velocity.start()

    def total(acc):
        return jnp.sum(jnp.sum(acc, axis=0, keepdims=True), axis=1, keepdims=True)

    acc = jnp.zeros((64, 128), F32)
    for a in range(8):
        x[slabs[a], :] = jnp.zeros((64, 128), F32)
        for h in halves:
            res = r[h, slabs[a], :]
            p[h, slabs[a], :] = jnp.zeros((64, 128), F32)
            acc += res * res * w[h, slabs[a], :]

    def sweep(_, carry):
        progress, beta = carry
        for b in range(8):
            cross = cross_ref[pl.ds(8 * b, 8), :]
            for h in halves:
                search = []
                for a in range(8):
                    here = r[h, columns[b][a], :] * dinv[h, columns[b][a], :]
                    here += beta * p[h, columns[b][a], :]
                    p[h, columns[b][a], :] = here
                    search.append(here)
                first = along_first(search, stiffness, False)
                for a in range(8):
                    y[h, columns[b][a], :] = cross * first[a] + rm[h, columns[b][a], :] * search[a]
        acc = jnp.zeros((64, 128), F32)
        for a in range(8):
            at = 128 + 64 * min(a, 7 - a)
            g = jnp.dot(matrix_ref[pl.ds(at, 64), :], slab(p, a), preferred_element_type=F32)
            for h in halves:
                image = y[h, slabs[a], :] + g[:, 128 * h : 128 * (h + 1)]
                y[h, slabs[a], :] = image
                acc += image * p[h, slabs[a], :]
        alpha = progress / total(acc)
        join([(y, "sum")], lanes)
        acc = jnp.zeros((64, 128), F32)
        for a in range(8):
            x[slabs[a], :] += alpha * p[0, slabs[a], :]
            for h in halves:
                res = r[h, slabs[a], :] - alpha * y[h, slabs[a], :]
                r[h, slabs[a], :] = res
                acc += res * res * w[h, slabs[a], :]
        following = total(acc)
        return following, following / progress

    lax.fori_loop(0, ITERS, sweep, (total(acc), jnp.zeros((1, 1), F32)))

    own_block(x[...], pre_own)
    send_pressure = pltpu.make_async_copy(pre_own, pre_out, sems.at[1])
    send_pressure.start()
    own_block(r[0], res_own)
    send_residual = pltpu.make_async_copy(res_own, res_out, sems.at[2])
    send_residual.start()
    send_velocity.wait()
    send_pressure.wait()
    send_residual.wait()


def whole_body(devices, velocity, reaction):
    fields = velocity.shape[0]
    lanes = int(np.prod(devices)) * 8
    weights, derivative = host_tables()
    eye = np.eye(8)
    stiffness = derivative.T @ (weights[:, None] * derivative)
    stiff_sum = np.sum(weights[:, None] * derivative * derivative, axis=0)
    across = np.kron(stiffness, np.diag(weights)) + np.kron(np.diag(weights), stiffness)
    matrices = np.concatenate(
        [
            split_matrix(step_size * np.kron(derivative, eye)),
            split_matrix(step_size * np.kron(eye, derivative)),
        ]
        + [split_matrix(weights[a] * across) for a in range(4)]
    )
    cross = np.outer(weights, weights).reshape(-1)
    sides = np.outer(stiff_sum, weights).reshape(-1) + np.outer(weights, stiff_sum).reshape(-1)
    cross = np.broadcast_to(np.concatenate([cross, sides])[:, None], (128, 128))

    vmem = pl.BlockSpec(memory_space=pltpu.VMEM)
    hbm = pl.BlockSpec(memory_space=pltpu.HBM)
    packed = pl.pallas_call(
        pack_kernel,
        out_shape=jax.ShapeDtypeStruct((devices[1], fields + 1, 8, 512), F32),
        in_specs=[hbm, hbm],
        out_specs=vmem,
        scratch_shapes=[
            pltpu.VMEM((fields + 1,) + reaction.shape, F32),
            pltpu.SemaphoreType.DMA((2,)),
        ],
    )(velocity, reaction)

    def shifted(block, axis, step):
        count = lax.axis_size(axis)
        return lax.ppermute(block, axis, [(i, (i + step) % count) for i in range(count)])

    column = lax.all_to_all(packed, "gy", 0, 0, tiled=True)
    mine = [column] + [shifted(column, "gx", step) for step in range(1, devices[0])]
    others = [shifted(block, "gz", 1) for block in mine]

    field = pltpu.VMEM((lanes // 128, 512, 128), F32)
    own = pltpu.VMEM(reaction.shape, F32)
    return pl.pallas_call(
        functools.partial(whole_kernel, devices, weights, derivative),
        out_shape=(
            jax.ShapeDtypeStruct(velocity.shape, F32),
            jax.ShapeDtypeStruct(reaction.shape, F32),
            jax.ShapeDtypeStruct(reaction.shape, F32),
        ),
        in_specs=[vmem] * (2 * devices[0] + 2),
        out_specs=(hbm, hbm, hbm),
        scratch_shapes=[pltpu.VMEM((2, fields, lanes // 128, 512, 128), F32)]
        + [field] * 6
        + [
            pltpu.VMEM((512, 128), F32),
            pltpu.VMEM((128, 512), F32),
            pltpu.VMEM(velocity.shape, F32),
            own,
            own,
            pltpu.SemaphoreType.DMA((3,)),
        ],
        compiler_params=pltpu.CompilerParams(vmem_limit_bytes=40 << 20),
    )(
        *mine, *others, jnp.asarray(cross, F32), jnp.asarray(matrices),
    )


def extended(block, sides, width, periodic):
    for axis, dim in sides:
        count = lax.axis_size(axis)
        forward = [(i, i + 1) for i in range(count - 1)]
        if periodic:
            forward.append((count - 1, 0))
        backward = [(target, source) for source, target in forward]
        low = lax.ppermute(
            lax.slice_in_dim(block, block.shape[dim] - width, None, axis=dim), axis, forward
        )
        high = lax.ppermute(lax.slice_in_dim(block, 0, width, axis=dim), axis, backward)
        block = jnp.concatenate([low, block, high], axis=dim)
    return block


def derive(values, derivative, along_dim, transposed):
    layout = values.shape
    matrix = derivative.T if transposed else derivative
    blocks = values.reshape(-1, 8, 8, 8)
    patterns = ("aq,nqbc->nabc", "bq,naqc->nabc", "cq,nabq->nabc")
    result = jnp.einsum(patterns[along_dim], matrix, blocks, precision=lax.Precision.HIGHEST)
    return result.reshape(layout)


def place_face(values, target_axis, position, update):
    selector = tuple(
        (position if place == target_axis else slice(None) for place in range(values.ndim))
    )
    return values.at[selector].set(update)


def faces_along_x(sequence):
    return extended(sequence, (("gx", 0),), 1, True)


def faces_along_y(sequence):
    return extended(sequence, (("gy", 0),), 1, False)


def faces_along_z(sequence):
    return extended(sequence, (("gz", 0),), 1, False)


def join_faces(values, along_dim, exchanger):
    lower_face = jnp.moveaxis(jnp.take(values, 0, axis=4 + along_dim), 1 + along_dim, 0)
    upper_face = jnp.moveaxis(jnp.take(values, 7, axis=4 + along_dim), 1 + along_dim, 0)
    elements = lower_face.shape[0]
    face_shape = lower_face.shape
    sequence = jnp.stack([lower_face, upper_face], axis=1).reshape(2 * elements, -1)
    padded = exchanger(sequence)
    paired = padded.reshape(elements + 1, 2, -1)
    totals = paired[:, 0] + paired[:, 1]
    new_lower = jnp.moveaxis(totals[:-1].reshape(face_shape), 0, 1 + along_dim)
    new_upper = jnp.moveaxis(totals[1:].reshape(face_shape), 0, 1 + along_dim)
    values = place_face(values, 4 + along_dim, 0, new_lower)
    return place_face(values, 4 + along_dim, 7, new_upper)


def assemble(values):
    exchangers = (faces_along_x, faces_along_y, faces_along_z)
    dim_order = (0, 1, 2)
    for along_dim in dim_order:
        values = join_faces(values, along_dim, exchangers[along_dim])
    return values


def dim_factors(local_count, offset, total_count, bounded_by_walls):
    element_ids = offset + jnp.arange(local_count)
    node_ids = jnp.arange(8)
    at_end = (node_ids[None, :] == 0) | (node_ids[None, :] == 7)
    low_wall = (element_ids[:, None] == 0) & (node_ids[None, :] == 0)
    high_wall = (element_ids[:, None] == total_count - 1) & (node_ids[None, :] == 7)
    on_wall = (low_wall | high_wall) & bounded_by_walls
    shared = at_end & jnp.logical_not(on_wall)
    return (jnp.where(shared, 2.0, 1.0).astype(jnp.float32), on_wall.astype(jnp.float32))


def spread_body(velocity, reaction):
    weights, derivative = tables()
    count_x, count_y, count_z = (reaction.shape[0], reaction.shape[1], reaction.shape[2])
    speed = velocity.reshape(3, count_x, count_y, count_z, 8, 8, 8)
    react = reaction.reshape(1, count_x, count_y, count_z, 8, 8, 8)
    mass_matrix = weights[:, None, None] * weights[None, :, None] * weights[None, None, :]
    factor_x, wall_x = dim_factors(
        count_x, lax.axis_index("gx") * count_x, lax.axis_size("gx") * count_x, False
    )
    factor_y, wall_y = dim_factors(
        count_y, lax.axis_index("gy") * count_y, lax.axis_size("gy") * count_y, True
    )
    factor_z, wall_z = dim_factors(
        count_z, lax.axis_index("gz") * count_z, lax.axis_size("gz") * count_z, True
    )
    multiplicity = (
        factor_x[None, :, None, None, :, None, None]
        * factor_y[None, None, :, None, None, :, None]
        * factor_z[None, None, None, :, None, None, :]
    )
    interior = (1.0 - wall_y[None, None, :, None, None, :, None]) * (
        1.0 - wall_z[None, None, None, :, None, None, :]
    )
    stiff_sum = jnp.sum(weights[:, None] * derivative * derivative, axis=0)
    diag_local = (
        stiff_sum[:, None, None] * weights[None, :, None] * weights[None, None, :]
        + weights[:, None, None] * stiff_sum[None, :, None] * weights[None, None, :]
        + weights[:, None, None] * weights[None, :, None] * stiff_sum[None, None, :]
    )
    diag_terms = diag_local + react * mass_matrix
    speed = assemble(speed) / multiplicity
    diagonal = None
    for substep in range(SUBSTEPS):
        gradient_fields = [derive(speed, derivative, along_dim, False) for along_dim in range(3)]
        transport = (
            speed[0:1] * gradient_fields[0]
            + speed[1:2] * gradient_fields[1]
            + speed[2:3] * gradient_fields[2]
        )
        tendency = assemble(mass_matrix * transport) / (mass_matrix * multiplicity)
        speed = interior * (speed - step_size * tendency)
    spread = (
        derive(speed[0:1], derivative, 0, False)
        + derive(speed[1:2], derivative, 1, False)
        + derive(speed[2:3], derivative, 2, False)
    )
    source = -assemble(mass_matrix * spread)
    diagonal = assemble(diag_terms)

    def local_inner(first, second):
        return jnp.sum(first * second / multiplicity)

    def norm_weighted_mass(residual_vec, precond_vec):
        return lax.psum(local_inner(residual_vec, precond_vec), ("gx", "gy", "gz"))

    pressure = jnp.zeros_like(source)
    residual = source
    precond = residual / diagonal
    search = precond
    progress = norm_weighted_mass(residual, precond)
    for sweep_index in range(ITERS):
        local_sum = react * mass_matrix * search
        for apply_along_dim in range(3):
            local_sum = local_sum + derive(
                mass_matrix * derive(search, derivative, apply_along_dim, False),
                derivative,
                apply_along_dim,
                True,
            )
        applied = assemble(local_sum)
        step_length = progress / lax.psum(local_inner(search, applied), ("gx", "gy", "gz"))
        pressure = pressure + step_length * search
        residual = residual - step_length * applied
        precond = residual / diagonal
        progress_next = norm_weighted_mass(residual, precond)
        search = precond + progress_next / progress * search
        progress = progress_next
    return (
        speed.reshape(3, count_x, count_y, count_z, 512),
        pressure.reshape(count_x, count_y, count_z, 512),
        residual.reshape(count_x, count_y, count_z, 512),
    )


def solution(mesh):
    in_specs = (P(None, "gx", "gy", "gz", None), P("gx", "gy", "gz", None))
    out_specs = (
        P(None, "gx", "gy", "gz", None),
        P("gx", "gy", "gz", None),
        P("gx", "gy", "gz", None),
    )
    devices = tuple(mesh.shape[axis] for axis in ("gx", "gy", "gz"))

    def body(velocity, reaction):
        lanes = int(np.prod(reaction.shape[:3])) * int(np.prod(devices))
        blocks = reaction.shape[:3] == (2, 1, 4) and devices[0] % 2 == 0 and devices[2] == 2
        section = 8 * devices[1]
        if blocks and 128 % section == 0 and lanes == 256:
            return whole_body(devices, velocity, reaction)
        return spread_body(velocity, reaction)

    return jax.shard_map(body, mesh=mesh, in_specs=in_specs, out_specs=out_specs, check_vma=False)
```

```python
import functools

import jax
import jax.numpy as jnp
import numpy as np
from jax import lax
from jax.experimental import pallas as pl
from jax.experimental.pallas import tpu as pltpu
from jax.sharding import PartitionSpec as P

SUBSTEPS = 2
ITERS = 4
step_size = 0.02

F32 = jnp.float32
BF16 = jnp.bfloat16


def legendre_seven(points):
    earlier = points * 0.0 + 1.0
    current = points
    for degree in range(1, 7):
        earlier, current = (
            current,
            ((2 * degree + 1) * points * current - degree * earlier) / (degree + 1),
        )
    return current


def host_tables():
    half = np.array([0.20929921790247888, 0.5917001814331423, 0.8717401485096066, 1.0])
    points = np.concatenate([-half[::-1], half])
    legendre = legendre_seven(points)
    weights = 2.0 / (56.0 * legendre**2)
    spacing = points[:, None] - points[None, :] + np.eye(8)
    derivative = legendre[:, None] / legendre[None, :] / spacing * (1.0 - np.eye(8))
    derivative[0, 0] = -14.0
    derivative[7, 7] = 14.0
    return weights, derivative


def tables():
    weights, derivative = host_tables()
    return (jnp.asarray(weights, F32), jnp.asarray(derivative, F32))


def split_matrix(matrix):
    matrix = matrix.astype(np.float32)
    high = matrix.astype(jnp.bfloat16)
    low = (matrix - high.astype(np.float32)).astype(jnp.bfloat16)
    return np.concatenate([high, high, low, low], axis=1)


def split_rows(values):
    high = values.astype(BF16)
    low = (values - high.astype(F32)).astype(BF16)
    return jnp.concatenate([high, low, high, low], axis=0)


def roll_lanes(parts, shift):
    turned = [pltpu.roll(part, shift, 1) for part in parts]
    lane = lax.broadcasted_iota(jnp.int32, parts[0].shape, 1)
    return [jnp.where(lane < shift, turned[i - 1], turned[i]) for i in range(len(parts))]


def roll_lanes_back(parts, shift):
    turned = [pltpu.roll(part, 128 - shift, 1) for part in parts]
    lane = lax.broadcasted_iota(jnp.int32, parts[0].shape, 1)
    count = len(parts)
    return [
        jnp.where(lane < 128 - shift, turned[i], turned[(i + 1) % count]) for i in range(count)
    ]


class Lanes:
    def __init__(self, counts):
        self.strides = (counts[1] * counts[2], counts[2], 1)
        lane = lax.broadcasted_iota(jnp.int32, (1, 128), 1)
        place = {1: (lane // counts[2]) % counts[1], 2: lane % counts[2]}
        self.has_next = {d: place[d] < counts[d] - 1 for d in (1, 2)}
        self.has_prev = {d: place[d] > 0 for d in (1, 2)}

    def factors(self, direction, mode):
        n, p = self.has_next[direction], self.has_prev[direction]
        if mode == "sum":
            return None, None, jnp.where(n, 1.0, 0.0), jnp.where(p, 1.0, 0.0)
        alone = 1.0 if mode == "avg" else 0.0
        return (
            jnp.where(n, 0.5, alone),
            jnp.where(p, 0.5, alone),
            jnp.where(n, 0.5, 0.0),
            jnp.where(p, 0.5, 0.0),
        )


def settle(ref, slabs, lanes, mode):
    if 0 in slabs:
        lower, upper = slabs[0], slabs[7]
        stride = lanes.strides[0]
        new_upper = [a + b for a, b in zip(upper, roll_lanes_back(lower, stride))]
        new_lower = [a + b for a, b in zip(lower, roll_lanes(upper, stride))]
        if mode != "sum":
            new_upper = [0.5 * a for a in new_upper]
            new_lower = [0.5 * a for a in new_lower]
        slabs = {**slabs, 0: new_lower, 7: new_upper}

    def joined(lower, upper, direction):
        stride = lanes.strides[direction]
        own_up, own_low, from_next, from_prev = lanes.factors(direction, mode)
        up, low = (upper, lower) if own_up is None else (upper * own_up, lower * own_low)
        up = up + pltpu.roll(lower, 128 - stride, 1) * from_next
        return low + pltpu.roll(upper, stride, 1) * from_prev, up

    for a, parts in slabs.items():
        for h, part in enumerate(parts):
            lower, upper = joined(part[:8], part[56:], 1)
            ref[h, pl.ds(64 * a, 8), :] = lower
            ref[h, pl.ds(64 * a + 8, 48), :] = part[8:56]
            ref[h, pl.ds(64 * a + 56, 8), :] = upper
            first, last = pl.ds(64 * a, 8, stride=8), pl.ds(64 * a + 7, 8, stride=8)
            lower, upper = joined(ref[h, first, :], ref[h, last, :], 2)
            ref[h, first, :] = lower
            ref[h, last, :] = upper


SLAB_ORDER = ((0, 7), (1,), (2,), (3,), (4,), (5,), (6,))


def along_first(values, matrix, odd):
    total = [values[j] + values[7 - j] for j in range(4)]
    gap = [values[j] - values[7 - j] for j in range(4)]
    plus = 0.5 * (matrix[:4, :4] + matrix[:4, :3:-1])
    minus = 0.5 * (matrix[:4, :4] - matrix[:4, :3:-1])
    out = [None] * 8
    for i in range(4):
        from_total = total[0] * float(plus[i, 0])
        from_gap = gap[0] * float(minus[i, 0])
        for j in range(1, 4):
            from_total += total[j] * float(plus[i, j])
            from_gap += gap[j] * float(minus[i, j])
        out[i] = from_total + from_gap
        out[7 - i] = from_gap - from_total if odd else from_total - from_gap
    return out


def stack_kernel(counts, *refs):
    blocks, outs = refs[: sum(counts)], refs[sum(counts) :]
    for out, count in zip(outs, counts):
        for i in range(count):
            out[i] = blocks[i][...]
        blocks = blocks[count:]


def stacked(*groups):
    vmem = pl.BlockSpec(memory_space=pltpu.VMEM)
    counts = [len(group) for group in groups]
    return pl.pallas_call(
        functools.partial(stack_kernel, counts),
        out_shape=[jax.ShapeDtypeStruct((len(g),) + g[0].shape, F32) for g in groups],
        in_specs=[vmem] * sum(counts),
        out_specs=[vmem] * len(groups),
        compiler_params=pltpu.CompilerParams(vmem_limit_bytes=1 << 20),
    )(*(block for group in groups for block in group))


def whole_kernel(devices, weights, derivative, *refs):
    count_x = devices[0]
    mine, others = refs[:count_x], refs[count_x : 2 * count_x]
    (
        react_mine, react_others, cross_ref, matrix_ref,
        vel_out, pre_out, res_out,
        u, v, rm, w, dinv, z, r, y, s, p, x, flip, vel_own, pre_own, res_own, sems,
    ) = refs[2 * count_x :]
    my_y, my_z = lax.axis_index("gy"), lax.axis_index("gz")
    fields = u.shape[0]
    halves = range(u.shape[1])
    per_half = count_x // len(halves)
    lanes = Lanes((2 * devices[0], devices[1], 8))
    stiffness = derivative.T @ (weights[:, None] * derivative)
    stiff_sum = np.sum(weights[:, None] * derivative * derivative, axis=0)
    slab_rows = [pl.ds(64 * a, 64) for a in range(8)]
    columns = [[pl.ds(64 * a + 8 * b, 8) for a in range(8)] for b in range(8)]

    is_low = my_z == 0
    below = [(my_y + (devices[1] - j)) % devices[1] for j in range(devices[1])]

    def to_lanes(here_of, there_of, chunk):
        cols = pl.ds(128 * chunk, 128)
        parts = []
        for half in halves:
            tiles = []
            for i in range(per_half):
                piece = -(half * per_half + i) % count_x
                for local_x in range(2):
                    for at in below:
                        here = here_of(piece, at, local_x, cols)
                        there = there_of(piece, at, local_x, cols)
                        tiles.append(jnp.where(is_low, here, there))
                        tiles.append(jnp.where(is_low, there, here))
            parts.append(jnp.concatenate(tiles, axis=0).T)
        return parts

    def halves_of(parts, chunk):
        return {2 * chunk + i: [part[64 * i : 64 * i + 64] for part in parts] for i in range(2)}

    for k in range(fields):
        for chunks in ((0, 3), (1,), (2,)):
            slabs = {}
            for chunk in chunks:
                parts = to_lanes(
                    lambda piece, at, i, cols: mine[piece][at, k, i, 0, :, cols],
                    lambda piece, at, i, cols: others[piece][at, k, i, 0, :, cols],
                    chunk,
                )
                slabs.update(halves_of(parts, chunk))
            settle(u.at[k], slabs, lanes, "avg")

    for chunks in ((0, 3), (1,), (2,)):
        slabs = {}
        for chunk in chunks:
            parts = to_lanes(
                lambda piece, at, i, cols: react_mine[at, piece, i, 0, :, cols],
                lambda piece, at, i, cols: react_others[at, piece, i, 0, :, cols],
                chunk,
            )
            for a, react in halves_of(parts, chunk).items():
                mass = cross_ref[pl.ds(0, 64), :] * float(weights[a])
                diag = cross_ref[pl.ds(0, 64), :] * float(stiff_sum[a])
                diag += cross_ref[pl.ds(64, 64), :] * float(weights[a])
                react = [part * mass for part in react]
                for h in halves:
                    rm[h, slab_rows[a], :] = react[h]
                slabs[a] = [part + diag for part in react]
        settle(dinv, slabs, lanes, "sum")

    sublane = lax.broadcasted_iota(jnp.int32, (8, 128), 0)
    up, low, _, _ = lanes.factors(2, "avg")
    share_z = jnp.where(sublane == 7, up, jnp.where(sublane == 0, low, 1.0))
    up, low, _, _ = lanes.factors(1, "avg")
    for b in range(8):
        share = share_z * (low if b == 0 else up) if b in (0, 7) else share_z
        for a in range(8):
            for h in halves:
                inverse = 1.0 / dinv[h, columns[b][a], :]
                dinv[h, columns[b][a], :] = inverse
                w[h, columns[b][a], :] = inverse * (share * 0.5 if a in (0, 7) else share)

    def product(row, count, ref, a):
        values = jnp.concatenate([ref[h, slab_rows[a], :] for h in halves], axis=1)
        g = jnp.dot(
            matrix_ref[pl.ds(row, count), :], split_rows(values), preferred_element_type=F32
        )
        return [g[:, 128 * h : 128 * (h + 1)] for h in halves]

    now, after = u, v
    for _ in range(SUBSTEPS):
        for b in range(8):
            for h in halves:
                along = [now[0, h, columns[b][a], :] for a in range(8)]
                for k in range(fields):
                    values = [now[k, h, columns[b][a], :] for a in range(8)] if k else along
                    first = along_first(values, step_size * derivative, True)
                    for a in range(8):
                        after[k, h, columns[b][a], :] = values[a] - along[a] * first[a]
        for group in SLAB_ORDER:
            for k in range(fields):
                slabs = {}
                for a in group:
                    g = product(0, 128, now.at[k], a)
                    slabs[a] = [
                        after[k, h, slab_rows[a], :]
                        - now[1, h, slab_rows[a], :] * g[h][:64]
                        - now[2, h, slab_rows[a], :] * g[h][64:]
                        for h in halves
                    ]
                settle(after.at[k], slabs, lanes, "wall")
        now, after = after, now

    def own_block(source, own):
        flip[...] = source.T
        size = own.shape[2]
        for i in range(own.shape[0]):
            start = i * lanes.strides[0] + my_y * lanes.strides[1]
            block = flip[pl.ds(pl.multiple_of(start, 8), 8), :]
            own[i, 0] = jnp.where(is_low, block[:size], block[size:])

    for b in range(8):
        for h in halves:
            first = along_first(
                [now[0, h, columns[b][a], :] for a in range(8)], step_size * derivative, True
            )
            for a in range(8):
                r[h, columns[b][a], :] = first[a]
    for group in SLAB_ORDER:
        slabs = {}
        for a in group:
            second, third = product(0, 64, now.at[1], a), product(64, 64, now.at[2], a)
            mass = cross_ref[pl.ds(0, 64), :] * float(-weights[a] / step_size)
            slabs[a] = [
                mass * (r[h, slab_rows[a], :] + second[h] + third[h]) for h in halves
            ]
        settle(r, slabs, lanes, "sum")

    for k in range(fields):
        own_block(now[k, 0], vel_own.at[k])
    send_velocity = pltpu.make_async_copy(vel_own, vel_out, sems.at[0])
    send_velocity.start()

    def total(acc):
        return jnp.sum(jnp.sum(acc, axis=0, keepdims=True), axis=1, keepdims=True)

    def begin_sweep(update):
        acc = jnp.zeros((8, 128), F32)
        for b in range(8):
            cross = cross_ref[pl.ds(8 * b, 8), :]
            for h in halves:
                z_column = []
                for a in range(8):
                    rows = columns[b][a]
                    res = r[h, rows, :]
                    if update is not None:
                        alpha, beta = update
                        image = y[h, rows, :]
                        if beta is not None:
                            image = image + beta * s[h, rows, :]
                        s[h, rows, :] = image
                        res = res - alpha * image
                        r[h, rows, :] = res
                    acc += res * res * w[h, rows, :]
                    here = res * dinv[h, rows, :]
                    z[h, rows, :] = here
                    z_column.append(here)
                first = along_first(z_column, stiffness, False)
                for a in range(8):
                    rows = columns[b][a]
                    y[h, rows, :] = cross * first[a] + rm[h, rows, :] * z_column[a]
        return total(acc)

    gamma = begin_sweep(None)
    alpha = beta = None
    for sweep in range(ITERS):
        acc = jnp.zeros((64, 128), F32)
        for group in SLAB_ORDER:
            slabs = {}
            for a in group:
                g = product(128 + 64 * min(a, 7 - a), 64, z, a)
                slabs[a] = [y[h, slab_rows[a], :] + g[h] for h in halves]
                for h in halves:
                    acc += slabs[a][h] * z[h, slab_rows[a], :]
            settle(y, slabs, lanes, "sum")
        delta = total(acc)
        if sweep:
            beta = gamma / gamma_before
            alpha = gamma / (delta - beta * gamma / alpha)
        else:
            alpha = gamma / delta
        for rows in slab_rows:
            search = z[0, rows, :]
            if sweep:
                search = search + beta * p[rows, :]
            p[rows, :] = search
            x[rows, :] = x[rows, :] + alpha * search if sweep else alpha * search
        if sweep < ITERS - 1:
            gamma_before, gamma = gamma, begin_sweep((alpha, beta))
    for rows in slab_rows:
        r[0, rows, :] -= alpha * (y[0, rows, :] + beta * s[0, rows, :])

    own_block(x[...], pre_own)
    send_pressure = pltpu.make_async_copy(pre_own, pre_out, sems.at[1])
    send_pressure.start()
    own_block(r[0], res_own)
    send_residual = pltpu.make_async_copy(res_own, res_out, sems.at[2])
    send_residual.start()
    send_velocity.wait()
    send_pressure.wait()
    send_residual.wait()


def whole_body(devices, velocity, reaction):
    fields = velocity.shape[0]
    lanes = int(np.prod(devices)) * 8
    weights, derivative = host_tables()
    eye = np.eye(8)
    stiffness = derivative.T @ (weights[:, None] * derivative)
    stiff_sum = np.sum(weights[:, None] * derivative * derivative, axis=0)
    across = np.kron(stiffness, np.diag(weights)) + np.kron(np.diag(weights), stiffness)
    matrices = np.concatenate(
        [
            split_matrix(step_size * np.kron(derivative, eye)),
            split_matrix(step_size * np.kron(eye, derivative)),
        ]
        + [split_matrix(weights[a] * across) for a in range(4)]
    )
    cross = np.outer(weights, weights).reshape(-1)
    sides = np.outer(stiff_sum, weights).reshape(-1) + np.outer(weights, stiff_sum).reshape(-1)
    cross = np.broadcast_to(np.concatenate([cross, sides])[:, None], (128, 128))

    vmem = pl.BlockSpec(memory_space=pltpu.VMEM)
    hbm = pl.BlockSpec(memory_space=pltpu.HBM)
    def shifted(block, axis, step):
        count = lax.axis_size(axis)
        return lax.ppermute(block, axis, [(i, (i + step) % count) for i in range(count)])

    def around(block, axis):
        return [block] + [shifted(block, axis, step) for step in range(1, lax.axis_size(axis))]

    column_block, react_row = stacked(around(velocity, "gy"), around(reaction, "gx"))
    mine = around(column_block, "gx")
    others = [shifted(block, "gz", 1) for block in mine]
    (react_mine,) = stacked(around(react_row, "gy"))
    react_others = shifted(react_mine, "gz", 1)

    field = pltpu.VMEM((lanes // 128, 512, 128), F32)
    three = pltpu.VMEM((fields, lanes // 128, 512, 128), F32)
    one_half = pltpu.VMEM((512, 128), F32)
    own = pltpu.VMEM(reaction.shape, F32)
    return pl.pallas_call(
        functools.partial(whole_kernel, devices, weights, derivative),
        out_shape=(
            jax.ShapeDtypeStruct(velocity.shape, F32),
            jax.ShapeDtypeStruct(reaction.shape, F32),
            jax.ShapeDtypeStruct(reaction.shape, F32),
        ),
        in_specs=[vmem] * (2 * devices[0] + 4),
        out_specs=(hbm, hbm, hbm),
        scratch_shapes=[three, three]
        + [field] * 7
        + [one_half] * 2
        + [
            pltpu.VMEM((128, 512), F32),
            pltpu.VMEM(velocity.shape, F32),
            own,
            own,
            pltpu.SemaphoreType.DMA((3,)),
        ],
        compiler_params=pltpu.CompilerParams(vmem_limit_bytes=40 << 20),
    )(
        *mine, *others, react_mine, react_others,
        jnp.asarray(cross, F32), jnp.asarray(matrices),
    )


def extended(block, sides, width, periodic):
    for axis, dim in sides:
        count = lax.axis_size(axis)
        forward = [(i, i + 1) for i in range(count - 1)]
        if periodic:
            forward.append((count - 1, 0))
        backward = [(target, source) for source, target in forward]
        low = lax.ppermute(
            lax.slice_in_dim(block, block.shape[dim] - width, None, axis=dim), axis, forward
        )
        high = lax.ppermute(lax.slice_in_dim(block, 0, width, axis=dim), axis, backward)
        block = jnp.concatenate([low, block, high], axis=dim)
    return block


def derive(values, derivative, along_dim, transposed):
    layout = values.shape
    matrix = derivative.T if transposed else derivative
    blocks = values.reshape(-1, 8, 8, 8)
    patterns = ("aq,nqbc->nabc", "bq,naqc->nabc", "cq,nabq->nabc")
    result = jnp.einsum(patterns[along_dim], matrix, blocks, precision=lax.Precision.HIGHEST)
    return result.reshape(layout)


def place_face(values, target_axis, position, update):
    selector = tuple(
        (position if place == target_axis else slice(None) for place in range(values.ndim))
    )
    return values.at[selector].set(update)


def faces_along_x(sequence):
    return extended(sequence, (("gx", 0),), 1, True)


def faces_along_y(sequence):
    return extended(sequence, (("gy", 0),), 1, False)


def faces_along_z(sequence):
    return extended(sequence, (("gz", 0),), 1, False)


def join_faces(values, along_dim, exchanger):
    lower_face = jnp.moveaxis(jnp.take(values, 0, axis=4 + along_dim), 1 + along_dim, 0)
    upper_face = jnp.moveaxis(jnp.take(values, 7, axis=4 + along_dim), 1 + along_dim, 0)
    elements = lower_face.shape[0]
    face_shape = lower_face.shape
    sequence = jnp.stack([lower_face, upper_face], axis=1).reshape(2 * elements, -1)
    padded = exchanger(sequence)
    paired = padded.reshape(elements + 1, 2, -1)
    totals = paired[:, 0] + paired[:, 1]
    new_lower = jnp.moveaxis(totals[:-1].reshape(face_shape), 0, 1 + along_dim)
    new_upper = jnp.moveaxis(totals[1:].reshape(face_shape), 0, 1 + along_dim)
    values = place_face(values, 4 + along_dim, 0, new_lower)
    return place_face(values, 4 + along_dim, 7, new_upper)


def assemble(values):
    exchangers = (faces_along_x, faces_along_y, faces_along_z)
    dim_order = (0, 1, 2)
    for along_dim in dim_order:
        values = join_faces(values, along_dim, exchangers[along_dim])
    return values


def dim_factors(local_count, offset, total_count, bounded_by_walls):
    element_ids = offset + jnp.arange(local_count)
    node_ids = jnp.arange(8)
    at_end = (node_ids[None, :] == 0) | (node_ids[None, :] == 7)
    low_wall = (element_ids[:, None] == 0) & (node_ids[None, :] == 0)
    high_wall = (element_ids[:, None] == total_count - 1) & (node_ids[None, :] == 7)
    on_wall = (low_wall | high_wall) & bounded_by_walls
    shared = at_end & jnp.logical_not(on_wall)
    return (jnp.where(shared, 2.0, 1.0).astype(jnp.float32), on_wall.astype(jnp.float32))


def spread_body(velocity, reaction):
    weights, derivative = tables()
    count_x, count_y, count_z = (reaction.shape[0], reaction.shape[1], reaction.shape[2])
    speed = velocity.reshape(3, count_x, count_y, count_z, 8, 8, 8)
    react = reaction.reshape(1, count_x, count_y, count_z, 8, 8, 8)
    mass_matrix = weights[:, None, None] * weights[None, :, None] * weights[None, None, :]
    factor_x, wall_x = dim_factors(
        count_x, lax.axis_index("gx") * count_x, lax.axis_size("gx") * count_x, False
    )
    factor_y, wall_y = dim_factors(
        count_y, lax.axis_index("gy") * count_y, lax.axis_size("gy") * count_y, True
    )
    factor_z, wall_z = dim_factors(
        count_z, lax.axis_index("gz") * count_z, lax.axis_size("gz") * count_z, True
    )
    multiplicity = (
        factor_x[None, :, None, None, :, None, None]
        * factor_y[None, None, :, None, None, :, None]
        * factor_z[None, None, None, :, None, None, :]
    )
    interior = (1.0 - wall_y[None, None, :, None, None, :, None]) * (
        1.0 - wall_z[None, None, None, :, None, None, :]
    )
    stiff_sum = jnp.sum(weights[:, None] * derivative * derivative, axis=0)
    diag_local = (
        stiff_sum[:, None, None] * weights[None, :, None] * weights[None, None, :]
        + weights[:, None, None] * stiff_sum[None, :, None] * weights[None, None, :]
        + weights[:, None, None] * weights[None, :, None] * stiff_sum[None, None, :]
    )
    diag_terms = diag_local + react * mass_matrix
    speed = assemble(speed) / multiplicity
    diagonal = None
    for substep in range(SUBSTEPS):
        gradient_fields = [derive(speed, derivative, along_dim, False) for along_dim in range(3)]
        transport = (
            speed[0:1] * gradient_fields[0]
            + speed[1:2] * gradient_fields[1]
            + speed[2:3] * gradient_fields[2]
        )
        tendency = assemble(mass_matrix * transport) / (mass_matrix * multiplicity)
        speed = interior * (speed - step_size * tendency)
    spread = (
        derive(speed[0:1], derivative, 0, False)
        + derive(speed[1:2], derivative, 1, False)
        + derive(speed[2:3], derivative, 2, False)
    )
    source = -assemble(mass_matrix * spread)
    diagonal = assemble(diag_terms)

    def local_inner(first, second):
        return jnp.sum(first * second / multiplicity)

    def norm_weighted_mass(residual_vec, precond_vec):
        return lax.psum(local_inner(residual_vec, precond_vec), ("gx", "gy", "gz"))

    pressure = jnp.zeros_like(source)
    residual = source
    precond = residual / diagonal
    search = precond
    progress = norm_weighted_mass(residual, precond)
    for sweep_index in range(ITERS):
        local_sum = react * mass_matrix * search
        for apply_along_dim in range(3):
            local_sum = local_sum + derive(
                mass_matrix * derive(search, derivative, apply_along_dim, False),
                derivative,
                apply_along_dim,
                True,
            )
        applied = assemble(local_sum)
        step_length = progress / lax.psum(local_inner(search, applied), ("gx", "gy", "gz"))
        pressure = pressure + step_length * search
        residual = residual - step_length * applied
        precond = residual / diagonal
        progress_next = norm_weighted_mass(residual, precond)
        search = precond + progress_next / progress * search
        progress = progress_next
    return (
        speed.reshape(3, count_x, count_y, count_z, 512),
        pressure.reshape(count_x, count_y, count_z, 512),
        residual.reshape(count_x, count_y, count_z, 512),
    )


def solution(mesh):
    in_specs = (P(None, "gx", "gy", "gz", None), P("gx", "gy", "gz", None))
    out_specs = (
        P(None, "gx", "gy", "gz", None),
        P("gx", "gy", "gz", None),
        P("gx", "gy", "gz", None),
    )
    devices = tuple(mesh.shape[axis] for axis in ("gx", "gy", "gz"))

    def body(velocity, reaction):
        lanes = int(np.prod(reaction.shape[:3])) * int(np.prod(devices))
        blocks = reaction.shape[:3] == (2, 1, 4) and devices[0] % 2 == 0 and devices[2] == 2
        section = 8 * devices[1]
        if blocks and 128 % section == 0 and lanes == 256:
            return whole_body(devices, velocity, reaction)
        return spread_body(velocity, reaction)

    return jax.shard_map(body, mesh=mesh, in_specs=in_specs, out_specs=out_specs, check_vma=False)
```

```python
import functools

import jax
import jax.numpy as jnp
import numpy as np
from jax import lax
from jax.experimental import pallas as pl
from jax.experimental.pallas import tpu as pltpu
from jax.sharding import PartitionSpec as P

SUBSTEPS = 2
ITERS = 4
step_size = 0.02

F32 = jnp.float32
BF16 = jnp.bfloat16


def legendre_seven(points):
    earlier = points * 0.0 + 1.0
    current = points
    for degree in range(1, 7):
        earlier, current = (
            current,
            ((2 * degree + 1) * points * current - degree * earlier) / (degree + 1),
        )
    return current


def host_tables():
    half = np.array([0.20929921790247888, 0.5917001814331423, 0.8717401485096066, 1.0])
    points = np.concatenate([-half[::-1], half])
    legendre = legendre_seven(points)
    weights = 2.0 / (56.0 * legendre**2)
    spacing = points[:, None] - points[None, :] + np.eye(8)
    derivative = legendre[:, None] / legendre[None, :] / spacing * (1.0 - np.eye(8))
    derivative[0, 0] = -14.0
    derivative[7, 7] = 14.0
    return weights, derivative


def tables():
    weights, derivative = host_tables()
    return (jnp.asarray(weights, F32), jnp.asarray(derivative, F32))


def split_matrix(matrix):
    matrix = matrix.astype(np.float32)
    high = matrix.astype(jnp.bfloat16)
    low = (matrix - high.astype(np.float32)).astype(jnp.bfloat16)
    return np.concatenate([high, high, low, low], axis=1)


def split_rows(values):
    high = values.astype(BF16)
    low = (values - high.astype(F32)).astype(BF16)
    return jnp.concatenate([high, low, high, low], axis=0)


def roll_lanes(parts, shift):
    turned = [pltpu.roll(part, shift, 1) for part in parts]
    lane = lax.broadcasted_iota(jnp.int32, parts[0].shape, 1)
    return [jnp.where(lane < shift, turned[i - 1], turned[i]) for i in range(len(parts))]


def roll_lanes_back(parts, shift):
    turned = [pltpu.roll(part, 128 - shift, 1) for part in parts]
    lane = lax.broadcasted_iota(jnp.int32, parts[0].shape, 1)
    count = len(parts)
    return [
        jnp.where(lane < 128 - shift, turned[i], turned[(i + 1) % count]) for i in range(count)
    ]


class Lanes:
    def __init__(self, counts):
        self.strides = (counts[1] * counts[2], counts[2], 1)
        lane = lax.broadcasted_iota(jnp.int32, (1, 128), 1)
        place = {1: (lane // counts[2]) % counts[1], 2: lane % counts[2]}
        self.has_next = {d: place[d] < counts[d] - 1 for d in (1, 2)}
        self.has_prev = {d: place[d] > 0 for d in (1, 2)}

    def factors(self, direction, mode):
        n, p = self.has_next[direction], self.has_prev[direction]
        if mode == "sum":
            return None, None, jnp.where(n, 1.0, 0.0), jnp.where(p, 1.0, 0.0)
        alone = 1.0 if mode == "avg" else 0.0
        return (
            jnp.where(n, 0.5, alone),
            jnp.where(p, 0.5, alone),
            jnp.where(n, 0.5, 0.0),
            jnp.where(p, 0.5, 0.0),
        )


def settle(ref, slabs, lanes, mode):
    if 0 in slabs:
        lower, upper = slabs[0], slabs[7]
        stride = lanes.strides[0]
        new_upper = [a + b for a, b in zip(upper, roll_lanes_back(lower, stride))]
        new_lower = [a + b for a, b in zip(lower, roll_lanes(upper, stride))]
        if mode != "sum":
            new_upper = [0.5 * a for a in new_upper]
            new_lower = [0.5 * a for a in new_lower]
        slabs = {**slabs, 0: new_lower, 7: new_upper}

    def joined(lower, upper, direction):
        stride = lanes.strides[direction]
        own_up, own_low, from_next, from_prev = lanes.factors(direction, mode)
        up, low = (upper, lower) if own_up is None else (upper * own_up, lower * own_low)
        up = up + pltpu.roll(lower, 128 - stride, 1) * from_next
        return low + pltpu.roll(upper, stride, 1) * from_prev, up

    for a, parts in slabs.items():
        for h, part in enumerate(parts):
            lower, upper = joined(part[:8], part[56:], 1)
            ref[h, pl.ds(64 * a, 8), :] = lower
            ref[h, pl.ds(64 * a + 8, 48), :] = part[8:56]
            ref[h, pl.ds(64 * a + 56, 8), :] = upper
            first, last = pl.ds(64 * a, 8, stride=8), pl.ds(64 * a + 7, 8, stride=8)
            lower, upper = joined(ref[h, first, :], ref[h, last, :], 2)
            ref[h, first, :] = lower
            ref[h, last, :] = upper


SLAB_ORDER = ((0, 7), (1,), (2,), (3,), (4,), (5,), (6,))


def along_first(values, matrix, odd):
    total = [values[j] + values[7 - j] for j in range(4)]
    gap = [values[j] - values[7 - j] for j in range(4)]
    plus = 0.5 * (matrix[:4, :4] + matrix[:4, :3:-1])
    minus = 0.5 * (matrix[:4, :4] - matrix[:4, :3:-1])
    out = [None] * 8
    for i in range(4):
        from_total = total[0] * float(plus[i, 0])
        from_gap = gap[0] * float(minus[i, 0])
        for j in range(1, 4):
            from_total += total[j] * float(plus[i, j])
            from_gap += gap[j] * float(minus[i, j])
        out[i] = from_total + from_gap
        out[7 - i] = from_gap - from_total if odd else from_total - from_gap
    return out


def pack_kernel(velocity, reaction, out, sems):
    copies = [
        pltpu.make_async_copy(velocity, out.at[pl.ds(0, velocity.shape[0])], sems.at[0]),
        pltpu.make_async_copy(reaction, out.at[velocity.shape[0]], sems.at[1]),
    ]
    for copy in copies:
        copy.start()
    for copy in copies:
        copy.wait()


def column_kernel(*refs):
    blocks, outs = refs[:-2], refs[-2:]
    is_low = lax.axis_index("gz") == 0
    for j, block in enumerate(blocks):
        for k in range(block.shape[0]):
            low, high = block[k, 0, 0], block[k, 1, 0]
            straight = jnp.concatenate([low, high], axis=0)
            turned = jnp.concatenate([high, low], axis=0)
            outs[k // 2][j, k % 2] = jnp.where(is_low, straight, turned)


def stack_kernel(*refs):
    blocks, outs = refs[: len(refs) // 3 * 2], refs[len(refs) // 3 * 2 :]
    for i, block in enumerate(blocks):
        outs[i // 2][i % 2] = block[...]


SMALL = pltpu.CompilerParams(vmem_limit_bytes=1 << 20)


def in_pairs(*blocks):
    vmem = pl.BlockSpec(memory_space=pltpu.VMEM)
    count = len(blocks) // 2
    pair = jax.ShapeDtypeStruct((2,) + blocks[0].shape, F32)
    return pl.pallas_call(
        stack_kernel,
        out_shape=[pair] * count,
        in_specs=[vmem] * len(blocks),
        out_specs=[vmem] * count,
        compiler_params=SMALL,
    )(*blocks)


def whole_kernel(devices, weights, derivative, *refs):
    (
        near, far, near_other, far_other, cross_ref, matrix_ref,
        vel_out, pre_out, res_out,
        u, v, rm, w, dinv, z, r, y, s, p, x, flip, vel_own, pre_own, res_own, sems,
    ) = [refs[0:2], refs[2:4], refs[4:6], refs[6:8], *refs[8:]]
    my_y, my_z = lax.axis_index("gy"), lax.axis_index("gz")
    fields = u.shape[0]
    halves = range(u.shape[1])
    per_half = devices[0] // len(halves)
    lanes = Lanes((2 * devices[0], devices[1], 8))
    stiffness = derivative.T @ (weights[:, None] * derivative)
    stiff_sum = np.sum(weights[:, None] * derivative * derivative, axis=0)
    slab_rows = [pl.ds(64 * a, 64) for a in range(8)]
    columns = [[pl.ds(64 * a + 8 * b, 8) for a in range(8)] for b in range(8)]

    is_low = my_z == 0
    is_even = lax.axis_index("gx") % 2 == 0
    sublane = lax.broadcasted_iota(jnp.int32, (8, 128), 0)
    own_rows = (sublane < 4) == is_low
    entry = [my_y ^ j for j in range(devices[1])]

    def tile(near, far, k, ahead, at, cols):
        by_x = (near[0], 1) if k < 2 else (far[1], 0)
        diagonal = (far[k // 2], 1)
        if ahead == 0:
            ref, i = near[k // 2], 0
        elif ahead == 2:
            ref, i = (far[0], 0) if k < 2 else (near[1], 1)
        else:
            first, second = (by_x, diagonal) if ahead == 1 else (diagonal, by_x)
            first, second = (ref[i, at, k % 2, :, cols] for ref, i in (first, second))
            return jnp.where(is_even, first, second)
        return ref[i, at, k % 2, :, cols]

    def to_lanes(k, chunk):
        cols = pl.ds(128 * chunk, 128)
        parts = []
        for half in halves:
            tiles = []
            for i in range(per_half):
                first, second = [], []
                for at in entry:
                    here = tile(near, far, k, half * per_half + i, at, cols)
                    there = tile(near_other, far_other, k, half * per_half + i, at, cols)
                    first.append(jnp.where(own_rows, here, there))
                    second.append(pltpu.roll(jnp.where(own_rows, there, here), 4, 0))
                tiles += first + second
            parts.append(jnp.concatenate(tiles, axis=0).T)
        return parts

    def halves_of(parts, chunk):
        return {2 * chunk + i: [part[64 * i : 64 * i + 64] for part in parts] for i in range(2)}

    for k in range(fields):
        for chunks in ((0, 3), (1,), (2,)):
            slabs = {}
            for chunk in chunks:
                slabs.update(halves_of(to_lanes(k, chunk), chunk))
            settle(u.at[k], slabs, lanes, "avg")

    for chunks in ((0, 3), (1,), (2,)):
        slabs = {}
        for chunk in chunks:
            for a, react in halves_of(to_lanes(fields, chunk), chunk).items():
                mass = cross_ref[pl.ds(0, 64), :] * float(weights[a])
                diag = cross_ref[pl.ds(0, 64), :] * float(stiff_sum[a])
                diag += cross_ref[pl.ds(64, 64), :] * float(weights[a])
                react = [part * mass for part in react]
                for h in halves:
                    rm[h, slab_rows[a], :] = react[h]
                slabs[a] = [part + diag for part in react]
        settle(dinv, slabs, lanes, "sum")

    up, low, _, _ = lanes.factors(2, "avg")
    share_z = jnp.where(sublane == 7, up, jnp.where(sublane == 0, low, 1.0))
    up, low, _, _ = lanes.factors(1, "avg")
    for b in range(8):
        share = share_z * (low if b == 0 else up) if b in (0, 7) else share_z
        for a in range(8):
            for h in halves:
                inverse = 1.0 / dinv[h, columns[b][a], :]
                dinv[h, columns[b][a], :] = inverse
                w[h, columns[b][a], :] = inverse * (share * 0.5 if a in (0, 7) else share)

    def product(row, count, ref, a):
        values = jnp.concatenate([ref[h, slab_rows[a], :] for h in halves], axis=1)
        g = jnp.dot(
            matrix_ref[pl.ds(row, count), :], split_rows(values), preferred_element_type=F32
        )
        return [g[:, 128 * h : 128 * (h + 1)] for h in halves]

    now, after = u, v
    for _ in range(SUBSTEPS):
        for b in range(8):
            for h in halves:
                along = [now[0, h, columns[b][a], :] for a in range(8)]
                for k in range(fields):
                    values = [now[k, h, columns[b][a], :] for a in range(8)] if k else along
                    first = along_first(values, step_size * derivative, True)
                    for a in range(8):
                        after[k, h, columns[b][a], :] = values[a] - along[a] * first[a]
        for group in SLAB_ORDER:
            for k in range(fields):
                slabs = {}
                for a in group:
                    g = product(0, 128, now.at[k], a)
                    slabs[a] = [
                        after[k, h, slab_rows[a], :]
                        - now[1, h, slab_rows[a], :] * g[h][:64]
                        - now[2, h, slab_rows[a], :] * g[h][64:]
                        for h in halves
                    ]
                settle(after.at[k], slabs, lanes, "wall")
        now, after = after, now

    def own_block(source, own):
        flip[...] = source.T
        size = own.shape[2]
        for i in range(own.shape[0]):
            start = i * lanes.strides[0] + my_y * lanes.strides[1]
            block = flip[pl.ds(pl.multiple_of(start, 8), 8), :]
            own[i, 0] = jnp.where(is_low, block[:size], block[size:])

    for b in range(8):
        for h in halves:
            first = along_first(
                [now[0, h, columns[b][a], :] for a in range(8)], step_size * derivative, True
            )
            for a in range(8):
                r[h, columns[b][a], :] = first[a]
    for group in SLAB_ORDER:
        slabs = {}
        for a in group:
            second, third = product(0, 64, now.at[1], a), product(64, 64, now.at[2], a)
            mass = cross_ref[pl.ds(0, 64), :] * float(-weights[a] / step_size)
            slabs[a] = [
                mass * (r[h, slab_rows[a], :] + second[h] + third[h]) for h in halves
            ]
        settle(r, slabs, lanes, "sum")

    for k in range(fields):
        own_block(now[k, 0], vel_own.at[k])
    send_velocity = pltpu.make_async_copy(vel_own, vel_out, sems.at[0])
    send_velocity.start()

    def total(acc):
        return jnp.sum(jnp.sum(acc, axis=0, keepdims=True), axis=1, keepdims=True)

    def begin_sweep(update):
        acc = jnp.zeros((8, 128), F32)
        for b in range(8):
            cross = cross_ref[pl.ds(8 * b, 8), :]
            for h in halves:
                z_column = []
                for a in range(8):
                    rows = columns[b][a]
                    res = r[h, rows, :]
                    if update is not None:
                        alpha, beta = update
                        image = y[h, rows, :]
                        if beta is not None:
                            image = image + beta * s[h, rows, :]
                        s[h, rows, :] = image
                        res = res - alpha * image
                        r[h, rows, :] = res
                    acc += res * res * w[h, rows, :]
                    here = res * dinv[h, rows, :]
                    z[h, rows, :] = here
                    z_column.append(here)
                first = along_first(z_column, stiffness, False)
                for a in range(8):
                    rows = columns[b][a]
                    y[h, rows, :] = cross * first[a] + rm[h, rows, :] * z_column[a]
        return total(acc)

    gamma = begin_sweep(None)
    alpha = beta = None
    for sweep in range(ITERS):
        acc = jnp.zeros((64, 128), F32)
        for group in SLAB_ORDER:
            slabs = {}
            for a in group:
                g = product(128 + 64 * min(a, 7 - a), 64, z, a)
                slabs[a] = [y[h, slab_rows[a], :] + g[h] for h in halves]
                for h in halves:
                    acc += slabs[a][h] * z[h, slab_rows[a], :]
            settle(y, slabs, lanes, "sum")
        delta = total(acc)
        if sweep:
            beta = gamma / gamma_before
            alpha = gamma / (delta - beta * gamma / alpha)
        else:
            alpha = gamma / delta
        for rows in slab_rows:
            search = z[0, rows, :]
            if sweep:
                search = search + beta * p[rows, :]
            p[rows, :] = search
            x[rows, :] = x[rows, :] + alpha * search if sweep else alpha * search
        if sweep < ITERS - 1:
            gamma_before, gamma = gamma, begin_sweep((alpha, beta))
    for rows in slab_rows:
        r[0, rows, :] -= alpha * (y[0, rows, :] + beta * s[0, rows, :])

    own_block(x[...], pre_own)
    send_pressure = pltpu.make_async_copy(pre_own, pre_out, sems.at[1])
    send_pressure.start()
    own_block(r[0], res_own)
    send_residual = pltpu.make_async_copy(res_own, res_out, sems.at[2])
    send_residual.start()
    send_velocity.wait()
    send_pressure.wait()
    send_residual.wait()


def whole_body(devices, velocity, reaction):
    fields = velocity.shape[0]
    lanes = int(np.prod(devices)) * 8
    weights, derivative = host_tables()
    eye = np.eye(8)
    stiffness = derivative.T @ (weights[:, None] * derivative)
    stiff_sum = np.sum(weights[:, None] * derivative * derivative, axis=0)
    across = np.kron(stiffness, np.diag(weights)) + np.kron(np.diag(weights), stiffness)
    matrices = np.concatenate(
        [
            split_matrix(step_size * np.kron(derivative, eye)),
            split_matrix(step_size * np.kron(eye, derivative)),
        ]
        + [split_matrix(weights[a] * across) for a in range(4)]
    )
    cross = np.outer(weights, weights).reshape(-1)
    sides = np.outer(stiff_sum, weights).reshape(-1) + np.outer(weights, stiff_sum).reshape(-1)
    cross = np.broadcast_to(np.concatenate([cross, sides])[:, None], (128, 128))

    vmem = pl.BlockSpec(memory_space=pltpu.VMEM)
    hbm = pl.BlockSpec(memory_space=pltpu.HBM)
    def swapped(block, axis, mask):
        count = lax.axis_size(axis)
        return lax.ppermute(block, axis, [(i, i ^ mask) for i in range(count)])

    block = pl.pallas_call(
        pack_kernel,
        out_shape=jax.ShapeDtypeStruct((fields + 1,) + reaction.shape, F32),
        in_specs=[hbm, hbm],
        out_specs=vmem,
        scratch_shapes=[pltpu.SemaphoreType.DMA((2,))],
        compiler_params=SMALL,
    )(velocity, reaction)
    column = jax.ShapeDtypeStruct((devices[1], 2, 8, 512), F32)
    first, second = pl.pallas_call(
        column_kernel,
        out_shape=[column, column],
        in_specs=[vmem] * devices[1],
        out_specs=[vmem, vmem],
        compiler_params=SMALL,
    )(block, *(swapped(block, "gy", mask) for mask in range(1, devices[1])))
    near = in_pairs(first, swapped(first, "gx", 1), second, swapped(second, "gx", 2))
    far = [swapped(near[0], "gx", 2), swapped(near[1], "gx", 1)]
    others = [swapped(pair, "gz", 1) for pair in (*near, *far)]

    field = pltpu.VMEM((lanes // 128, 512, 128), F32)
    three = pltpu.VMEM((fields, lanes // 128, 512, 128), F32)
    one_half = pltpu.VMEM((512, 128), F32)
    own = pltpu.VMEM(reaction.shape, F32)
    return pl.pallas_call(
        functools.partial(whole_kernel, devices, weights, derivative),
        out_shape=(
            jax.ShapeDtypeStruct(velocity.shape, F32),
            jax.ShapeDtypeStruct(reaction.shape, F32),
            jax.ShapeDtypeStruct(reaction.shape, F32),
        ),
        in_specs=[vmem] * 10,
        out_specs=(hbm, hbm, hbm),
        scratch_shapes=[three, three]
        + [field] * 7
        + [one_half] * 2
        + [
            pltpu.VMEM((128, 512), F32),
            pltpu.VMEM(velocity.shape, F32),
            own,
            own,
            pltpu.SemaphoreType.DMA((3,)),
        ],
        compiler_params=pltpu.CompilerParams(vmem_limit_bytes=40 << 20),
    )(
        *near, *far, *others, jnp.asarray(cross, F32), jnp.asarray(matrices),
    )


def extended(block, sides, width, periodic):
    for axis, dim in sides:
        count = lax.axis_size(axis)
        forward = [(i, i + 1) for i in range(count - 1)]
        if periodic:
            forward.append((count - 1, 0))
        backward = [(target, source) for source, target in forward]
        low = lax.ppermute(
            lax.slice_in_dim(block, block.shape[dim] - width, None, axis=dim), axis, forward
        )
        high = lax.ppermute(lax.slice_in_dim(block, 0, width, axis=dim), axis, backward)
        block = jnp.concatenate([low, block, high], axis=dim)
    return block


def derive(values, derivative, along_dim, transposed):
    layout = values.shape
    matrix = derivative.T if transposed else derivative
    blocks = values.reshape(-1, 8, 8, 8)
    patterns = ("aq,nqbc->nabc", "bq,naqc->nabc", "cq,nabq->nabc")
    result = jnp.einsum(patterns[along_dim], matrix, blocks, precision=lax.Precision.HIGHEST)
    return result.reshape(layout)


def place_face(values, target_axis, position, update):
    selector = tuple(
        (position if place == target_axis else slice(None) for place in range(values.ndim))
    )
    return values.at[selector].set(update)


def faces_along_x(sequence):
    return extended(sequence, (("gx", 0),), 1, True)


def faces_along_y(sequence):
    return extended(sequence, (("gy", 0),), 1, False)


def faces_along_z(sequence):
    return extended(sequence, (("gz", 0),), 1, False)


def join_faces(values, along_dim, exchanger):
    lower_face = jnp.moveaxis(jnp.take(values, 0, axis=4 + along_dim), 1 + along_dim, 0)
    upper_face = jnp.moveaxis(jnp.take(values, 7, axis=4 + along_dim), 1 + along_dim, 0)
    elements = lower_face.shape[0]
    face_shape = lower_face.shape
    sequence = jnp.stack([lower_face, upper_face], axis=1).reshape(2 * elements, -1)
    padded = exchanger(sequence)
    paired = padded.reshape(elements + 1, 2, -1)
    totals = paired[:, 0] + paired[:, 1]
    new_lower = jnp.moveaxis(totals[:-1].reshape(face_shape), 0, 1 + along_dim)
    new_upper = jnp.moveaxis(totals[1:].reshape(face_shape), 0, 1 + along_dim)
    values = place_face(values, 4 + along_dim, 0, new_lower)
    return place_face(values, 4 + along_dim, 7, new_upper)


def assemble(values):
    exchangers = (faces_along_x, faces_along_y, faces_along_z)
    dim_order = (0, 1, 2)
    for along_dim in dim_order:
        values = join_faces(values, along_dim, exchangers[along_dim])
    return values


def dim_factors(local_count, offset, total_count, bounded_by_walls):
    element_ids = offset + jnp.arange(local_count)
    node_ids = jnp.arange(8)
    at_end = (node_ids[None, :] == 0) | (node_ids[None, :] == 7)
    low_wall = (element_ids[:, None] == 0) & (node_ids[None, :] == 0)
    high_wall = (element_ids[:, None] == total_count - 1) & (node_ids[None, :] == 7)
    on_wall = (low_wall | high_wall) & bounded_by_walls
    shared = at_end & jnp.logical_not(on_wall)
    return (jnp.where(shared, 2.0, 1.0).astype(jnp.float32), on_wall.astype(jnp.float32))


def spread_body(velocity, reaction):
    weights, derivative = tables()
    count_x, count_y, count_z = (reaction.shape[0], reaction.shape[1], reaction.shape[2])
    speed = velocity.reshape(3, count_x, count_y, count_z, 8, 8, 8)
    react = reaction.reshape(1, count_x, count_y, count_z, 8, 8, 8)
    mass_matrix = weights[:, None, None] * weights[None, :, None] * weights[None, None, :]
    factor_x, wall_x = dim_factors(
        count_x, lax.axis_index("gx") * count_x, lax.axis_size("gx") * count_x, False
    )
    factor_y, wall_y = dim_factors(
        count_y, lax.axis_index("gy") * count_y, lax.axis_size("gy") * count_y, True
    )
    factor_z, wall_z = dim_factors(
        count_z, lax.axis_index("gz") * count_z, lax.axis_size("gz") * count_z, True
    )
    multiplicity = (
        factor_x[None, :, None, None, :, None, None]
        * factor_y[None, None, :, None, None, :, None]
        * factor_z[None, None, None, :, None, None, :]
    )
    interior = (1.0 - wall_y[None, None, :, None, None, :, None]) * (
        1.0 - wall_z[None, None, None, :, None, None, :]
    )
    stiff_sum = jnp.sum(weights[:, None] * derivative * derivative, axis=0)
    diag_local = (
        stiff_sum[:, None, None] * weights[None, :, None] * weights[None, None, :]
        + weights[:, None, None] * stiff_sum[None, :, None] * weights[None, None, :]
        + weights[:, None, None] * weights[None, :, None] * stiff_sum[None, None, :]
    )
    diag_terms = diag_local + react * mass_matrix
    speed = assemble(speed) / multiplicity
    diagonal = None
    for substep in range(SUBSTEPS):
        gradient_fields = [derive(speed, derivative, along_dim, False) for along_dim in range(3)]
        transport = (
            speed[0:1] * gradient_fields[0]
            + speed[1:2] * gradient_fields[1]
            + speed[2:3] * gradient_fields[2]
        )
        tendency = assemble(mass_matrix * transport) / (mass_matrix * multiplicity)
        speed = interior * (speed - step_size * tendency)
    spread = (
        derive(speed[0:1], derivative, 0, False)
        + derive(speed[1:2], derivative, 1, False)
        + derive(speed[2:3], derivative, 2, False)
    )
    source = -assemble(mass_matrix * spread)
    diagonal = assemble(diag_terms)

    def local_inner(first, second):
        return jnp.sum(first * second / multiplicity)

    def norm_weighted_mass(residual_vec, precond_vec):
        return lax.psum(local_inner(residual_vec, precond_vec), ("gx", "gy", "gz"))

    pressure = jnp.zeros_like(source)
    residual = source
    precond = residual / diagonal
    search = precond
    progress = norm_weighted_mass(residual, precond)
    for sweep_index in range(ITERS):
        local_sum = react * mass_matrix * search
        for apply_along_dim in range(3):
            local_sum = local_sum + derive(
                mass_matrix * derive(search, derivative, apply_along_dim, False),
                derivative,
                apply_along_dim,
                True,
            )
        applied = assemble(local_sum)
        step_length = progress / lax.psum(local_inner(search, applied), ("gx", "gy", "gz"))
        pressure = pressure + step_length * search
        residual = residual - step_length * applied
        precond = residual / diagonal
        progress_next = norm_weighted_mass(residual, precond)
        search = precond + progress_next / progress * search
        progress = progress_next
    return (
        speed.reshape(3, count_x, count_y, count_z, 512),
        pressure.reshape(count_x, count_y, count_z, 512),
        residual.reshape(count_x, count_y, count_z, 512),
    )


def solution(mesh):
    in_specs = (P(None, "gx", "gy", "gz", None), P("gx", "gy", "gz", None))
    out_specs = (
        P(None, "gx", "gy", "gz", None),
        P("gx", "gy", "gz", None),
        P("gx", "gy", "gz", None),
    )
    devices = tuple(mesh.shape[axis] for axis in ("gx", "gy", "gz"))

    def body(velocity, reaction):
        if devices == (4, 4, 2) and reaction.shape[:3] == (2, 1, 4):
            return whole_body(devices, velocity, reaction)
        return spread_body(velocity, reaction)

    return jax.shard_map(body, mesh=mesh, in_specs=in_specs, out_specs=out_specs, check_vma=False)
```

```python
import functools

import jax
import jax.numpy as jnp
import numpy as np
from jax import lax
from jax.experimental import pallas as pl
from jax.experimental.pallas import tpu as pltpu
from jax.sharding import PartitionSpec as P

SUBSTEPS = 2
ITERS = 4
step_size = 0.02

F32 = jnp.float32
BF16 = jnp.bfloat16


def legendre_seven(points):
    earlier = points * 0.0 + 1.0
    current = points
    for degree in range(1, 7):
        earlier, current = (
            current,
            ((2 * degree + 1) * points * current - degree * earlier) / (degree + 1),
        )
    return current


def host_tables():
    half = np.array([0.20929921790247888, 0.5917001814331423, 0.8717401485096066, 1.0])
    points = np.concatenate([-half[::-1], half])
    legendre = legendre_seven(points)
    weights = 2.0 / (56.0 * legendre**2)
    spacing = points[:, None] - points[None, :] + np.eye(8)
    derivative = legendre[:, None] / legendre[None, :] / spacing * (1.0 - np.eye(8))
    derivative[0, 0] = -14.0
    derivative[7, 7] = 14.0
    return weights, derivative


def tables():
    weights, derivative = host_tables()
    return (jnp.asarray(weights, F32), jnp.asarray(derivative, F32))


def split_matrix(matrix):
    matrix = matrix.astype(np.float32)
    high = matrix.astype(jnp.bfloat16)
    low = (matrix - high.astype(np.float32)).astype(jnp.bfloat16)
    return np.concatenate([high, high, low, low], axis=1)


def split_parts(values):
    high = values.astype(BF16)
    return high, (values - high.astype(F32)).astype(BF16)


def roll_lanes(parts, shift):
    turned = [pltpu.roll(part, shift, 1) for part in parts]
    lane = lax.broadcasted_iota(jnp.int32, parts[0].shape, 1)
    return [jnp.where(lane < shift, turned[i - 1], turned[i]) for i in range(len(parts))]


def roll_lanes_back(parts, shift):
    turned = [pltpu.roll(part, 128 - shift, 1) for part in parts]
    lane = lax.broadcasted_iota(jnp.int32, parts[0].shape, 1)
    count = len(parts)
    return [
        jnp.where(lane < 128 - shift, turned[i], turned[(i + 1) % count]) for i in range(count)
    ]


class Lanes:
    def __init__(self, counts):
        self.strides = (counts[1] * counts[2], counts[2], 1)
        lane = lax.broadcasted_iota(jnp.int32, (1, 128), 1)
        place = {1: (lane // counts[2]) % counts[1], 2: lane % counts[2]}
        self.has_next = {d: place[d] < counts[d] - 1 for d in (1, 2)}
        self.has_prev = {d: place[d] > 0 for d in (1, 2)}

    def factors(self, direction, mode):
        n, p = self.has_next[direction], self.has_prev[direction]
        if mode == "sum":
            return None, None, jnp.where(n, 1.0, 0.0), jnp.where(p, 1.0, 0.0)
        alone = 1.0 if mode == "avg" else 0.0
        return (
            jnp.where(n, 0.5, alone),
            jnp.where(p, 0.5, alone),
            jnp.where(n, 0.5, 0.0),
            jnp.where(p, 0.5, 0.0),
        )


def settle(ref, slabs, lanes, mode, split=None):
    if 0 in slabs:
        lower, upper = slabs[0], slabs[7]
        stride = lanes.strides[0]
        new_upper = [a + b for a, b in zip(upper, roll_lanes_back(lower, stride))]
        new_lower = [a + b for a, b in zip(lower, roll_lanes(upper, stride))]
        if mode != "sum":
            new_upper = [0.5 * a for a in new_upper]
            new_lower = [0.5 * a for a in new_lower]
        slabs = {**slabs, 0: new_lower, 7: new_upper}

    def joined(lower, upper, direction):
        stride = lanes.strides[direction]
        own_up, own_low, from_next, from_prev = lanes.factors(direction, mode)
        following, previous = pltpu.roll(lower, 128 - stride, 1), pltpu.roll(upper, stride, 1)
        if mode == "sum":
            return lower + previous * from_prev, upper + following * from_next
        if mode == "wall":
            return (lower + previous) * from_prev, (upper + following) * from_next
        return lower * own_low + previous * from_prev, upper * own_up + following * from_next

    for a, parts in slabs.items():
        for h, part in enumerate(parts):
            lower, upper = joined(part[:8], part[56:], 1)
            ref[h, pl.ds(64 * a, 8), :] = lower
            ref[h, pl.ds(64 * a + 8, 48), :] = part[8:56]
            ref[h, pl.ds(64 * a + 56, 8), :] = upper
            first, last = pl.ds(64 * a, 8, stride=8), pl.ds(64 * a + 7, 8, stride=8)
            lower, upper = joined(ref[h, first, :], ref[h, last, :], 2)
            ref[h, first, :] = lower
            ref[h, last, :] = upper
        if split is not None:
            store_split(split, ref, a)


def store_split(split, ref, a):
    rows = pl.ds(64 * a, 64)
    values = jnp.concatenate([ref[h, rows, :] for h in range(ref.shape[0])], axis=1)
    split[0, rows, :], split[1, rows, :] = split_parts(values)


SLAB_ORDER = ((0, 7), (1,), (2,), (3,), (4,), (5,), (6,))


def column_kernel(*refs):
    blocks, outs = refs[:-2], refs[-2:]
    is_low = lax.axis_index("gz") == 0
    for j, block in enumerate(blocks):
        for k in range(block.shape[0]):
            low, high = block[k, 0, 0], block[k, 1, 0]
            straight = jnp.concatenate([low, high], axis=0)
            turned = jnp.concatenate([high, low], axis=0)
            outs[k // 2][j, k % 2] = jnp.where(is_low, straight, turned)


def stack_kernel(*refs):
    blocks, outs = refs[: len(refs) // 3 * 2], refs[len(refs) // 3 * 2 :]
    for i, block in enumerate(blocks):
        outs[i // 2][i % 2] = block[...]


SMALL = pltpu.CompilerParams(vmem_limit_bytes=1 << 20)


def in_pairs(*blocks):
    vmem = pl.BlockSpec(memory_space=pltpu.VMEM)
    count = len(blocks) // 2
    pair = jax.ShapeDtypeStruct((2,) + blocks[0].shape, F32)
    return pl.pallas_call(
        stack_kernel,
        out_shape=[pair] * count,
        in_specs=[vmem] * len(blocks),
        out_specs=[vmem] * count,
        compiler_params=SMALL,
    )(*blocks)


def whole_kernel(devices, weights, derivative, *refs):
    (
        near, far, near_other, far_other, cross_ref, matrix_ref, pair_ref,
        vel_out, pre_out, res_out,
        u, v, xs, rm, w, dinv, z, r, y, s, p, x, flip, vel_own, pre_own, res_own, sems,
    ) = [refs[0:2], refs[2:4], refs[4:6], refs[6:8], *refs[8:]]
    my_y, my_z = lax.axis_index("gy"), lax.axis_index("gz")
    fields = u.shape[0]
    halves = range(u.shape[1])
    per_half = devices[0] // len(halves)
    lanes = Lanes((2 * devices[0], devices[1], 8))
    stiff_sum = np.sum(weights[:, None] * derivative * derivative, axis=0)
    slab_rows = [pl.ds(64 * a, 64) for a in range(8)]
    columns = [[pl.ds(64 * a + 8 * b, 8) for a in range(8)] for b in range(8)]
    pair_rows = [[pl.ds(64 * a + 16 * j, 16) for a in range(8)] for j in range(4)]

    is_low = my_z == 0
    is_even = lax.axis_index("gx") % 2 == 0
    sublane = lax.broadcasted_iota(jnp.int32, (8, 128), 0)
    own_rows = (sublane < 4) == is_low
    entry = [my_y ^ j for j in range(devices[1])]

    def tile(near, far, k, ahead, at, cols):
        by_x = (near[0], 1) if k < 2 else (far[1], 0)
        diagonal = (far[k // 2], 1)
        if ahead == 0:
            ref, i = near[k // 2], 0
        elif ahead == 2:
            ref, i = (far[0], 0) if k < 2 else (near[1], 1)
        else:
            first, second = (by_x, diagonal) if ahead == 1 else (diagonal, by_x)
            first, second = (ref[i, at, k % 2, :, cols] for ref, i in (first, second))
            return jnp.where(is_even, first, second)
        return ref[i, at, k % 2, :, cols]

    def to_lanes(k, chunk):
        cols = pl.ds(128 * chunk, 128)
        parts = []
        for half in halves:
            tiles = []
            for i in range(per_half):
                first, second = [], []
                for at in entry:
                    here = tile(near, far, k, half * per_half + i, at, cols)
                    there = tile(near_other, far_other, k, half * per_half + i, at, cols)
                    first.append(jnp.where(own_rows, here, there))
                    second.append(pltpu.roll(jnp.where(own_rows, there, here), 4, 0))
                tiles += first + second
            parts.append(jnp.concatenate(tiles, axis=0).T)
        return parts

    def halves_of(parts, chunk):
        return {2 * chunk + i: [part[64 * i : 64 * i + 64] for part in parts] for i in range(2)}

    for k in range(fields):
        for chunks in ((0, 3), (1,), (2,)):
            slabs = {}
            for chunk in chunks:
                slabs.update(halves_of(to_lanes(k, chunk), chunk))
            settle(u.at[k], slabs, lanes, "avg", xs.at[k])

    for chunks in ((0, 3), (1,), (2,)):
        slabs = {}
        for chunk in chunks:
            for a, react in halves_of(to_lanes(fields, chunk), chunk).items():
                mass = cross_ref[pl.ds(0, 64), :] * float(weights[a])
                diag = cross_ref[pl.ds(0, 64), :] * float(stiff_sum[a])
                diag += cross_ref[pl.ds(64, 64), :] * float(weights[a])
                react = [part * mass for part in react]
                for h in halves:
                    rm[h, slab_rows[a], :] = react[h]
                slabs[a] = [part + diag for part in react]
        settle(dinv, slabs, lanes, "sum")

    up, low, _, _ = lanes.factors(2, "avg")
    share_z = jnp.where(sublane == 7, up, jnp.where(sublane == 0, low, 1.0))
    up, low, _, _ = lanes.factors(1, "avg")
    for b in range(8):
        share = share_z * (low if b == 0 else up) if b in (0, 7) else share_z
        for a in range(8):
            for h in halves:
                inverse = 1.0 / dinv[h, columns[b][a], :]
                dinv[h, columns[b][a], :] = inverse
                w[h, columns[b][a], :] = inverse * (share * 0.5 if a in (0, 7) else share)

    def in_halves(g):
        return [g[:, 128 * h : 128 * (h + 1)] for h in halves]

    def product(row, count, k, a):
        high, low = xs[k, 0, slab_rows[a], :], xs[k, 1, slab_rows[a], :]
        parts = jnp.concatenate([high, low, high, low], axis=0)
        return in_halves(
            jnp.dot(matrix_ref[pl.ds(row, count), :], parts, preferred_element_type=F32)
        )

    def product_first(row, k, j):
        high, low = (
            jnp.concatenate([xs[k, i, pair_rows[j][a], :] for a in range(8)], axis=0)
            for i in range(2)
        )
        parts = jnp.concatenate([high, low, high], axis=0)
        g = in_halves(
            jnp.dot(pair_ref[pl.ds(row, 128), :], parts, preferred_element_type=F32)
        )
        return [[part[16 * a : 16 * a + 16] for part in g] for a in range(8)]

    now, after = u, v
    for _ in range(SUBSTEPS):
        for j in range(4):
            for k in range(fields):
                g = product_first(0, k, j)
                for a, rows in enumerate(pair_rows[j]):
                    for h in halves:
                        after[k, h, rows, :] = now[k, h, rows, :] - now[0, h, rows, :] * g[a][h]
        for group in SLAB_ORDER:
            for k in range(fields):
                slabs = {}
                for a in group:
                    g = product(0, 128, k, a)
                    slabs[a] = [
                        after[k, h, slab_rows[a], :]
                        - now[1, h, slab_rows[a], :] * g[h][:64]
                        - now[2, h, slab_rows[a], :] * g[h][64:]
                        for h in halves
                    ]
                settle(after.at[k], slabs, lanes, "wall", xs.at[k])
        now, after = after, now

    def own_block(source, own):
        flip[...] = source.T
        size = own.shape[2]
        for i in range(own.shape[0]):
            start = i * lanes.strides[0] + my_y * lanes.strides[1]
            block = flip[pl.ds(pl.multiple_of(start, 8), 8), :]
            own[i, 0] = jnp.where(is_low, block[:size], block[size:])

    for j in range(4):
        g = product_first(0, 0, j)
        for a, rows in enumerate(pair_rows[j]):
            for h in halves:
                r[h, rows, :] = g[a][h]
    for group in SLAB_ORDER:
        slabs = {}
        for a in group:
            second, third = product(0, 64, 1, a), product(64, 64, 2, a)
            mass = cross_ref[pl.ds(0, 64), :] * float(-weights[a] / step_size)
            slabs[a] = [
                mass * (r[h, slab_rows[a], :] + second[h] + third[h]) for h in halves
            ]
        settle(r, slabs, lanes, "sum")

    for k in range(fields):
        own_block(now[k, 0], vel_own.at[k])
    send_velocity = pltpu.make_async_copy(vel_own, vel_out, sems.at[0])
    send_velocity.start()

    def total(acc):
        return jnp.sum(jnp.sum(acc, axis=0, keepdims=True), axis=1, keepdims=True)

    def begin_sweep(update):
        acc = jnp.zeros((64, 128), F32)
        for a, rows in enumerate(slab_rows):
            for h in halves:
                res = r[h, rows, :]
                if update is not None:
                    alpha, beta = update
                    image = y[h, rows, :]
                    if beta is not None:
                        image = image + beta * s[h, rows, :]
                    s[h, rows, :] = image
                    res = res - alpha * image
                    r[h, rows, :] = res
                acc += res * res * w[h, rows, :]
                z[h, rows, :] = res * dinv[h, rows, :]
            store_split(xs.at[0], z, a)
        for j in range(4):
            g = product_first(128, 0, j)
            cross = cross_ref[pl.ds(16 * j, 16), :]
            for a, rows in enumerate(pair_rows[j]):
                for h in halves:
                    y[h, rows, :] = cross * g[a][h]
        return total(acc)

    gamma = begin_sweep(None)
    alpha = beta = None
    for sweep in range(ITERS):
        acc = jnp.zeros((64, 128), F32)
        for group in SLAB_ORDER:
            slabs = {}
            for a in group:
                g = product(128 + 64 * min(a, 7 - a), 64, 0, a)
                slabs[a] = []
                for h in halves:
                    here = z[h, slab_rows[a], :]
                    image = y[h, slab_rows[a], :] + g[h] + rm[h, slab_rows[a], :] * here
                    acc += image * here
                    slabs[a].append(image)
            settle(y, slabs, lanes, "sum")
        delta = total(acc)
        if sweep:
            beta = gamma / gamma_before
            alpha = gamma / (delta - beta * gamma / alpha)
        else:
            alpha = gamma / delta
        for rows in slab_rows:
            search = z[0, rows, :]
            if sweep:
                search = search + beta * p[rows, :]
            p[rows, :] = search
            x[rows, :] = x[rows, :] + alpha * search if sweep else alpha * search
        if sweep < ITERS - 1:
            gamma_before, gamma = gamma, begin_sweep((alpha, beta))
    for rows in slab_rows:
        r[0, rows, :] -= alpha * (y[0, rows, :] + beta * s[0, rows, :])

    own_block(x[...], pre_own)
    send_pressure = pltpu.make_async_copy(pre_own, pre_out, sems.at[1])
    send_pressure.start()
    own_block(r[0], res_own)
    send_residual = pltpu.make_async_copy(res_own, res_out, sems.at[2])
    send_residual.start()
    send_velocity.wait()
    send_pressure.wait()
    send_residual.wait()


def whole_body(devices, velocity, reaction):
    fields = velocity.shape[0]
    lanes = int(np.prod(devices)) * 8
    weights, derivative = host_tables()
    eye = np.eye(8)
    stiffness = derivative.T @ (weights[:, None] * derivative)
    stiff_sum = np.sum(weights[:, None] * derivative * derivative, axis=0)
    across = np.kron(stiffness, np.diag(weights)) + np.kron(np.diag(weights), stiffness)
    matrices = np.concatenate(
        [
            split_matrix(step_size * np.kron(derivative, eye)),
            split_matrix(step_size * np.kron(eye, derivative)),
        ]
        + [split_matrix(weights[a] * across) for a in range(4)]
    )
    along = [step_size * derivative, stiffness]
    pairs = np.concatenate([split_matrix(np.kron(m, np.eye(16)))[:, :384] for m in along])
    cross = np.outer(weights, weights).reshape(-1)
    sides = np.outer(stiff_sum, weights).reshape(-1) + np.outer(weights, stiff_sum).reshape(-1)
    cross = np.broadcast_to(np.concatenate([cross, sides])[:, None], (128, 128))

    vmem = pl.BlockSpec(memory_space=pltpu.VMEM)
    hbm = pl.BlockSpec(memory_space=pltpu.HBM)
    def swapped(block, axis, mask):
        count = lax.axis_size(axis)
        return lax.ppermute(block, axis, [(i, i ^ mask) for i in range(count)])

    block = jnp.concatenate([velocity, reaction[None]], axis=0)
    column = jax.ShapeDtypeStruct((devices[1], 2, 8, 512), F32)
    first, second = pl.pallas_call(
        column_kernel,
        out_shape=[column, column],
        in_specs=[vmem] * devices[1],
        out_specs=[vmem, vmem],
        compiler_params=SMALL,
    )(block, *(swapped(block, "gy", mask) for mask in range(1, devices[1])))
    near = in_pairs(first, swapped(first, "gx", 1), second, swapped(second, "gx", 2))
    far = [swapped(near[0], "gx", 2), swapped(near[1], "gx", 1)]
    others = [swapped(pair, "gz", 1) for pair in (*near, *far)]

    field = pltpu.VMEM((lanes // 128, 512, 128), F32)
    three = pltpu.VMEM((fields, lanes // 128, 512, 128), F32)
    one_half = pltpu.VMEM((512, 128), F32)
    own = pltpu.VMEM(reaction.shape, F32)
    return pl.pallas_call(
        functools.partial(whole_kernel, devices, weights, derivative),
        out_shape=(
            jax.ShapeDtypeStruct(velocity.shape, F32),
            jax.ShapeDtypeStruct(reaction.shape, F32),
            jax.ShapeDtypeStruct(reaction.shape, F32),
        ),
        in_specs=[vmem] * 11,
        out_specs=(hbm, hbm, hbm),
        scratch_shapes=[three, three, pltpu.VMEM((fields, 2, 512, lanes), BF16)]
        + [field] * 7
        + [one_half] * 2
        + [
            pltpu.VMEM((128, 512), F32),
            pltpu.VMEM(velocity.shape, F32),
            own,
            own,
            pltpu.SemaphoreType.DMA((3,)),
        ],
        compiler_params=pltpu.CompilerParams(vmem_limit_bytes=40 << 20),
    )(
        *near, *far, *others, jnp.asarray(cross, F32), jnp.asarray(matrices), jnp.asarray(pairs),
    )


def extended(block, sides, width, periodic):
    for axis, dim in sides:
        count = lax.axis_size(axis)
        forward = [(i, i + 1) for i in range(count - 1)]
        if periodic:
            forward.append((count - 1, 0))
        backward = [(target, source) for source, target in forward]
        low = lax.ppermute(
            lax.slice_in_dim(block, block.shape[dim] - width, None, axis=dim), axis, forward
        )
        high = lax.ppermute(lax.slice_in_dim(block, 0, width, axis=dim), axis, backward)
        block = jnp.concatenate([low, block, high], axis=dim)
    return block


def derive(values, derivative, along_dim, transposed):
    layout = values.shape
    matrix = derivative.T if transposed else derivative
    blocks = values.reshape(-1, 8, 8, 8)
    patterns = ("aq,nqbc->nabc", "bq,naqc->nabc", "cq,nabq->nabc")
    result = jnp.einsum(patterns[along_dim], matrix, blocks, precision=lax.Precision.HIGHEST)
    return result.reshape(layout)


def place_face(values, target_axis, position, update):
    selector = tuple(
        (position if place == target_axis else slice(None) for place in range(values.ndim))
    )
    return values.at[selector].set(update)


def faces_along_x(sequence):
    return extended(sequence, (("gx", 0),), 1, True)


def faces_along_y(sequence):
    return extended(sequence, (("gy", 0),), 1, False)


def faces_along_z(sequence):
    return extended(sequence, (("gz", 0),), 1, False)


def join_faces(values, along_dim, exchanger):
    lower_face = jnp.moveaxis(jnp.take(values, 0, axis=4 + along_dim), 1 + along_dim, 0)
    upper_face = jnp.moveaxis(jnp.take(values, 7, axis=4 + along_dim), 1 + along_dim, 0)
    elements = lower_face.shape[0]
    face_shape = lower_face.shape
    sequence = jnp.stack([lower_face, upper_face], axis=1).reshape(2 * elements, -1)
    padded = exchanger(sequence)
    paired = padded.reshape(elements + 1, 2, -1)
    totals = paired[:, 0] + paired[:, 1]
    new_lower = jnp.moveaxis(totals[:-1].reshape(face_shape), 0, 1 + along_dim)
    new_upper = jnp.moveaxis(totals[1:].reshape(face_shape), 0, 1 + along_dim)
    values = place_face(values, 4 + along_dim, 0, new_lower)
    return place_face(values, 4 + along_dim, 7, new_upper)


def assemble(values):
    exchangers = (faces_along_x, faces_along_y, faces_along_z)
    dim_order = (0, 1, 2)
    for along_dim in dim_order:
        values = join_faces(values, along_dim, exchangers[along_dim])
    return values


def dim_factors(local_count, offset, total_count, bounded_by_walls):
    element_ids = offset + jnp.arange(local_count)
    node_ids = jnp.arange(8)
    at_end = (node_ids[None, :] == 0) | (node_ids[None, :] == 7)
    low_wall = (element_ids[:, None] == 0) & (node_ids[None, :] == 0)
    high_wall = (element_ids[:, None] == total_count - 1) & (node_ids[None, :] == 7)
    on_wall = (low_wall | high_wall) & bounded_by_walls
    shared = at_end & jnp.logical_not(on_wall)
    return (jnp.where(shared, 2.0, 1.0).astype(jnp.float32), on_wall.astype(jnp.float32))


def spread_body(velocity, reaction):
    weights, derivative = tables()
    count_x, count_y, count_z = (reaction.shape[0], reaction.shape[1], reaction.shape[2])
    speed = velocity.reshape(3, count_x, count_y, count_z, 8, 8, 8)
    react = reaction.reshape(1, count_x, count_y, count_z, 8, 8, 8)
    mass_matrix = weights[:, None, None] * weights[None, :, None] * weights[None, None, :]
    factor_x, wall_x = dim_factors(
        count_x, lax.axis_index("gx") * count_x, lax.axis_size("gx") * count_x, False
    )
    factor_y, wall_y = dim_factors(
        count_y, lax.axis_index("gy") * count_y, lax.axis_size("gy") * count_y, True
    )
    factor_z, wall_z = dim_factors(
        count_z, lax.axis_index("gz") * count_z, lax.axis_size("gz") * count_z, True
    )
    multiplicity = (
        factor_x[None, :, None, None, :, None, None]
        * factor_y[None, None, :, None, None, :, None]
        * factor_z[None, None, None, :, None, None, :]
    )
    interior = (1.0 - wall_y[None, None, :, None, None, :, None]) * (
        1.0 - wall_z[None, None, None, :, None, None, :]
    )
    stiff_sum = jnp.sum(weights[:, None] * derivative * derivative, axis=0)
    diag_local = (
        stiff_sum[:, None, None] * weights[None, :, None] * weights[None, None, :]
        + weights[:, None, None] * stiff_sum[None, :, None] * weights[None, None, :]
        + weights[:, None, None] * weights[None, :, None] * stiff_sum[None, None, :]
    )
    diag_terms = diag_local + react * mass_matrix
    speed = assemble(speed) / multiplicity
    diagonal = None
    for substep in range(SUBSTEPS):
        gradient_fields = [derive(speed, derivative, along_dim, False) for along_dim in range(3)]
        transport = (
            speed[0:1] * gradient_fields[0]
            + speed[1:2] * gradient_fields[1]
            + speed[2:3] * gradient_fields[2]
        )
        tendency = assemble(mass_matrix * transport) / (mass_matrix * multiplicity)
        speed = interior * (speed - step_size * tendency)
    spread = (
        derive(speed[0:1], derivative, 0, False)
        + derive(speed[1:2], derivative, 1, False)
        + derive(speed[2:3], derivative, 2, False)
    )
    source = -assemble(mass_matrix * spread)
    diagonal = assemble(diag_terms)

    def local_inner(first, second):
        return jnp.sum(first * second / multiplicity)

    def norm_weighted_mass(residual_vec, precond_vec):
        return lax.psum(local_inner(residual_vec, precond_vec), ("gx", "gy", "gz"))

    pressure = jnp.zeros_like(source)
    residual = source
    precond = residual / diagonal
    search = precond
    progress = norm_weighted_mass(residual, precond)
    for sweep_index in range(ITERS):
        local_sum = react * mass_matrix * search
        for apply_along_dim in range(3):
            local_sum = local_sum + derive(
                mass_matrix * derive(search, derivative, apply_along_dim, False),
                derivative,
                apply_along_dim,
                True,
            )
        applied = assemble(local_sum)
        step_length = progress / lax.psum(local_inner(search, applied), ("gx", "gy", "gz"))
        pressure = pressure + step_length * search
        residual = residual - step_length * applied
        precond = residual / diagonal
        progress_next = norm_weighted_mass(residual, precond)
        search = precond + progress_next / progress * search
        progress = progress_next
    return (
        speed.reshape(3, count_x, count_y, count_z, 512),
        pressure.reshape(count_x, count_y, count_z, 512),
        residual.reshape(count_x, count_y, count_z, 512),
    )


def solution(mesh):
    in_specs = (P(None, "gx", "gy", "gz", None), P("gx", "gy", "gz", None))
    out_specs = (
        P(None, "gx", "gy", "gz", None),
        P("gx", "gy", "gz", None),
        P("gx", "gy", "gz", None),
    )
    devices = tuple(mesh.shape[axis] for axis in ("gx", "gy", "gz"))

    def body(velocity, reaction):
        if devices == (4, 4, 2) and reaction.shape[:3] == (2, 1, 4):
            return whole_body(devices, velocity, reaction)
        return spread_body(velocity, reaction)

    return jax.shard_map(body, mesh=mesh, in_specs=in_specs, out_specs=out_specs, check_vma=False)
```

```python
import functools

import jax
import jax.numpy as jnp
import numpy as np
from jax import lax
from jax.experimental import pallas as pl
from jax.experimental.pallas import tpu as pltpu
from jax.sharding import PartitionSpec as P

SUBSTEPS = 2
ITERS = 4
step_size = 0.02

F32 = jnp.float32
BF16 = jnp.bfloat16


def legendre_seven(points):
    earlier = points * 0.0 + 1.0
    current = points
    for degree in range(1, 7):
        earlier, current = (
            current,
            ((2 * degree + 1) * points * current - degree * earlier) / (degree + 1),
        )
    return current


def host_tables():
    half = np.array([0.20929921790247888, 0.5917001814331423, 0.8717401485096066, 1.0])
    points = np.concatenate([-half[::-1], half])
    legendre = legendre_seven(points)
    weights = 2.0 / (56.0 * legendre**2)
    spacing = points[:, None] - points[None, :] + np.eye(8)
    derivative = legendre[:, None] / legendre[None, :] / spacing * (1.0 - np.eye(8))
    derivative[0, 0] = -14.0
    derivative[7, 7] = 14.0
    return weights, derivative


def tables():
    weights, derivative = host_tables()
    return (jnp.asarray(weights, F32), jnp.asarray(derivative, F32))


def split_matrix(matrix):
    matrix = matrix.astype(np.float32)
    high = matrix.astype(jnp.bfloat16)
    low = (matrix - high.astype(np.float32)).astype(jnp.bfloat16)
    return np.concatenate([high, high, low, low], axis=1)


def split_parts(values):
    high = values.astype(BF16)
    return high, (values - high.astype(F32)).astype(BF16)


def roll_lanes(parts, shift):
    turned = [pltpu.roll(part, shift, 1) for part in parts]
    lane = lax.broadcasted_iota(jnp.int32, parts[0].shape, 1)
    return [jnp.where(lane < shift, turned[i - 1], turned[i]) for i in range(len(parts))]


def roll_lanes_back(parts, shift):
    turned = [pltpu.roll(part, 128 - shift, 1) for part in parts]
    lane = lax.broadcasted_iota(jnp.int32, parts[0].shape, 1)
    count = len(parts)
    return [
        jnp.where(lane < 128 - shift, turned[i], turned[(i + 1) % count]) for i in range(count)
    ]


class Lanes:
    def __init__(self, counts):
        self.strides = (counts[1] * counts[2], counts[2], 1)
        lane = lax.broadcasted_iota(jnp.int32, (1, 128), 1)
        place = {1: (lane // counts[2]) % counts[1], 2: lane % counts[2]}
        self.has_next = {d: place[d] < counts[d] - 1 for d in (1, 2)}
        self.has_prev = {d: place[d] > 0 for d in (1, 2)}

    def factors(self, direction, mode):
        n, p = self.has_next[direction], self.has_prev[direction]
        if mode == "sum":
            return None, None, jnp.where(n, 1.0, 0.0), jnp.where(p, 1.0, 0.0)
        alone = 1.0 if mode == "avg" else 0.0
        return (
            jnp.where(n, 0.5, alone),
            jnp.where(p, 0.5, alone),
            jnp.where(n, 0.5, 0.0),
            jnp.where(p, 0.5, 0.0),
        )


def settle(ref, slabs, lanes, mode, split=None):
    if 0 in slabs:
        lower, upper = slabs[0], slabs[7]
        stride = lanes.strides[0]
        new_upper = [a + b for a, b in zip(upper, roll_lanes_back(lower, stride))]
        new_lower = [a + b for a, b in zip(lower, roll_lanes(upper, stride))]
        if mode != "sum":
            new_upper = [0.5 * a for a in new_upper]
            new_lower = [0.5 * a for a in new_lower]
        slabs = {**slabs, 0: new_lower, 7: new_upper}

    def joined(lower, upper, direction):
        stride = lanes.strides[direction]
        own_up, own_low, from_next, from_prev = lanes.factors(direction, mode)
        following, previous = pltpu.roll(lower, 128 - stride, 1), pltpu.roll(upper, stride, 1)
        if mode == "sum":
            return lower + previous * from_prev, upper + following * from_next
        if mode == "wall":
            return (lower + previous) * from_prev, (upper + following) * from_next
        return lower * own_low + previous * from_prev, upper * own_up + following * from_next

    for a, parts in slabs.items():
        for h, part in enumerate(parts):
            lower, upper = joined(part[:8], part[56:], 1)
            ref[h, pl.ds(64 * a, 8), :] = lower
            ref[h, pl.ds(64 * a + 8, 48), :] = part[8:56]
            ref[h, pl.ds(64 * a + 56, 8), :] = upper
            first, last = pl.ds(64 * a, 8, stride=8), pl.ds(64 * a + 7, 8, stride=8)
            lower, upper = joined(ref[h, first, :], ref[h, last, :], 2)
            ref[h, first, :] = lower
            ref[h, last, :] = upper
        if split is not None:
            store_split(split, ref, a)


def store_split(split, ref, a):
    rows = pl.ds(64 * a, 64)
    values = jnp.concatenate([ref[h, rows, :] for h in range(ref.shape[0])], axis=1)
    split[0, rows, :], split[1, rows, :] = split_parts(values)


SLAB_ORDER = ((0, 7), (1,), (2,), (3,), (4,), (5,), (6,))


def column_kernel(*refs):
    blocks, outs = refs[:-2], refs[-2:]
    is_low = lax.axis_index("gz") == 0
    for j, block in enumerate(blocks):
        for k in range(block.shape[0]):
            low, high = block[k, 0, 0], block[k, 1, 0]
            straight = jnp.concatenate([low, high], axis=0)
            turned = jnp.concatenate([high, low], axis=0)
            outs[k // 2][j, k % 2] = jnp.where(is_low, straight, turned)


def pair_kernel(first, second, out):
    out[0] = first[...]
    out[1] = second[...]


SMALL = pltpu.CompilerParams(vmem_limit_bytes=1 << 20)


def paired(first, second):
    vmem = pl.BlockSpec(memory_space=pltpu.VMEM)
    return pl.pallas_call(
        pair_kernel,
        out_shape=jax.ShapeDtypeStruct((2,) + first.shape, F32),
        in_specs=[vmem] * 2,
        out_specs=vmem,
        compiler_params=SMALL,
    )(first, second)


def whole_kernel(devices, weights, derivative, *refs):
    (
        near, far, near_other, far_other, cross_ref, matrix_ref, pair_ref,
        vel_out, pre_out, res_out,
        u, v, xs, rm, w, dinv, z, r, y, s, p, x, flip, vel_own, pre_own, res_own, sems,
    ) = [refs[0:2], refs[2:4], refs[4:6], refs[6:8], *refs[8:]]
    my_y, my_z = lax.axis_index("gy"), lax.axis_index("gz")
    fields = u.shape[0]
    halves = range(u.shape[1])
    per_half = devices[0] // len(halves)
    lanes = Lanes((2 * devices[0], devices[1], 8))
    stiff_sum = np.sum(weights[:, None] * derivative * derivative, axis=0)
    slab_rows = [pl.ds(64 * a, 64) for a in range(8)]
    pair_rows = [[pl.ds(64 * a + 16 * j, 16) for a in range(8)] for j in range(4)]

    is_low = my_z == 0
    is_even = lax.axis_index("gx") % 2 == 0
    sublane = lax.broadcasted_iota(jnp.int32, (8, 128), 0)
    own_rows = (sublane < 4) == is_low
    entry = [my_y ^ j for j in range(devices[1])]

    def tile(near, far, k, ahead, at, cols):
        by_x = (near[0], 1) if k < 2 else (far[1], 0)
        diagonal = (far[k // 2], 1)
        if ahead == 0:
            ref, i = near[k // 2], 0
        elif ahead == 2:
            ref, i = (far[0], 0) if k < 2 else (near[1], 1)
        else:
            first, second = (by_x, diagonal) if ahead == 1 else (diagonal, by_x)
            first, second = (ref[i, at, k % 2, :, cols] for ref, i in (first, second))
            return jnp.where(is_even, first, second)
        return ref[i, at, k % 2, :, cols]

    def to_lanes(k, chunk):
        cols = pl.ds(128 * chunk, 128)
        parts = []
        for half in halves:
            tiles = []
            for i in range(per_half):
                first, second = [], []
                for at in entry:
                    here = tile(near, far, k, half * per_half + i, at, cols)
                    there = tile(near_other, far_other, k, half * per_half + i, at, cols)
                    first.append(jnp.where(own_rows, here, there))
                    second.append(pltpu.roll(jnp.where(own_rows, there, here), 4, 0))
                tiles += first + second
            parts.append(jnp.concatenate(tiles, axis=0).T)
        return parts

    def halves_of(parts, chunk):
        return {2 * chunk + i: [part[64 * i : 64 * i + 64] for part in parts] for i in range(2)}

    for k in range(fields):
        for chunks in ((0, 3), (1,), (2,)):
            slabs = {}
            for chunk in chunks:
                slabs.update(halves_of(to_lanes(k, chunk), chunk))
            settle(u.at[k], slabs, lanes, "avg", xs.at[k])

    for chunks in ((0, 3), (1,), (2,)):
        slabs = {}
        for chunk in chunks:
            for a, react in halves_of(to_lanes(fields, chunk), chunk).items():
                mass = cross_ref[pl.ds(0, 64), :] * float(weights[a])
                diag = cross_ref[pl.ds(0, 64), :] * float(stiff_sum[a])
                diag += cross_ref[pl.ds(64, 64), :] * float(weights[a])
                react = [part * mass for part in react]
                for h in halves:
                    rm[h, slab_rows[a], :] = react[h]
                slabs[a] = [part + diag for part in react]
        settle(dinv, slabs, lanes, "sum")

    up, low, _, _ = lanes.factors(2, "avg")
    share_z = jnp.where(sublane == 7, up, jnp.where(sublane == 0, low, 1.0))
    up, low, _, _ = lanes.factors(1, "avg")
    for b in range(8):
        share = share_z * (low if b == 0 else up) if b in (0, 7) else share_z
        for a in range(8):
            for h in halves:
                rows = pl.ds(64 * a + 8 * b, 8)
                inverse = 1.0 / dinv[h, rows, :]
                dinv[h, rows, :] = inverse
                w[h, rows, :] = inverse * (share * 0.5 if a in (0, 7) else share)

    def in_halves(g):
        return [g[:, 128 * h : 128 * (h + 1)] for h in halves]

    def product(row, count, k, a):
        high, low = xs[k, 0, slab_rows[a], :], xs[k, 1, slab_rows[a], :]
        parts = jnp.concatenate([high, low, high, low], axis=0)
        return in_halves(
            jnp.dot(matrix_ref[pl.ds(row, count), :], parts, preferred_element_type=F32)
        )

    def product_first(row, k, j):
        high, low = (
            jnp.concatenate([xs[k, i, pair_rows[j][a], :] for a in range(8)], axis=0)
            for i in range(2)
        )
        parts = jnp.concatenate([high, low, high], axis=0)
        g = in_halves(
            jnp.dot(pair_ref[pl.ds(row, 128), :], parts, preferred_element_type=F32)
        )
        return [[part[16 * a : 16 * a + 16] for part in g] for a in range(8)]

    now, after = u, v
    for _ in range(SUBSTEPS):
        for j in range(4):
            for k in range(fields):
                g = product_first(0, k, j)
                for a, rows in enumerate(pair_rows[j]):
                    for h in halves:
                        after[k, h, rows, :] = now[k, h, rows, :] - now[0, h, rows, :] * g[a][h]
        for group in SLAB_ORDER:
            for k in range(fields):
                slabs = {}
                for a in group:
                    g = product(0, 128, k, a)
                    slabs[a] = [
                        after[k, h, slab_rows[a], :]
                        - now[1, h, slab_rows[a], :] * g[h][:64]
                        - now[2, h, slab_rows[a], :] * g[h][64:]
                        for h in halves
                    ]
                settle(after.at[k], slabs, lanes, "wall", xs.at[k])
        now, after = after, now

    def own_block(source, own):
        flip[...] = source.T
        size = own.shape[2]
        for i in range(own.shape[0]):
            start = i * lanes.strides[0] + my_y * lanes.strides[1]
            block = flip[pl.ds(pl.multiple_of(start, 8), 8), :]
            own[i, 0] = jnp.where(is_low, block[:size], block[size:])

    for j in range(4):
        g = product_first(0, 0, j)
        for a, rows in enumerate(pair_rows[j]):
            for h in halves:
                r[h, rows, :] = g[a][h]
    for group in SLAB_ORDER:
        slabs = {}
        for a in group:
            second, third = product(0, 64, 1, a), product(64, 64, 2, a)
            mass = cross_ref[pl.ds(0, 64), :] * float(-weights[a] / step_size)
            slabs[a] = [
                mass * (r[h, slab_rows[a], :] + second[h] + third[h]) for h in halves
            ]
        settle(r, slabs, lanes, "sum")

    for k in range(fields):
        own_block(now[k, 0], vel_own.at[k])
    send_velocity = pltpu.make_async_copy(vel_own, vel_out, sems.at[0])
    send_velocity.start()

    def total(acc):
        return jnp.sum(jnp.sum(acc, axis=0, keepdims=True), axis=1, keepdims=True)

    def begin_sweep(update):
        acc = jnp.zeros((64, 128), F32)
        for a, rows in enumerate(slab_rows):
            for h in halves:
                res = r[h, rows, :]
                if update is not None:
                    alpha, beta = update
                    image = y[h, rows, :]
                    if beta is not None:
                        image = image + beta * s[h, rows, :]
                    s[h, rows, :] = image
                    res = res - alpha * image
                    r[h, rows, :] = res
                acc += res * res * w[h, rows, :]
                z[h, rows, :] = res * dinv[h, rows, :]
            store_split(xs.at[0], z, a)
        for j in range(4):
            g = product_first(128, 0, j)
            cross = cross_ref[pl.ds(16 * j, 16), :]
            for a, rows in enumerate(pair_rows[j]):
                for h in halves:
                    y[h, rows, :] = cross * g[a][h]
        return total(acc)

    gamma = begin_sweep(None)
    alpha = beta = None
    for sweep in range(ITERS):
        acc = jnp.zeros((64, 128), F32)
        for group in SLAB_ORDER:
            slabs = {}
            for a in group:
                g = product(128 + 64 * min(a, 7 - a), 64, 0, a)
                slabs[a] = []
                for h in halves:
                    here = z[h, slab_rows[a], :]
                    image = y[h, slab_rows[a], :] + g[h] + rm[h, slab_rows[a], :] * here
                    acc += image * here
                    slabs[a].append(image)
            settle(y, slabs, lanes, "sum")
        delta = total(acc)
        if sweep:
            beta = gamma / gamma_before
            alpha = gamma / (delta - beta * gamma / alpha)
        else:
            alpha = gamma / delta
        for rows in slab_rows:
            search = z[0, rows, :]
            if sweep:
                search = search + beta * p[rows, :]
            p[rows, :] = search
            x[rows, :] = x[rows, :] + alpha * search if sweep else alpha * search
        if sweep < ITERS - 1:
            gamma_before, gamma = gamma, begin_sweep((alpha, beta))
    for rows in slab_rows:
        r[0, rows, :] -= alpha * (y[0, rows, :] + beta * s[0, rows, :])

    own_block(x[...], pre_own)
    send_pressure = pltpu.make_async_copy(pre_own, pre_out, sems.at[1])
    send_pressure.start()
    own_block(r[0], res_own)
    send_residual = pltpu.make_async_copy(res_own, res_out, sems.at[2])
    send_residual.start()
    send_velocity.wait()
    send_pressure.wait()
    send_residual.wait()


def whole_body(devices, velocity, reaction):
    fields = velocity.shape[0]
    lanes = int(np.prod(devices)) * 8
    weights, derivative = host_tables()
    eye = np.eye(8)
    stiffness = derivative.T @ (weights[:, None] * derivative)
    stiff_sum = np.sum(weights[:, None] * derivative * derivative, axis=0)
    across = np.kron(stiffness, np.diag(weights)) + np.kron(np.diag(weights), stiffness)
    matrices = np.concatenate(
        [
            split_matrix(step_size * np.kron(derivative, eye)),
            split_matrix(step_size * np.kron(eye, derivative)),
        ]
        + [split_matrix(weights[a] * across) for a in range(4)]
    )
    along = [step_size * derivative, stiffness]
    pairs = np.concatenate([split_matrix(np.kron(m, np.eye(16)))[:, :384] for m in along])
    cross = np.outer(weights, weights).reshape(-1)
    sides = np.outer(stiff_sum, weights).reshape(-1) + np.outer(weights, stiff_sum).reshape(-1)
    cross = np.broadcast_to(np.concatenate([cross, sides])[:, None], (128, 128))

    vmem = pl.BlockSpec(memory_space=pltpu.VMEM)
    hbm = pl.BlockSpec(memory_space=pltpu.HBM)
    def swapped(block, axis, mask):
        count = lax.axis_size(axis)
        return lax.ppermute(block, axis, [(i, i ^ mask) for i in range(count)])

    block = jnp.concatenate([velocity, reaction[None]], axis=0)
    column = jax.ShapeDtypeStruct((devices[1], 2, 8, 512), F32)
    first, second = pl.pallas_call(
        column_kernel,
        out_shape=[column, column],
        in_specs=[vmem] * devices[1],
        out_specs=[vmem, vmem],
        compiler_params=SMALL,
    )(block, *(swapped(block, "gy", mask) for mask in range(1, devices[1])))
    near = [paired(first, swapped(first, "gx", 1)), paired(second, swapped(second, "gx", 2))]
    far = [swapped(near[0], "gx", 2), swapped(near[1], "gx", 1)]
    others = [swapped(pair, "gz", 1) for pair in (*near, *far)]

    field = pltpu.VMEM((lanes // 128, 512, 128), F32)
    three = pltpu.VMEM((fields, lanes // 128, 512, 128), F32)
    one_half = pltpu.VMEM((512, 128), F32)
    own = pltpu.VMEM(reaction.shape, F32)
    return pl.pallas_call(
        functools.partial(whole_kernel, devices, weights, derivative),
        out_shape=(
            jax.ShapeDtypeStruct(velocity.shape, F32),
            jax.ShapeDtypeStruct(reaction.shape, F32),
            jax.ShapeDtypeStruct(reaction.shape, F32),
        ),
        in_specs=[vmem] * 11,
        out_specs=(hbm, hbm, hbm),
        scratch_shapes=[three, three, pltpu.VMEM((fields, 2, 512, lanes), BF16)]
        + [field] * 7
        + [one_half] * 2
        + [
            pltpu.VMEM((128, 512), F32),
            pltpu.VMEM(velocity.shape, F32),
            own,
            own,
            pltpu.SemaphoreType.DMA((3,)),
        ],
        compiler_params=pltpu.CompilerParams(vmem_limit_bytes=40 << 20),
    )(
        *near, *far, *others, jnp.asarray(cross, F32), jnp.asarray(matrices), jnp.asarray(pairs),
    )


def extended(block, sides, width, periodic):
    for axis, dim in sides:
        count = lax.axis_size(axis)
        forward = [(i, i + 1) for i in range(count - 1)]
        if periodic:
            forward.append((count - 1, 0))
        backward = [(target, source) for source, target in forward]
        low = lax.ppermute(
            lax.slice_in_dim(block, block.shape[dim] - width, None, axis=dim), axis, forward
        )
        high = lax.ppermute(lax.slice_in_dim(block, 0, width, axis=dim), axis, backward)
        block = jnp.concatenate([low, block, high], axis=dim)
    return block


def derive(values, derivative, along_dim, transposed):
    layout = values.shape
    matrix = derivative.T if transposed else derivative
    blocks = values.reshape(-1, 8, 8, 8)
    patterns = ("aq,nqbc->nabc", "bq,naqc->nabc", "cq,nabq->nabc")
    result = jnp.einsum(patterns[along_dim], matrix, blocks, precision=lax.Precision.HIGHEST)
    return result.reshape(layout)


def place_face(values, target_axis, position, update):
    selector = tuple(
        (position if place == target_axis else slice(None) for place in range(values.ndim))
    )
    return values.at[selector].set(update)


def faces_along_x(sequence):
    return extended(sequence, (("gx", 0),), 1, True)


def faces_along_y(sequence):
    return extended(sequence, (("gy", 0),), 1, False)


def faces_along_z(sequence):
    return extended(sequence, (("gz", 0),), 1, False)


def join_faces(values, along_dim, exchanger):
    lower_face = jnp.moveaxis(jnp.take(values, 0, axis=4 + along_dim), 1 + along_dim, 0)
    upper_face = jnp.moveaxis(jnp.take(values, 7, axis=4 + along_dim), 1 + along_dim, 0)
    elements = lower_face.shape[0]
    face_shape = lower_face.shape
    sequence = jnp.stack([lower_face, upper_face], axis=1).reshape(2 * elements, -1)
    padded = exchanger(sequence)
    paired = padded.reshape(elements + 1, 2, -1)
    totals = paired[:, 0] + paired[:, 1]
    new_lower = jnp.moveaxis(totals[:-1].reshape(face_shape), 0, 1 + along_dim)
    new_upper = jnp.moveaxis(totals[1:].reshape(face_shape), 0, 1 + along_dim)
    values = place_face(values, 4 + along_dim, 0, new_lower)
    return place_face(values, 4 + along_dim, 7, new_upper)


def assemble(values):
    exchangers = (faces_along_x, faces_along_y, faces_along_z)
    dim_order = (0, 1, 2)
    for along_dim in dim_order:
        values = join_faces(values, along_dim, exchangers[along_dim])
    return values


def dim_factors(local_count, offset, total_count, bounded_by_walls):
    element_ids = offset + jnp.arange(local_count)
    node_ids = jnp.arange(8)
    at_end = (node_ids[None, :] == 0) | (node_ids[None, :] == 7)
    low_wall = (element_ids[:, None] == 0) & (node_ids[None, :] == 0)
    high_wall = (element_ids[:, None] == total_count - 1) & (node_ids[None, :] == 7)
    on_wall = (low_wall | high_wall) & bounded_by_walls
    shared = at_end & jnp.logical_not(on_wall)
    return (jnp.where(shared, 2.0, 1.0).astype(jnp.float32), on_wall.astype(jnp.float32))


def spread_body(velocity, reaction):
    weights, derivative = tables()
    count_x, count_y, count_z = (reaction.shape[0], reaction.shape[1], reaction.shape[2])
    speed = velocity.reshape(3, count_x, count_y, count_z, 8, 8, 8)
    react = reaction.reshape(1, count_x, count_y, count_z, 8, 8, 8)
    mass_matrix = weights[:, None, None] * weights[None, :, None] * weights[None, None, :]
    factor_x, wall_x = dim_factors(
        count_x, lax.axis_index("gx") * count_x, lax.axis_size("gx") * count_x, False
    )
    factor_y, wall_y = dim_factors(
        count_y, lax.axis_index("gy") * count_y, lax.axis_size("gy") * count_y, True
    )
    factor_z, wall_z = dim_factors(
        count_z, lax.axis_index("gz") * count_z, lax.axis_size("gz") * count_z, True
    )
    multiplicity = (
        factor_x[None, :, None, None, :, None, None]
        * factor_y[None, None, :, None, None, :, None]
        * factor_z[None, None, None, :, None, None, :]
    )
    interior = (1.0 - wall_y[None, None, :, None, None, :, None]) * (
        1.0 - wall_z[None, None, None, :, None, None, :]
    )
    stiff_sum = jnp.sum(weights[:, None] * derivative * derivative, axis=0)
    diag_local = (
        stiff_sum[:, None, None] * weights[None, :, None] * weights[None, None, :]
        + weights[:, None, None] * stiff_sum[None, :, None] * weights[None, None, :]
        + weights[:, None, None] * weights[None, :, None] * stiff_sum[None, None, :]
    )
    diag_terms = diag_local + react * mass_matrix
    speed = assemble(speed) / multiplicity
    diagonal = None
    for substep in range(SUBSTEPS):
        gradient_fields = [derive(speed, derivative, along_dim, False) for along_dim in range(3)]
        transport = (
            speed[0:1] * gradient_fields[0]
            + speed[1:2] * gradient_fields[1]
            + speed[2:3] * gradient_fields[2]
        )
        tendency = assemble(mass_matrix * transport) / (mass_matrix * multiplicity)
        speed = interior * (speed - step_size * tendency)
    spread = (
        derive(speed[0:1], derivative, 0, False)
        + derive(speed[1:2], derivative, 1, False)
        + derive(speed[2:3], derivative, 2, False)
    )
    source = -assemble(mass_matrix * spread)
    diagonal = assemble(diag_terms)

    def local_inner(first, second):
        return jnp.sum(first * second / multiplicity)

    def norm_weighted_mass(residual_vec, precond_vec):
        return lax.psum(local_inner(residual_vec, precond_vec), ("gx", "gy", "gz"))

    pressure = jnp.zeros_like(source)
    residual = source
    precond = residual / diagonal
    search = precond
    progress = norm_weighted_mass(residual, precond)
    for sweep_index in range(ITERS):
        local_sum = react * mass_matrix * search
        for apply_along_dim in range(3):
            local_sum = local_sum + derive(
                mass_matrix * derive(search, derivative, apply_along_dim, False),
                derivative,
                apply_along_dim,
                True,
            )
        applied = assemble(local_sum)
        step_length = progress / lax.psum(local_inner(search, applied), ("gx", "gy", "gz"))
        pressure = pressure + step_length * search
        residual = residual - step_length * applied
        precond = residual / diagonal
        progress_next = norm_weighted_mass(residual, precond)
        search = precond + progress_next / progress * search
        progress = progress_next
    return (
        speed.reshape(3, count_x, count_y, count_z, 512),
        pressure.reshape(count_x, count_y, count_z, 512),
        residual.reshape(count_x, count_y, count_z, 512),
    )


def solution(mesh):
    in_specs = (P(None, "gx", "gy", "gz", None), P("gx", "gy", "gz", None))
    out_specs = (
        P(None, "gx", "gy", "gz", None),
        P("gx", "gy", "gz", None),
        P("gx", "gy", "gz", None),
    )
    devices = tuple(mesh.shape[axis] for axis in ("gx", "gy", "gz"))

    def body(velocity, reaction):
        if devices == (4, 4, 2) and reaction.shape[:3] == (2, 1, 4):
            return whole_body(devices, velocity, reaction)
        return spread_body(velocity, reaction)

    return jax.shard_map(body, mesh=mesh, in_specs=in_specs, out_specs=out_specs, check_vma=False)
```

```python
import functools

import jax
import jax.numpy as jnp
import numpy as np
from jax import lax
from jax.experimental import pallas as pl
from jax.experimental.pallas import tpu as pltpu
from jax.sharding import PartitionSpec as P

SUBSTEPS = 2
ITERS = 4
step_size = 0.02

F32 = jnp.float32
BF16 = jnp.bfloat16


def legendre_seven(points):
    earlier = points * 0.0 + 1.0
    current = points
    for degree in range(1, 7):
        earlier, current = (
            current,
            ((2 * degree + 1) * points * current - degree * earlier) / (degree + 1),
        )
    return current


def host_tables():
    half = np.array([0.20929921790247888, 0.5917001814331423, 0.8717401485096066, 1.0])
    points = np.concatenate([-half[::-1], half])
    legendre = legendre_seven(points)
    weights = 2.0 / (56.0 * legendre**2)
    spacing = points[:, None] - points[None, :] + np.eye(8)
    derivative = legendre[:, None] / legendre[None, :] / spacing * (1.0 - np.eye(8))
    derivative[0, 0] = -14.0
    derivative[7, 7] = 14.0
    return weights, derivative


def tables():
    weights, derivative = host_tables()
    return (jnp.asarray(weights, F32), jnp.asarray(derivative, F32))


def split_matrix(matrix):
    matrix = matrix.astype(np.float32)
    high = matrix.astype(jnp.bfloat16)
    low = (matrix - high.astype(np.float32)).astype(jnp.bfloat16)
    return np.concatenate([high, high, low, low], axis=1)


def split_parts(values):
    high = values.astype(BF16)
    return high, (values - high.astype(F32)).astype(BF16)


def roll_lanes(parts, shift):
    turned = [pltpu.roll(part, shift, 1) for part in parts]
    lane = lax.broadcasted_iota(jnp.int32, parts[0].shape, 1)
    return [jnp.where(lane < shift, turned[i - 1], turned[i]) for i in range(len(parts))]


def roll_lanes_back(parts, shift):
    turned = [pltpu.roll(part, 128 - shift, 1) for part in parts]
    lane = lax.broadcasted_iota(jnp.int32, parts[0].shape, 1)
    count = len(parts)
    return [
        jnp.where(lane < 128 - shift, turned[i], turned[(i + 1) % count]) for i in range(count)
    ]


class Lanes:
    def __init__(self, counts):
        self.strides = (counts[1] * counts[2], counts[2], 1)
        lane = lax.broadcasted_iota(jnp.int32, (1, 128), 1)
        place = {1: (lane // counts[2]) % counts[1], 2: lane % counts[2]}
        self.has_next = {d: place[d] < counts[d] - 1 for d in (1, 2)}
        self.has_prev = {d: place[d] > 0 for d in (1, 2)}

    def factors(self, direction, mode):
        n, p = self.has_next[direction], self.has_prev[direction]
        if mode == "sum":
            return None, None, jnp.where(n, 1.0, 0.0), jnp.where(p, 1.0, 0.0)
        alone = 1.0 if mode == "avg" else 0.0
        return (
            jnp.where(n, 0.5, alone),
            jnp.where(p, 0.5, alone),
            jnp.where(n, 0.5, 0.0),
            jnp.where(p, 0.5, 0.0),
        )


def settle(ref, slabs, lanes, mode, split=None):
    if 0 in slabs:
        lower, upper = slabs[0], slabs[7]
        stride = lanes.strides[0]
        new_upper = [a + b for a, b in zip(upper, roll_lanes_back(lower, stride))]
        new_lower = [a + b for a, b in zip(lower, roll_lanes(upper, stride))]
        if mode != "sum":
            new_upper = [0.5 * a for a in new_upper]
            new_lower = [0.5 * a for a in new_lower]
        slabs = {**slabs, 0: new_lower, 7: new_upper}

    def joined(lower, upper, direction):
        stride = lanes.strides[direction]
        own_up, own_low, from_next, from_prev = lanes.factors(direction, mode)
        following, previous = pltpu.roll(lower, 128 - stride, 1), pltpu.roll(upper, stride, 1)
        if mode == "sum":
            return lower + previous * from_prev, upper + following * from_next
        if mode == "wall":
            return (lower + previous) * from_prev, (upper + following) * from_next
        return lower * own_low + previous * from_prev, upper * own_up + following * from_next

    for a, parts in slabs.items():
        for h, part in enumerate(parts):
            lower, upper = joined(part[:8], part[56:], 1)
            ref[h, pl.ds(64 * a, 8), :] = lower
            ref[h, pl.ds(64 * a + 8, 48), :] = part[8:56]
            ref[h, pl.ds(64 * a + 56, 8), :] = upper
            first, last = pl.ds(64 * a, 8, stride=8), pl.ds(64 * a + 7, 8, stride=8)
            lower, upper = joined(ref[h, first, :], ref[h, last, :], 2)
            ref[h, first, :] = lower
            ref[h, last, :] = upper
        if split is not None:
            store_split(split, ref, a)


def store_split(split, ref, a):
    rows = pl.ds(64 * a, 64)
    values = jnp.concatenate([ref[h, rows, :] for h in range(ref.shape[0])], axis=1)
    split[0, rows, :], split[1, rows, :] = split_parts(values)


SLAB_ORDER = ((0, 7), (1,), (2,), (3,), (4,), (5,), (6,))


def column_kernel(count, picks, own, *refs):
    out = refs[-1]
    is_low = lax.axis_index("gz") == 0
    for i, (place, array, other_place) in enumerate(picks):
        for j in range(count + 1):
            ref, k = (refs[array * count + j - 1], other_place) if j else (own, place)
            ref = ref if k is None else ref.at[k]
            low, high = ref[0, 0], ref[1, 0]
            straight = jnp.concatenate([low, high], axis=0)
            turned = jnp.concatenate([high, low], axis=0)
            out[j, i] = jnp.where(is_low, straight, turned)


def pair_kernel(first, second, out):
    out[0] = first[...]
    out[1] = second[...]


SMALL = pltpu.CompilerParams(vmem_limit_bytes=1 << 20)


def paired(first, second):
    vmem = pl.BlockSpec(memory_space=pltpu.VMEM)
    return pl.pallas_call(
        pair_kernel,
        out_shape=jax.ShapeDtypeStruct((2,) + first.shape, F32),
        in_specs=[vmem] * 2,
        out_specs=vmem,
        compiler_params=SMALL,
    )(first, second)


class Blocks:
    def __init__(self, devices, x_first, near, far, near_other, far_other):
        self.devices = devices
        self.x_first = x_first
        self.cores = ((near, far), (near_other, far_other))
        is_low = lax.axis_index("gz") == 0
        sublane = lax.broadcasted_iota(jnp.int32, (8, 128), 0)
        self.own_rows = (sublane < 4) == is_low
        self.is_even = lax.axis_index("gx") % 2 == 0
        self.entry = [lax.axis_index("gy") ^ j for j in range(devices[1])]

    def tile(self, core, k, ahead, at, cols):
        near, far = self.cores[core]
        if ahead == 0:
            return near[0, at, k, :, cols]
        by_x, by_y = ((near, 1), (far, 0)) if self.x_first else ((far, 0), (near, 1))
        if ahead == 2:
            ref, i = by_y
            return ref[i, at, k, :, cols]
        ref, i = by_x
        by_x, diagonal = ref[i, at, k, :, cols], far[1, at, k, :, cols]
        if ahead == 1:
            return jnp.where(self.is_even, by_x, diagonal)
        return jnp.where(self.is_even, diagonal, by_x)

    def slabs(self, k, chunk):
        cols = pl.ds(128 * chunk, 128)
        per_half = self.devices[0] // 2
        parts = []
        for half in range(2):
            tiles = []
            for i in range(per_half):
                first, second = [], []
                for at in self.entry:
                    here = self.tile(0, k, half * per_half + i, at, cols)
                    there = self.tile(1, k, half * per_half + i, at, cols)
                    first.append(jnp.where(self.own_rows, here, there))
                    second.append(pltpu.roll(jnp.where(self.own_rows, there, here), 4, 0))
                tiles += first + second
            parts.append(jnp.concatenate(tiles, axis=0).T)
        return {2 * chunk + i: [part[64 * i : 64 * i + 64] for part in parts] for i in range(2)}


CHUNK_ORDER = ((0, 3), (1,), (2,))


def load_field(blocks, k, ref, split, lanes):
    for chunks in CHUNK_ORDER:
        slabs = {}
        for chunk in chunks:
            slabs.update(blocks.slabs(k, chunk))
        settle(ref, slabs, lanes, "avg", split)


def diagonal_kernel(devices, weights, derivative, *refs):
    near, far, near_other, far_other, cross_ref, u, xs, rm, dinv, w = refs
    halves = range(u.shape[0])
    lanes = Lanes((2 * devices[0], devices[1], 8))
    stiff_sum = np.sum(weights[:, None] * derivative * derivative, axis=0)
    slab_rows = [pl.ds(64 * a, 64) for a in range(8)]
    blocks = Blocks(devices, False, near, far, near_other, far_other)
    load_field(blocks, 0, u, xs, lanes)

    for chunks in CHUNK_ORDER:
        slabs = {}
        for chunk in chunks:
            for a, react in blocks.slabs(1, chunk).items():
                mass = cross_ref[pl.ds(0, 64), :] * float(weights[a])
                diag = cross_ref[pl.ds(0, 64), :] * float(stiff_sum[a])
                diag += cross_ref[pl.ds(64, 64), :] * float(weights[a])
                react = [part * mass for part in react]
                for h in halves:
                    rm[h, slab_rows[a], :] = react[h]
                slabs[a] = [part + diag for part in react]
        settle(dinv, slabs, lanes, "sum")

    sublane = lax.broadcasted_iota(jnp.int32, (8, 128), 0)
    up, low, _, _ = lanes.factors(2, "avg")
    share_z = jnp.where(sublane == 7, up, jnp.where(sublane == 0, low, 1.0))
    up, low, _, _ = lanes.factors(1, "avg")
    for b in range(8):
        share = share_z * (low if b == 0 else up) if b in (0, 7) else share_z
        for a in range(8):
            for h in halves:
                rows = pl.ds(64 * a + 8 * b, 8)
                inverse = 1.0 / dinv[h, rows, :]
                dinv[h, rows, :] = inverse
                w[h, rows, :] = inverse * (share * 0.5 if a in (0, 7) else share)

def whole_kernel(devices, weights, derivative, *refs):
    (
        near, far, near_other, far_other, third, third_parts, rm, dinv, w,
        cross_ref, matrix_ref, pair_ref,
        vel_out, pre_out, res_out,
        u, v, xs, z, r, y, s, p, x, flip, vel_own, pre_own, res_own, sems,
    ) = refs
    my_y, my_z = lax.axis_index("gy"), lax.axis_index("gz")
    is_low = my_z == 0
    fields = u.shape[0]
    halves = range(u.shape[1])
    lanes = Lanes((2 * devices[0], devices[1], 8))
    slab_rows = [pl.ds(64 * a, 64) for a in range(8)]
    pair_rows = [[pl.ds(64 * a + 16 * j, 16) for a in range(8)] for j in range(4)]

    blocks = Blocks(devices, True, near, far, near_other, far_other)
    for k in range(2):
        load_field(blocks, k, u.at[k], xs.at[k], lanes)

    def in_halves(g):
        return [g[:, 128 * h : 128 * (h + 1)] for h in halves]

    def product(row, count, split, a):
        high, low = split[0, slab_rows[a], :], split[1, slab_rows[a], :]
        parts = jnp.concatenate([high, low, high, low], axis=0)
        return in_halves(
            jnp.dot(matrix_ref[pl.ds(row, count), :], parts, preferred_element_type=F32)
        )

    def product_first(row, split, j):
        high, low = (
            jnp.concatenate([split[i, pair_rows[j][a], :] for a in range(8)], axis=0)
            for i in range(2)
        )
        parts = jnp.concatenate([high, low, high], axis=0)
        g = in_halves(
            jnp.dot(pair_ref[pl.ds(row, 128), :], parts, preferred_element_type=F32)
        )
        return [[part[16 * a : 16 * a + 16] for part in g] for a in range(8)]

    now, split = [u.at[0], u.at[1], third], [xs.at[0], xs.at[1], third_parts]
    buffers = (v, u)
    for step in range(SUBSTEPS):
        after = [buffers[step % 2].at[k] for k in range(fields)]
        for j in range(4):
            for k in range(fields):
                g = product_first(0, split[k], j)
                for a, rows in enumerate(pair_rows[j]):
                    for h in halves:
                        after[k][h, rows, :] = now[k][h, rows, :] - now[0][h, rows, :] * g[a][h]
        for group in SLAB_ORDER:
            for k in range(fields):
                slabs = {}
                for a in group:
                    g = product(0, 128, split[k], a)
                    slabs[a] = [
                        after[k][h, slab_rows[a], :]
                        - now[1][h, slab_rows[a], :] * g[h][:64]
                        - now[2][h, slab_rows[a], :] * g[h][64:]
                        for h in halves
                    ]
                settle(after[k], slabs, lanes, "wall", xs.at[k])
        now, split = after, [xs.at[k] for k in range(fields)]

    def own_block(source, own):
        flip[...] = source.T
        size = own.shape[2]
        for i in range(own.shape[0]):
            start = i * lanes.strides[0] + my_y * lanes.strides[1]
            block = flip[pl.ds(pl.multiple_of(start, 8), 8), :]
            own[i, 0] = jnp.where(is_low, block[:size], block[size:])

    for j in range(4):
        g = product_first(0, split[0], j)
        for a, rows in enumerate(pair_rows[j]):
            for h in halves:
                r[h, rows, :] = g[a][h]
    for group in SLAB_ORDER:
        slabs = {}
        for a in group:
            second, third = product(0, 64, split[1], a), product(64, 64, split[2], a)
            mass = cross_ref[pl.ds(0, 64), :] * float(-weights[a] / step_size)
            slabs[a] = [
                mass * (r[h, slab_rows[a], :] + second[h] + third[h]) for h in halves
            ]
        settle(r, slabs, lanes, "sum")

    for k in range(fields):
        own_block(now[k][0], vel_own.at[k])
    send_velocity = pltpu.make_async_copy(vel_own, vel_out, sems.at[0])
    send_velocity.start()

    def total(acc):
        return jnp.sum(jnp.sum(acc, axis=0, keepdims=True), axis=1, keepdims=True)

    def begin_sweep(update):
        acc = jnp.zeros((64, 128), F32)
        for a, rows in enumerate(slab_rows):
            for h in halves:
                res = r[h, rows, :]
                if update is not None:
                    alpha, beta = update
                    image = y[h, rows, :]
                    if beta is not None:
                        image = image + beta * s[h, rows, :]
                    s[h, rows, :] = image
                    res = res - alpha * image
                    r[h, rows, :] = res
                acc += res * res * w[h, rows, :]
                z[h, rows, :] = res * dinv[h, rows, :]
            store_split(xs.at[0], z, a)
        for j in range(4):
            g = product_first(128, xs.at[0], j)
            cross = cross_ref[pl.ds(16 * j, 16), :]
            for a, rows in enumerate(pair_rows[j]):
                for h in halves:
                    y[h, rows, :] = cross * g[a][h]
        return total(acc)

    gamma = begin_sweep(None)
    alpha = beta = None
    for sweep in range(ITERS):
        acc = jnp.zeros((64, 128), F32)
        for group in SLAB_ORDER:
            slabs = {}
            for a in group:
                g = product(128 + 64 * min(a, 7 - a), 64, xs.at[0], a)
                slabs[a] = []
                for h in halves:
                    here = z[h, slab_rows[a], :]
                    image = y[h, slab_rows[a], :] + g[h] + rm[h, slab_rows[a], :] * here
                    acc += image * here
                    slabs[a].append(image)
            settle(y, slabs, lanes, "sum")
        delta = total(acc)
        if sweep:
            beta = gamma / gamma_before
            alpha = gamma / (delta - beta * gamma / alpha)
        else:
            alpha = gamma / delta
        for rows in slab_rows:
            search = z[0, rows, :]
            if sweep:
                search = search + beta * p[rows, :]
            p[rows, :] = search
            x[rows, :] = x[rows, :] + alpha * search if sweep else alpha * search
        if sweep < ITERS - 1:
            gamma_before, gamma = gamma, begin_sweep((alpha, beta))
    for rows in slab_rows:
        r[0, rows, :] -= alpha * (y[0, rows, :] + beta * s[0, rows, :])

    own_block(x[...], pre_own)
    send_pressure = pltpu.make_async_copy(pre_own, pre_out, sems.at[1])
    send_pressure.start()
    own_block(r[0], res_own)
    send_residual = pltpu.make_async_copy(res_own, res_out, sems.at[2])
    send_residual.start()
    send_velocity.wait()
    send_pressure.wait()
    send_residual.wait()


def whole_body(devices, velocity, reaction):
    fields = velocity.shape[0]
    lanes = int(np.prod(devices)) * 8
    weights, derivative = host_tables()
    eye = np.eye(8)
    stiffness = derivative.T @ (weights[:, None] * derivative)
    stiff_sum = np.sum(weights[:, None] * derivative * derivative, axis=0)
    across = np.kron(stiffness, np.diag(weights)) + np.kron(np.diag(weights), stiffness)
    matrices = np.concatenate(
        [
            split_matrix(step_size * np.kron(derivative, eye)),
            split_matrix(step_size * np.kron(eye, derivative)),
        ]
        + [split_matrix(weights[a] * across) for a in range(4)]
    )
    along = [step_size * derivative, stiffness]
    pairs = np.concatenate([split_matrix(np.kron(m, np.eye(16)))[:, :384] for m in along])
    cross = np.outer(weights, weights).reshape(-1)
    sides = np.outer(stiff_sum, weights).reshape(-1) + np.outer(weights, stiff_sum).reshape(-1)
    cross = np.broadcast_to(np.concatenate([cross, sides])[:, None], (128, 128))

    vmem = pl.BlockSpec(memory_space=pltpu.VMEM)
    hbm = pl.BlockSpec(memory_space=pltpu.HBM)
    def swapped(block, axis, mask):
        count = lax.axis_size(axis)
        return lax.ppermute(block, axis, [(i, i ^ mask) for i in range(count)])

    block = jnp.concatenate([velocity, reaction[None]], axis=0)
    masks = range(1, devices[1])
    speeds = [swapped(velocity, "gy", mask) for mask in masks]
    reacts = [swapped(reaction, "gy", mask) for mask in masks]

    def column(picks, *others):
        return pl.pallas_call(
            functools.partial(column_kernel, len(masks), picks),
            out_shape=jax.ShapeDtypeStruct((devices[1], 2, 8, 512), F32),
            in_specs=[vmem] * (1 + len(others)),
            out_specs=vmem,
            compiler_params=SMALL,
        )(block, *others)

    first = column(((0, 0, 0), (1, 0, 1)), *speeds)
    second = column(((2, 0, 2), (fields, 1, None)), *speeds, *reacts)
    near = [paired(first, swapped(first, "gx", 1)), paired(second, swapped(second, "gx", 2))]
    far = [swapped(near[0], "gx", 2), swapped(near[1], "gx", 1)]
    others = [swapped(pair, "gz", 1) for pair in (*near, *far)]

    cross = jnp.asarray(cross, F32)
    shape = jax.ShapeDtypeStruct((lanes // 128, 512, 128), F32)
    field = pltpu.VMEM(shape.shape, F32)
    three = pltpu.VMEM((fields,) + shape.shape, F32)
    one_half = pltpu.VMEM((512, 128), F32)
    third = pl.pallas_call(
        functools.partial(diagonal_kernel, devices, weights, derivative),
        out_shape=[shape, jax.ShapeDtypeStruct((2, 512, lanes), BF16)] + [shape] * 3,
        in_specs=[vmem] * 5,
        out_specs=[vmem] * 5,
        compiler_params=pltpu.CompilerParams(vmem_limit_bytes=16 << 20),
        cost_estimate=pl.CostEstimate(flops=4000000, bytes_accessed=4000000, transcendentals=0),
    )(near[1], far[1], others[1], others[3], cross)
    own = pltpu.VMEM(reaction.shape, F32)
    return pl.pallas_call(
        functools.partial(whole_kernel, devices, weights, derivative),
        out_shape=(
            jax.ShapeDtypeStruct(velocity.shape, F32),
            jax.ShapeDtypeStruct(reaction.shape, F32),
            jax.ShapeDtypeStruct(reaction.shape, F32),
        ),
        in_specs=[vmem] * 12,
        out_specs=(hbm, hbm, hbm),
        scratch_shapes=[three, three, pltpu.VMEM((fields, 2, 512, lanes), BF16)]
        + [field] * 4
        + [one_half] * 2
        + [
            pltpu.VMEM((128, 512), F32),
            pltpu.VMEM(velocity.shape, F32),
            own,
            own,
            pltpu.SemaphoreType.DMA((3,)),
        ],
        compiler_params=pltpu.CompilerParams(vmem_limit_bytes=40 << 20),
    )(
        near[0], far[0], others[0], others[2], *third,
        cross, jnp.asarray(matrices), jnp.asarray(pairs),
    )


def extended(block, sides, width, periodic):
    for axis, dim in sides:
        count = lax.axis_size(axis)
        forward = [(i, i + 1) for i in range(count - 1)]
        if periodic:
            forward.append((count - 1, 0))
        backward = [(target, source) for source, target in forward]
        low = lax.ppermute(
            lax.slice_in_dim(block, block.shape[dim] - width, None, axis=dim), axis, forward
        )
        high = lax.ppermute(lax.slice_in_dim(block, 0, width, axis=dim), axis, backward)
        block = jnp.concatenate([low, block, high], axis=dim)
    return block


def derive(values, derivative, along_dim, transposed):
    layout = values.shape
    matrix = derivative.T if transposed else derivative
    blocks = values.reshape(-1, 8, 8, 8)
    patterns = ("aq,nqbc->nabc", "bq,naqc->nabc", "cq,nabq->nabc")
    result = jnp.einsum(patterns[along_dim], matrix, blocks, precision=lax.Precision.HIGHEST)
    return result.reshape(layout)


def place_face(values, target_axis, position, update):
    selector = tuple(
        (position if place == target_axis else slice(None) for place in range(values.ndim))
    )
    return values.at[selector].set(update)


def faces_along_x(sequence):
    return extended(sequence, (("gx", 0),), 1, True)


def faces_along_y(sequence):
    return extended(sequence, (("gy", 0),), 1, False)


def faces_along_z(sequence):
    return extended(sequence, (("gz", 0),), 1, False)


def join_faces(values, along_dim, exchanger):
    lower_face = jnp.moveaxis(jnp.take(values, 0, axis=4 + along_dim), 1 + along_dim, 0)
    upper_face = jnp.moveaxis(jnp.take(values, 7, axis=4 + along_dim), 1 + along_dim, 0)
    elements = lower_face.shape[0]
    face_shape = lower_face.shape
    sequence = jnp.stack([lower_face, upper_face], axis=1).reshape(2 * elements, -1)
    padded = exchanger(sequence)
    paired = padded.reshape(elements + 1, 2, -1)
    totals = paired[:, 0] + paired[:, 1]
    new_lower = jnp.moveaxis(totals[:-1].reshape(face_shape), 0, 1 + along_dim)
    new_upper = jnp.moveaxis(totals[1:].reshape(face_shape), 0, 1 + along_dim)
    values = place_face(values, 4 + along_dim, 0, new_lower)
    return place_face(values, 4 + along_dim, 7, new_upper)


def assemble(values):
    exchangers = (faces_along_x, faces_along_y, faces_along_z)
    dim_order = (0, 1, 2)
    for along_dim in dim_order:
        values = join_faces(values, along_dim, exchangers[along_dim])
    return values


def dim_factors(local_count, offset, total_count, bounded_by_walls):
    element_ids = offset + jnp.arange(local_count)
    node_ids = jnp.arange(8)
    at_end = (node_ids[None, :] == 0) | (node_ids[None, :] == 7)
    low_wall = (element_ids[:, None] == 0) & (node_ids[None, :] == 0)
    high_wall = (element_ids[:, None] == total_count - 1) & (node_ids[None, :] == 7)
    on_wall = (low_wall | high_wall) & bounded_by_walls
    shared = at_end & jnp.logical_not(on_wall)
    return (jnp.where(shared, 2.0, 1.0).astype(jnp.float32), on_wall.astype(jnp.float32))


def spread_body(velocity, reaction):
    weights, derivative = tables()
    count_x, count_y, count_z = (reaction.shape[0], reaction.shape[1], reaction.shape[2])
    speed = velocity.reshape(3, count_x, count_y, count_z, 8, 8, 8)
    react = reaction.reshape(1, count_x, count_y, count_z, 8, 8, 8)
    mass_matrix = weights[:, None, None] * weights[None, :, None] * weights[None, None, :]
    factor_x, wall_x = dim_factors(
        count_x, lax.axis_index("gx") * count_x, lax.axis_size("gx") * count_x, False
    )
    factor_y, wall_y = dim_factors(
        count_y, lax.axis_index("gy") * count_y, lax.axis_size("gy") * count_y, True
    )
    factor_z, wall_z = dim_factors(
        count_z, lax.axis_index("gz") * count_z, lax.axis_size("gz") * count_z, True
    )
    multiplicity = (
        factor_x[None, :, None, None, :, None, None]
        * factor_y[None, None, :, None, None, :, None]
        * factor_z[None, None, None, :, None, None, :]
    )
    interior = (1.0 - wall_y[None, None, :, None, None, :, None]) * (
        1.0 - wall_z[None, None, None, :, None, None, :]
    )
    stiff_sum = jnp.sum(weights[:, None] * derivative * derivative, axis=0)
    diag_local = (
        stiff_sum[:, None, None] * weights[None, :, None] * weights[None, None, :]
        + weights[:, None, None] * stiff_sum[None, :, None] * weights[None, None, :]
        + weights[:, None, None] * weights[None, :, None] * stiff_sum[None, None, :]
    )
    diag_terms = diag_local + react * mass_matrix
    speed = assemble(speed) / multiplicity
    diagonal = None
    for substep in range(SUBSTEPS):
        gradient_fields = [derive(speed, derivative, along_dim, False) for along_dim in range(3)]
        transport = (
            speed[0:1] * gradient_fields[0]
            + speed[1:2] * gradient_fields[1]
            + speed[2:3] * gradient_fields[2]
        )
        tendency = assemble(mass_matrix * transport) / (mass_matrix * multiplicity)
        speed = interior * (speed - step_size * tendency)
    spread = (
        derive(speed[0:1], derivative, 0, False)
        + derive(speed[1:2], derivative, 1, False)
        + derive(speed[2:3], derivative, 2, False)
    )
    source = -assemble(mass_matrix * spread)
    diagonal = assemble(diag_terms)

    def local_inner(first, second):
        return jnp.sum(first * second / multiplicity)

    def norm_weighted_mass(residual_vec, precond_vec):
        return lax.psum(local_inner(residual_vec, precond_vec), ("gx", "gy", "gz"))

    pressure = jnp.zeros_like(source)
    residual = source
    precond = residual / diagonal
    search = precond
    progress = norm_weighted_mass(residual, precond)
    for sweep_index in range(ITERS):
        local_sum = react * mass_matrix * search
        for apply_along_dim in range(3):
            local_sum = local_sum + derive(
                mass_matrix * derive(search, derivative, apply_along_dim, False),
                derivative,
                apply_along_dim,
                True,
            )
        applied = assemble(local_sum)
        step_length = progress / lax.psum(local_inner(search, applied), ("gx", "gy", "gz"))
        pressure = pressure + step_length * search
        residual = residual - step_length * applied
        precond = residual / diagonal
        progress_next = norm_weighted_mass(residual, precond)
        search = precond + progress_next / progress * search
        progress = progress_next
    return (
        speed.reshape(3, count_x, count_y, count_z, 512),
        pressure.reshape(count_x, count_y, count_z, 512),
        residual.reshape(count_x, count_y, count_z, 512),
    )


def solution(mesh):
    in_specs = (P(None, "gx", "gy", "gz", None), P("gx", "gy", "gz", None))
    out_specs = (
        P(None, "gx", "gy", "gz", None),
        P("gx", "gy", "gz", None),
        P("gx", "gy", "gz", None),
    )
    devices = tuple(mesh.shape[axis] for axis in ("gx", "gy", "gz"))

    def body(velocity, reaction):
        if devices == (4, 4, 2) and reaction.shape[:3] == (2, 1, 4):
            return whole_body(devices, velocity, reaction)
        return spread_body(velocity, reaction)

    return jax.shard_map(body, mesh=mesh, in_specs=in_specs, out_specs=out_specs, check_vma=False)
```

```python
import functools

import jax
import jax.numpy as jnp
import numpy as np
from jax import lax
from jax.experimental import pallas as pl
from jax.experimental.pallas import tpu as pltpu
from jax.sharding import PartitionSpec as P

SUBSTEPS = 2
ITERS = 4
step_size = 0.02

F32 = jnp.float32
BF16 = jnp.bfloat16


def legendre_seven(points):
    earlier = points * 0.0 + 1.0
    current = points
    for degree in range(1, 7):
        earlier, current = (
            current,
            ((2 * degree + 1) * points * current - degree * earlier) / (degree + 1),
        )
    return current


def host_tables():
    half = np.array([0.20929921790247888, 0.5917001814331423, 0.8717401485096066, 1.0])
    points = np.concatenate([-half[::-1], half])
    legendre = legendre_seven(points)
    weights = 2.0 / (56.0 * legendre**2)
    spacing = points[:, None] - points[None, :] + np.eye(8)
    derivative = legendre[:, None] / legendre[None, :] / spacing * (1.0 - np.eye(8))
    derivative[0, 0] = -14.0
    derivative[7, 7] = 14.0
    return weights, derivative


def tables():
    weights, derivative = host_tables()
    return (jnp.asarray(weights, F32), jnp.asarray(derivative, F32))


def split_matrix(matrix):
    matrix = matrix.astype(np.float32)
    high = matrix.astype(jnp.bfloat16)
    low = (matrix - high.astype(np.float32)).astype(jnp.bfloat16)
    return np.concatenate([high, high, low], axis=1)


def split_parts(values):
    high = values.astype(BF16)
    return high, (values - high.astype(F32)).astype(BF16)


def roll_lanes(parts, shift):
    turned = [pltpu.roll(part, shift, 1) for part in parts]
    lane = lax.broadcasted_iota(jnp.int32, parts[0].shape, 1)
    return [jnp.where(lane < shift, turned[i - 1], turned[i]) for i in range(len(parts))]


def roll_lanes_back(parts, shift):
    turned = [pltpu.roll(part, 128 - shift, 1) for part in parts]
    lane = lax.broadcasted_iota(jnp.int32, parts[0].shape, 1)
    count = len(parts)
    return [
        jnp.where(lane < 128 - shift, turned[i], turned[(i + 1) % count]) for i in range(count)
    ]


class Lanes:
    def __init__(self, counts):
        self.strides = (counts[1] * counts[2], counts[2], 1)
        lane = lax.broadcasted_iota(jnp.int32, (1, 128), 1)
        place = {1: (lane // counts[2]) % counts[1], 2: lane % counts[2]}
        self.has_next = {d: place[d] < counts[d] - 1 for d in (1, 2)}
        self.has_prev = {d: place[d] > 0 for d in (1, 2)}

    def factors(self, direction, mode):
        n, p = self.has_next[direction], self.has_prev[direction]
        if mode == "sum":
            return None, None, jnp.where(n, 1.0, 0.0), jnp.where(p, 1.0, 0.0)
        alone = 1.0 if mode == "avg" else 0.0
        return (
            jnp.where(n, 0.5, alone),
            jnp.where(p, 0.5, alone),
            jnp.where(n, 0.5, 0.0),
            jnp.where(p, 0.5, 0.0),
        )


def settle(ref, slabs, lanes, mode, split=None):
    if 0 in slabs:
        lower, upper = slabs[0], slabs[7]
        stride = lanes.strides[0]
        new_upper = [a + b for a, b in zip(upper, roll_lanes_back(lower, stride))]
        new_lower = [a + b for a, b in zip(lower, roll_lanes(upper, stride))]
        if mode != "sum":
            new_upper = [0.5 * a for a in new_upper]
            new_lower = [0.5 * a for a in new_lower]
        slabs = {**slabs, 0: new_lower, 7: new_upper}

    def joined(lower, upper, direction):
        stride = lanes.strides[direction]
        own_up, own_low, from_next, from_prev = lanes.factors(direction, mode)
        following, previous = pltpu.roll(lower, 128 - stride, 1), pltpu.roll(upper, stride, 1)
        if mode == "sum":
            return lower + previous * from_prev, upper + following * from_next
        if mode == "wall":
            return (lower + previous) * from_prev, (upper + following) * from_next
        return lower * own_low + previous * from_prev, upper * own_up + following * from_next

    for a, parts in slabs.items():
        for h, part in enumerate(parts):
            lower, upper = joined(part[:8], part[56:], 1)
            ref[h, pl.ds(64 * a, 8), :] = lower
            ref[h, pl.ds(64 * a + 8, 48), :] = part[8:56]
            ref[h, pl.ds(64 * a + 56, 8), :] = upper
            first, last = pl.ds(64 * a, 8, stride=8), pl.ds(64 * a + 7, 8, stride=8)
            lower, upper = joined(ref[h, first, :], ref[h, last, :], 2)
            ref[h, first, :] = lower
            ref[h, last, :] = upper
        if split is not None:
            store_split(split, ref, a)


def store_split(split, ref, a):
    rows = pl.ds(64 * a, 64)
    values = jnp.concatenate([ref[h, rows, :] for h in range(ref.shape[0])], axis=1)
    split[0, rows, :], split[1, rows, :] = split_parts(values)


SLAB_ORDER = ((0, 7), (1,), (2,), (3,), (4,), (5,), (6,))


def column_kernel(*refs):
    blocks, outs = refs[:-2], refs[-2:]
    is_low = lax.axis_index("gz") == 0
    for j, block in enumerate(blocks):
        for k in range(block.shape[0]):
            low, high = block[k, 0, 0], block[k, 1, 0]
            straight = jnp.concatenate([low, high], axis=0)
            turned = jnp.concatenate([high, low], axis=0)
            outs[k // 2][j, k % 2] = jnp.where(is_low, straight, turned)


def pair_kernel(first, second, out):
    out[0] = first[...]
    out[1] = second[...]


SMALL = pltpu.CompilerParams(vmem_limit_bytes=1 << 20)


def paired(first, second):
    vmem = pl.BlockSpec(memory_space=pltpu.VMEM)
    return pl.pallas_call(
        pair_kernel,
        out_shape=jax.ShapeDtypeStruct((2,) + first.shape, F32),
        in_specs=[vmem] * 2,
        out_specs=vmem,
        compiler_params=SMALL,
    )(first, second)


def whole_kernel(devices, weights, derivative, *refs):
    (
        near, far, near_other, far_other, cross_ref, matrix_ref, pair_ref,
        vel_out, pre_out, res_out,
        u, v, xs, rm, w, dinv, z, r, y, s, p, x, flip, vel_own, pre_own, res_own, sems,
    ) = [refs[0:2], refs[2:4], refs[4:6], refs[6:8], *refs[8:]]
    my_y, my_z = lax.axis_index("gy"), lax.axis_index("gz")
    fields = u.shape[0]
    halves = range(u.shape[1])
    per_half = devices[0] // len(halves)
    lanes = Lanes((2 * devices[0], devices[1], 8))
    stiff_sum = np.sum(weights[:, None] * derivative * derivative, axis=0)
    slab_rows = [pl.ds(64 * a, 64) for a in range(8)]
    pair_rows = [[pl.ds(64 * a + 16 * j, 16) for a in range(8)] for j in range(4)]

    is_low = my_z == 0
    is_even = lax.axis_index("gx") % 2 == 0
    sublane = lax.broadcasted_iota(jnp.int32, (8, 128), 0)
    own_rows = (sublane < 4) == is_low
    entry = [my_y ^ j for j in range(devices[1])]

    def tile(near, far, k, ahead, at, cols):
        by_x = (near[0], 1) if k < 2 else (far[1], 0)
        diagonal = (far[k // 2], 1)
        if ahead == 0:
            ref, i = near[k // 2], 0
        elif ahead == 2:
            ref, i = (far[0], 0) if k < 2 else (near[1], 1)
        else:
            first, second = (by_x, diagonal) if ahead == 1 else (diagonal, by_x)
            first, second = (ref[i, at, k % 2, :, cols] for ref, i in (first, second))
            return jnp.where(is_even, first, second)
        return ref[i, at, k % 2, :, cols]

    def to_lanes(k, chunk):
        cols = pl.ds(128 * chunk, 128)
        parts = []
        for half in halves:
            tiles = []
            for i in range(per_half):
                first, second = [], []
                for at in entry:
                    here = tile(near, far, k, half * per_half + i, at, cols)
                    there = tile(near_other, far_other, k, half * per_half + i, at, cols)
                    first.append(jnp.where(own_rows, here, there))
                    second.append(pltpu.roll(jnp.where(own_rows, there, here), 4, 0))
                tiles += first + second
            parts.append(jnp.concatenate(tiles, axis=0).T)
        return parts

    def halves_of(parts, chunk):
        return {2 * chunk + i: [part[64 * i : 64 * i + 64] for part in parts] for i in range(2)}

    for k in range(fields):
        for chunks in ((0, 3), (1,), (2,)):
            slabs = {}
            for chunk in chunks:
                slabs.update(halves_of(to_lanes(k, chunk), chunk))
            settle(u.at[k], slabs, lanes, "avg", xs.at[k])

    for chunks in ((0, 3), (1,), (2,)):
        slabs = {}
        for chunk in chunks:
            for a, react in halves_of(to_lanes(fields, chunk), chunk).items():
                mass = cross_ref[pl.ds(0, 64), :] * float(weights[a])
                diag = cross_ref[pl.ds(0, 64), :] * float(stiff_sum[a])
                diag += cross_ref[pl.ds(64, 64), :] * float(weights[a])
                react = [part * mass for part in react]
                for h in halves:
                    rm[h, slab_rows[a], :] = react[h]
                slabs[a] = [part + diag for part in react]
        settle(dinv, slabs, lanes, "sum")

    up, low, _, _ = lanes.factors(2, "avg")
    share_z = jnp.where(sublane == 7, up, jnp.where(sublane == 0, low, 1.0))
    up, low, _, _ = lanes.factors(1, "avg")
    for b in range(8):
        share = share_z * (low if b == 0 else up) if b in (0, 7) else share_z
        for a in range(8):
            for h in halves:
                rows = pl.ds(64 * a + 8 * b, 8)
                inverse = 1.0 / dinv[h, rows, :]
                dinv[h, rows, :] = inverse
                w[h, rows, :] = inverse * (share * 0.5 if a in (0, 7) else share)

    def in_halves(g):
        return [g[:, 128 * h : 128 * (h + 1)] for h in halves]

    def product(row, count, k, a):
        high, low = xs[k, 0, slab_rows[a], :], xs[k, 1, slab_rows[a], :]
        parts = jnp.concatenate([high, low, high], axis=0)
        return in_halves(
            jnp.dot(matrix_ref[pl.ds(row, count), :], parts, preferred_element_type=F32)
        )

    def product_first(row, k, j):
        high, low = (
            jnp.concatenate([xs[k, i, pair_rows[j][a], :] for a in range(8)], axis=0)
            for i in range(2)
        )
        parts = jnp.concatenate([high, low, high], axis=0)
        g = in_halves(
            jnp.dot(pair_ref[pl.ds(row, 128), :], parts, preferred_element_type=F32)
        )
        return [[part[16 * a : 16 * a + 16] for part in g] for a in range(8)]

    now, after = u, v
    for _ in range(SUBSTEPS):
        for k in range(fields):
            for j in range(4):
                g = product_first(0, k, j)
                for a, rows in enumerate(pair_rows[j]):
                    for h in halves:
                        after[k, h, rows, :] = now[k, h, rows, :] - now[0, h, rows, :] * g[a][h]
            for group in SLAB_ORDER:
                slabs = {}
                for a in group:
                    g = product(0, 128, k, a)
                    slabs[a] = [
                        after[k, h, slab_rows[a], :]
                        - now[1, h, slab_rows[a], :] * g[h][:64]
                        - now[2, h, slab_rows[a], :] * g[h][64:]
                        for h in halves
                    ]
                settle(after.at[k], slabs, lanes, "wall", xs.at[k])
        now, after = after, now

    def own_block(source, own):
        flip[...] = source.T
        size = own.shape[2]
        for i in range(own.shape[0]):
            start = i * lanes.strides[0] + my_y * lanes.strides[1]
            block = flip[pl.ds(pl.multiple_of(start, 8), 8), :]
            own[i, 0] = jnp.where(is_low, block[:size], block[size:])

    for j in range(4):
        g = product_first(0, 0, j)
        for a, rows in enumerate(pair_rows[j]):
            for h in halves:
                r[h, rows, :] = g[a][h]
    for group in SLAB_ORDER:
        slabs = {}
        for a in group:
            second, third = product(0, 64, 1, a), product(64, 64, 2, a)
            mass = cross_ref[pl.ds(0, 64), :] * float(-weights[a] / step_size)
            slabs[a] = [
                mass * (r[h, slab_rows[a], :] + second[h] + third[h]) for h in halves
            ]
        settle(r, slabs, lanes, "sum")

    for k in range(fields):
        own_block(now[k, 0], vel_own.at[k])
    send_velocity = pltpu.make_async_copy(vel_own, vel_out, sems.at[0])
    send_velocity.start()

    def total(acc):
        return jnp.sum(jnp.sum(acc, axis=0, keepdims=True), axis=1, keepdims=True)

    def begin_sweep(update):
        acc = jnp.zeros((64, 128), F32)
        for a, rows in enumerate(slab_rows):
            for h in halves:
                res = r[h, rows, :]
                if update is not None:
                    alpha, beta = update
                    image = y[h, rows, :]
                    if beta is not None:
                        image = image + beta * s[h, rows, :]
                    s[h, rows, :] = image
                    res = res - alpha * image
                    r[h, rows, :] = res
                acc += res * res * w[h, rows, :]
                z[h, rows, :] = res * dinv[h, rows, :]
            store_split(xs.at[0], z, a)
        for j in range(4):
            g = product_first(128, 0, j)
            cross = cross_ref[pl.ds(16 * j, 16), :]
            for a, rows in enumerate(pair_rows[j]):
                for h in halves:
                    y[h, rows, :] = cross * g[a][h]
        return total(acc)

    gamma = begin_sweep(None)
    alpha = beta = None
    for sweep in range(ITERS):
        acc = jnp.zeros((64, 128), F32)
        for group in SLAB_ORDER:
            slabs = {}
            for a in group:
                g = product(128 + 64 * min(a, 7 - a), 64, 0, a)
                slabs[a] = []
                for h in halves:
                    here = z[h, slab_rows[a], :]
                    image = y[h, slab_rows[a], :] + g[h] + rm[h, slab_rows[a], :] * here
                    acc += image * here
                    slabs[a].append(image)
            settle(y, slabs, lanes, "sum")
        delta = total(acc)
        if sweep:
            beta = gamma / gamma_before
            alpha = gamma / (delta - beta * gamma / alpha)
        else:
            alpha = gamma / delta
        for rows in slab_rows:
            search = z[0, rows, :]
            if sweep:
                search = search + beta * p[rows, :]
            p[rows, :] = search
            x[rows, :] = x[rows, :] + alpha * search if sweep else alpha * search
        if sweep < ITERS - 1:
            gamma_before, gamma = gamma, begin_sweep((alpha, beta))
    for rows in slab_rows:
        r[0, rows, :] -= alpha * (y[0, rows, :] + beta * s[0, rows, :])

    own_block(x[...], pre_own)
    send_pressure = pltpu.make_async_copy(pre_own, pre_out, sems.at[1])
    send_pressure.start()
    own_block(r[0], res_own)
    send_residual = pltpu.make_async_copy(res_own, res_out, sems.at[2])
    send_residual.start()
    send_velocity.wait()
    send_pressure.wait()
    send_residual.wait()


def whole_body(devices, velocity, reaction):
    fields = velocity.shape[0]
    lanes = int(np.prod(devices)) * 8
    weights, derivative = host_tables()
    eye = np.eye(8)
    stiffness = derivative.T @ (weights[:, None] * derivative)
    stiff_sum = np.sum(weights[:, None] * derivative * derivative, axis=0)
    across = np.kron(stiffness, np.diag(weights)) + np.kron(np.diag(weights), stiffness)
    matrices = np.concatenate(
        [
            split_matrix(step_size * np.kron(derivative, eye)),
            split_matrix(step_size * np.kron(eye, derivative)),
        ]
        + [split_matrix(weights[a] * across) for a in range(4)]
    )
    along = [step_size * derivative, stiffness]
    pairs = np.concatenate([split_matrix(np.kron(m, np.eye(16))) for m in along])
    cross = np.outer(weights, weights).reshape(-1)
    sides = np.outer(stiff_sum, weights).reshape(-1) + np.outer(weights, stiff_sum).reshape(-1)
    cross = np.broadcast_to(np.concatenate([cross, sides])[:, None], (128, 128))

    vmem = pl.BlockSpec(memory_space=pltpu.VMEM)
    hbm = pl.BlockSpec(memory_space=pltpu.HBM)
    def swapped(block, axis, mask):
        count = lax.axis_size(axis)
        return lax.ppermute(block, axis, [(i, i ^ mask) for i in range(count)])

    block = jnp.concatenate([velocity, reaction[None]], axis=0)
    column = jax.ShapeDtypeStruct((devices[1], 2, 8, 512), F32)
    first, second = pl.pallas_call(
        column_kernel,
        out_shape=[column, column],
        in_specs=[vmem] * devices[1],
        out_specs=[vmem, vmem],
        compiler_params=SMALL,
    )(block, *(swapped(block, "gy", mask) for mask in range(1, devices[1])))
    near = [paired(first, swapped(first, "gx", 1)), paired(second, swapped(second, "gx", 2))]
    far = [swapped(near[0], "gx", 2), swapped(near[1], "gx", 1)]
    others = [swapped(pair, "gz", 1) for pair in (*near, *far)]

    field = pltpu.VMEM((lanes // 128, 512, 128), F32)
    three = pltpu.VMEM((fields, lanes // 128, 512, 128), F32)
    one_half = pltpu.VMEM((512, 128), F32)
    own = pltpu.VMEM(reaction.shape, F32)
    return pl.pallas_call(
        functools.partial(whole_kernel, devices, weights, derivative),
        out_shape=(
            jax.ShapeDtypeStruct(velocity.shape, F32),
            jax.ShapeDtypeStruct(reaction.shape, F32),
            jax.ShapeDtypeStruct(reaction.shape, F32),
        ),
        in_specs=[vmem] * 11,
        out_specs=(hbm, hbm, hbm),
        scratch_shapes=[three, three, pltpu.VMEM((fields, 2, 512, lanes), BF16)]
        + [field] * 7
        + [one_half] * 2
        + [
            pltpu.VMEM((128, 512), F32),
            pltpu.VMEM(velocity.shape, F32),
            own,
            own,
            pltpu.SemaphoreType.DMA((3,)),
        ],
        compiler_params=pltpu.CompilerParams(vmem_limit_bytes=40 << 20),
    )(
        *near, *far, *others, jnp.asarray(cross, F32), jnp.asarray(matrices), jnp.asarray(pairs),
    )


def extended(block, sides, width, periodic):
    for axis, dim in sides:
        count = lax.axis_size(axis)
        forward = [(i, i + 1) for i in range(count - 1)]
        if periodic:
            forward.append((count - 1, 0))
        backward = [(target, source) for source, target in forward]
        low = lax.ppermute(
            lax.slice_in_dim(block, block.shape[dim] - width, None, axis=dim), axis, forward
        )
        high = lax.ppermute(lax.slice_in_dim(block, 0, width, axis=dim), axis, backward)
        block = jnp.concatenate([low, block, high], axis=dim)
    return block


def derive(values, derivative, along_dim, transposed):
    layout = values.shape
    matrix = derivative.T if transposed else derivative
    blocks = values.reshape(-1, 8, 8, 8)
    patterns = ("aq,nqbc->nabc", "bq,naqc->nabc", "cq,nabq->nabc")
    result = jnp.einsum(patterns[along_dim], matrix, blocks, precision=lax.Precision.HIGHEST)
    return result.reshape(layout)


def place_face(values, target_axis, position, update):
    selector = tuple(
        (position if place == target_axis else slice(None) for place in range(values.ndim))
    )
    return values.at[selector].set(update)


def faces_along_x(sequence):
    return extended(sequence, (("gx", 0),), 1, True)


def faces_along_y(sequence):
    return extended(sequence, (("gy", 0),), 1, False)


def faces_along_z(sequence):
    return extended(sequence, (("gz", 0),), 1, False)


def join_faces(values, along_dim, exchanger):
    lower_face = jnp.moveaxis(jnp.take(values, 0, axis=4 + along_dim), 1 + along_dim, 0)
    upper_face = jnp.moveaxis(jnp.take(values, 7, axis=4 + along_dim), 1 + along_dim, 0)
    elements = lower_face.shape[0]
    face_shape = lower_face.shape
    sequence = jnp.stack([lower_face, upper_face], axis=1).reshape(2 * elements, -1)
    padded = exchanger(sequence)
    paired = padded.reshape(elements + 1, 2, -1)
    totals = paired[:, 0] + paired[:, 1]
    new_lower = jnp.moveaxis(totals[:-1].reshape(face_shape), 0, 1 + along_dim)
    new_upper = jnp.moveaxis(totals[1:].reshape(face_shape), 0, 1 + along_dim)
    values = place_face(values, 4 + along_dim, 0, new_lower)
    return place_face(values, 4 + along_dim, 7, new_upper)


def assemble(values):
    exchangers = (faces_along_x, faces_along_y, faces_along_z)
    dim_order = (0, 1, 2)
    for along_dim in dim_order:
        values = join_faces(values, along_dim, exchangers[along_dim])
    return values


def dim_factors(local_count, offset, total_count, bounded_by_walls):
    element_ids = offset + jnp.arange(local_count)
    node_ids = jnp.arange(8)
    at_end = (node_ids[None, :] == 0) | (node_ids[None, :] == 7)
    low_wall = (element_ids[:, None] == 0) & (node_ids[None, :] == 0)
    high_wall = (element_ids[:, None] == total_count - 1) & (node_ids[None, :] == 7)
    on_wall = (low_wall | high_wall) & bounded_by_walls
    shared = at_end & jnp.logical_not(on_wall)
    return (jnp.where(shared, 2.0, 1.0).astype(jnp.float32), on_wall.astype(jnp.float32))


def spread_body(velocity, reaction):
    weights, derivative = tables()
    count_x, count_y, count_z = (reaction.shape[0], reaction.shape[1], reaction.shape[2])
    speed = velocity.reshape(3, count_x, count_y, count_z, 8, 8, 8)
    react = reaction.reshape(1, count_x, count_y, count_z, 8, 8, 8)
    mass_matrix = weights[:, None, None] * weights[None, :, None] * weights[None, None, :]
    factor_x, wall_x = dim_factors(
        count_x, lax.axis_index("gx") * count_x, lax.axis_size("gx") * count_x, False
    )
    factor_y, wall_y = dim_factors(
        count_y, lax.axis_index("gy") * count_y, lax.axis_size("gy") * count_y, True
    )
    factor_z, wall_z = dim_factors(
        count_z, lax.axis_index("gz") * count_z, lax.axis_size("gz") * count_z, True
    )
    multiplicity = (
        factor_x[None, :, None, None, :, None, None]
        * factor_y[None, None, :, None, None, :, None]
        * factor_z[None, None, None, :, None, None, :]
    )
    interior = (1.0 - wall_y[None, None, :, None, None, :, None]) * (
        1.0 - wall_z[None, None, None, :, None, None, :]
    )
    stiff_sum = jnp.sum(weights[:, None] * derivative * derivative, axis=0)
    diag_local = (
        stiff_sum[:, None, None] * weights[None, :, None] * weights[None, None, :]
        + weights[:, None, None] * stiff_sum[None, :, None] * weights[None, None, :]
        + weights[:, None, None] * weights[None, :, None] * stiff_sum[None, None, :]
    )
    diag_terms = diag_local + react * mass_matrix
    speed = assemble(speed) / multiplicity
    diagonal = None
    for substep in range(SUBSTEPS):
        gradient_fields = [derive(speed, derivative, along_dim, False) for along_dim in range(3)]
        transport = (
            speed[0:1] * gradient_fields[0]
            + speed[1:2] * gradient_fields[1]
            + speed[2:3] * gradient_fields[2]
        )
        tendency = assemble(mass_matrix * transport) / (mass_matrix * multiplicity)
        speed = interior * (speed - step_size * tendency)
    spread = (
        derive(speed[0:1], derivative, 0, False)
        + derive(speed[1:2], derivative, 1, False)
        + derive(speed[2:3], derivative, 2, False)
    )
    source = -assemble(mass_matrix * spread)
    diagonal = assemble(diag_terms)

    def local_inner(first, second):
        return jnp.sum(first * second / multiplicity)

    def norm_weighted_mass(residual_vec, precond_vec):
        return lax.psum(local_inner(residual_vec, precond_vec), ("gx", "gy", "gz"))

    pressure = jnp.zeros_like(source)
    residual = source
    precond = residual / diagonal
    search = precond
    progress = norm_weighted_mass(residual, precond)
    for sweep_index in range(ITERS):
        local_sum = react * mass_matrix * search
        for apply_along_dim in range(3):
            local_sum = local_sum + derive(
                mass_matrix * derive(search, derivative, apply_along_dim, False),
                derivative,
                apply_along_dim,
                True,
            )
        applied = assemble(local_sum)
        step_length = progress / lax.psum(local_inner(search, applied), ("gx", "gy", "gz"))
        pressure = pressure + step_length * search
        residual = residual - step_length * applied
        precond = residual / diagonal
        progress_next = norm_weighted_mass(residual, precond)
        search = precond + progress_next / progress * search
        progress = progress_next
    return (
        speed.reshape(3, count_x, count_y, count_z, 512),
        pressure.reshape(count_x, count_y, count_z, 512),
        residual.reshape(count_x, count_y, count_z, 512),
    )


def solution(mesh):
    in_specs = (P(None, "gx", "gy", "gz", None), P("gx", "gy", "gz", None))
    out_specs = (
        P(None, "gx", "gy", "gz", None),
        P("gx", "gy", "gz", None),
        P("gx", "gy", "gz", None),
    )
    devices = tuple(mesh.shape[axis] for axis in ("gx", "gy", "gz"))

    def body(velocity, reaction):
        if devices == (4, 4, 2) and reaction.shape[:3] == (2, 1, 4):
            return whole_body(devices, velocity, reaction)
        return spread_body(velocity, reaction)

    return jax.shard_map(body, mesh=mesh, in_specs=in_specs, out_specs=out_specs, check_vma=False)
```

```python
import functools

import jax
import jax.numpy as jnp
import numpy as np
from jax import lax
from jax.experimental import pallas as pl
from jax.experimental.pallas import tpu as pltpu
from jax.sharding import PartitionSpec as P

SUBSTEPS = 2
ITERS = 4
step_size = 0.02

F32 = jnp.float32
BF16 = jnp.bfloat16


def legendre_seven(points):
    earlier = points * 0.0 + 1.0
    current = points
    for degree in range(1, 7):
        earlier, current = (
            current,
            ((2 * degree + 1) * points * current - degree * earlier) / (degree + 1),
        )
    return current


def host_tables():
    half = np.array([0.20929921790247888, 0.5917001814331423, 0.8717401485096066, 1.0])
    points = np.concatenate([-half[::-1], half])
    legendre = legendre_seven(points)
    weights = 2.0 / (56.0 * legendre**2)
    spacing = points[:, None] - points[None, :] + np.eye(8)
    derivative = legendre[:, None] / legendre[None, :] / spacing * (1.0 - np.eye(8))
    derivative[0, 0] = -14.0
    derivative[7, 7] = 14.0
    return weights, derivative


def tables():
    weights, derivative = host_tables()
    return (jnp.asarray(weights, F32), jnp.asarray(derivative, F32))


def split_matrix(matrix):
    matrix = matrix.astype(np.float32)
    high = matrix.astype(jnp.bfloat16)
    low = (matrix - high.astype(np.float32)).astype(jnp.bfloat16)
    return np.concatenate([high, high, low], axis=1)


def split_parts(values):
    high = values.astype(BF16)
    return high, (values - high.astype(F32)).astype(BF16)


def roll_lanes(parts, shift):
    turned = [pltpu.roll(part, shift, 1) for part in parts]
    lane = lax.broadcasted_iota(jnp.int32, parts[0].shape, 1)
    return [jnp.where(lane < shift, turned[i - 1], turned[i]) for i in range(len(parts))]


def roll_lanes_back(parts, shift):
    turned = [pltpu.roll(part, 128 - shift, 1) for part in parts]
    lane = lax.broadcasted_iota(jnp.int32, parts[0].shape, 1)
    count = len(parts)
    return [
        jnp.where(lane < 128 - shift, turned[i], turned[(i + 1) % count]) for i in range(count)
    ]


class Lanes:
    def __init__(self, counts):
        self.strides = (counts[1] * counts[2], counts[2], 1)
        lane = lax.broadcasted_iota(jnp.int32, (1, 128), 1)
        place = {1: (lane // counts[2]) % counts[1], 2: lane % counts[2]}
        self.has_next = {d: place[d] < counts[d] - 1 for d in (1, 2)}
        self.has_prev = {d: place[d] > 0 for d in (1, 2)}

    def factors(self, direction, mode):
        n, p = self.has_next[direction], self.has_prev[direction]
        if mode == "sum":
            return None, None, jnp.where(n, 1.0, 0.0), jnp.where(p, 1.0, 0.0)
        alone = 1.0 if mode == "avg" else 0.0
        return (
            jnp.where(n, 0.5, alone),
            jnp.where(p, 0.5, alone),
            jnp.where(n, 0.5, 0.0),
            jnp.where(p, 0.5, 0.0),
        )


def settle(ref, slabs, lanes, mode, split=None):
    if 0 in slabs:
        lower, upper = slabs[0], slabs[7]
        stride = lanes.strides[0]
        new_upper = [a + b for a, b in zip(upper, roll_lanes_back(lower, stride))]
        new_lower = [a + b for a, b in zip(lower, roll_lanes(upper, stride))]
        if mode != "sum":
            new_upper = [0.5 * a for a in new_upper]
            new_lower = [0.5 * a for a in new_lower]
        slabs = {**slabs, 0: new_lower, 7: new_upper}

    def joined(lower, upper, direction):
        stride = lanes.strides[direction]
        own_up, own_low, from_next, from_prev = lanes.factors(direction, mode)
        following, previous = pltpu.roll(lower, 128 - stride, 1), pltpu.roll(upper, stride, 1)
        if mode == "sum":
            return lower + previous * from_prev, upper + following * from_next
        if mode == "wall":
            return (lower + previous) * from_prev, (upper + following) * from_next
        return lower * own_low + previous * from_prev, upper * own_up + following * from_next

    for a, parts in slabs.items():
        for h, part in enumerate(parts):
            lower, upper = joined(part[:8], part[56:], 1)
            ref[h, pl.ds(64 * a, 8), :] = lower
            ref[h, pl.ds(64 * a + 8, 48), :] = part[8:56]
            ref[h, pl.ds(64 * a + 56, 8), :] = upper
            first, last = pl.ds(64 * a, 8, stride=8), pl.ds(64 * a + 7, 8, stride=8)
            lower, upper = joined(ref[h, first, :], ref[h, last, :], 2)
            ref[h, first, :] = lower
            ref[h, last, :] = upper
        if split is not None:
            store_split(split, ref, a)


def store_split(split, ref, a):
    rows = pl.ds(64 * a, 64)
    values = jnp.concatenate([ref[h, rows, :] for h in range(ref.shape[0])], axis=1)
    split[0, rows, :], split[1, rows, :] = split_parts(values)


SLAB_ORDER = ((0, 7), (1,), (2,), (3,), (4,), (5,), (6,))


def column_kernel(*refs):
    blocks, outs = refs[:-2], refs[-2:]
    is_low = lax.axis_index("gz") == 0
    for j, block in enumerate(blocks):
        for k in range(block.shape[0]):
            low, high = block[k, 0, 0], block[k, 1, 0]
            straight = jnp.concatenate([low, high], axis=0)
            turned = jnp.concatenate([high, low], axis=0)
            outs[k // 2][j, k % 2] = jnp.where(is_low, straight, turned)


def pair_kernel(first, second, out):
    out[0] = first[...]
    out[1] = second[...]


SMALL = pltpu.CompilerParams(vmem_limit_bytes=1 << 20)


def paired(first, second):
    vmem = pl.BlockSpec(memory_space=pltpu.VMEM)
    return pl.pallas_call(
        pair_kernel,
        out_shape=jax.ShapeDtypeStruct((2,) + first.shape, F32),
        in_specs=[vmem] * 2,
        out_specs=vmem,
        compiler_params=SMALL,
    )(first, second)


def whole_kernel(devices, weights, derivative, *refs):
    (
        near, far, near_other, far_other, cross_ref, matrix_ref, pair_ref,
        vel_out, pre_out, res_out,
        u, v, xs, rm, w, dinv, z, r, y, s, p, x, flip, vel_own, pre_own, res_own, sems,
    ) = [refs[0:2], refs[2:4], refs[4:6], refs[6:8], *refs[8:]]
    my_y, my_z = lax.axis_index("gy"), lax.axis_index("gz")
    fields = u.shape[0]
    halves = range(u.shape[1])
    per_half = devices[0] // len(halves)
    lanes = Lanes((2 * devices[0], devices[1], 8))
    stiff_sum = np.sum(weights[:, None] * derivative * derivative, axis=0)
    slab_rows = [pl.ds(64 * a, 64) for a in range(8)]
    pair_rows = [[pl.ds(64 * a + 16 * j, 16) for a in range(8)] for j in range(4)]

    is_low = my_z == 0
    is_even = lax.axis_index("gx") % 2 == 0
    sublane = lax.broadcasted_iota(jnp.int32, (8, 128), 0)
    own_rows = (sublane < 4) == is_low
    entry = [my_y ^ j for j in range(devices[1])]

    def tile(near, far, k, ahead, at, cols):
        by_x = (near[0], 1) if k < 2 else (far[1], 0)
        diagonal = (far[k // 2], 1)
        if ahead == 0:
            ref, i = near[k // 2], 0
        elif ahead == 2:
            ref, i = (far[0], 0) if k < 2 else (near[1], 1)
        else:
            first, second = (by_x, diagonal) if ahead == 1 else (diagonal, by_x)
            first, second = (ref[i, at, k % 2, :, cols] for ref, i in (first, second))
            return jnp.where(is_even, first, second)
        return ref[i, at, k % 2, :, cols]

    def to_lanes(k, chunk):
        cols = pl.ds(128 * chunk, 128)
        parts = []
        for half in halves:
            tiles = []
            for i in range(per_half):
                first, second = [], []
                for at in entry:
                    here = tile(near, far, k, half * per_half + i, at, cols)
                    there = tile(near_other, far_other, k, half * per_half + i, at, cols)
                    first.append(jnp.where(own_rows, here, there))
                    second.append(pltpu.roll(jnp.where(own_rows, there, here), 4, 0))
                tiles += first + second
            parts.append(jnp.concatenate(tiles, axis=0).T)
        return parts

    def halves_of(parts, chunk):
        return {2 * chunk + i: [part[64 * i : 64 * i + 64] for part in parts] for i in range(2)}

    for k in range(fields):
        for chunks in ((0, 3), (1,), (2,)):
            slabs = {}
            for chunk in chunks:
                slabs.update(halves_of(to_lanes(k, chunk), chunk))
            settle(u.at[k], slabs, lanes, "avg", xs.at[k])

    for chunks in ((0, 3), (1,), (2,)):
        slabs = {}
        for chunk in chunks:
            for a, react in halves_of(to_lanes(fields, chunk), chunk).items():
                mass = cross_ref[pl.ds(0, 64), :] * float(weights[a])
                diag = cross_ref[pl.ds(0, 64), :] * float(stiff_sum[a])
                diag += cross_ref[pl.ds(64, 64), :] * float(weights[a])
                react = [part * mass for part in react]
                for h in halves:
                    rm[h, slab_rows[a], :] = react[h]
                slabs[a] = [part + diag for part in react]
        settle(dinv, slabs, lanes, "sum")

    up, low, _, _ = lanes.factors(2, "avg")
    share_z = jnp.where(sublane == 7, up, jnp.where(sublane == 0, low, 1.0))
    up, low, _, _ = lanes.factors(1, "avg")
    for b in range(8):
        share = share_z * (low if b == 0 else up) if b in (0, 7) else share_z
        for a in range(8):
            for h in halves:
                rows = pl.ds(64 * a + 8 * b, 8)
                inverse = 1.0 / dinv[h, rows, :]
                dinv[h, rows, :] = inverse
                w[h, rows, :] = inverse * (share * 0.5 if a in (0, 7) else share)

    def in_halves(g):
        return [g[:, 128 * h : 128 * (h + 1)] for h in halves]

    def product(row, count, k, a):
        high, low = xs[k, 0, slab_rows[a], :], xs[k, 1, slab_rows[a], :]
        parts = jnp.concatenate([high, low, high], axis=0)
        return in_halves(
            jnp.dot(matrix_ref[pl.ds(row, count), :], parts, preferred_element_type=F32)
        )

    def product_first(row, k, j):
        high, low = (
            jnp.concatenate([xs[k, i, pair_rows[j][a], :] for a in range(8)], axis=0)
            for i in range(2)
        )
        parts = jnp.concatenate([high, low, high], axis=0)
        g = in_halves(
            jnp.dot(pair_ref[pl.ds(row, 128), :], parts, preferred_element_type=F32)
        )
        return [[part[16 * a : 16 * a + 16] for part in g] for a in range(8)]

    now, after = u, v
    for _ in range(SUBSTEPS):
        for k in range(fields):
            for j in range(4):
                g = product_first(0, k, j)
                for a, rows in enumerate(pair_rows[j]):
                    for h in halves:
                        after[k, h, rows, :] = now[k, h, rows, :] - now[0, h, rows, :] * g[a][h]
            for group in SLAB_ORDER:
                slabs = {}
                for a in group:
                    g = product(0, 128, k, a)
                    slabs[a] = [
                        after[k, h, slab_rows[a], :]
                        - now[1, h, slab_rows[a], :] * g[h][:64]
                        - now[2, h, slab_rows[a], :] * g[h][64:]
                        for h in halves
                    ]
                settle(after.at[k], slabs, lanes, "wall", xs.at[k])
        now, after = after, now

    def own_block(source, own):
        flip[...] = source.T
        size = own.shape[2]
        for i in range(own.shape[0]):
            start = i * lanes.strides[0] + my_y * lanes.strides[1]
            block = flip[pl.ds(pl.multiple_of(start, 8), 8), :]
            own[i, 0] = jnp.where(is_low, block[:size], block[size:])

    for j in range(4):
        g = product_first(0, 0, j)
        for a, rows in enumerate(pair_rows[j]):
            for h in halves:
                r[h, rows, :] = g[a][h]
    for group in SLAB_ORDER:
        slabs = {}
        for a in group:
            second, third = product(0, 64, 1, a), product(64, 64, 2, a)
            mass = cross_ref[pl.ds(0, 64), :] * float(-weights[a] / step_size)
            slabs[a] = [
                mass * (r[h, slab_rows[a], :] + second[h] + third[h]) for h in halves
            ]
        settle(r, slabs, lanes, "sum")

    for k in range(fields):
        own_block(now[k, 0], vel_own.at[k])
    send_velocity = pltpu.make_async_copy(vel_own, vel_out, sems.at[0])
    send_velocity.start()

    def total(acc):
        return jnp.sum(jnp.sum(acc, axis=0, keepdims=True), axis=1, keepdims=True)

    def begin_sweep(update):
        acc = jnp.zeros((64, 128), F32)
        for a, rows in enumerate(slab_rows):
            for h in halves:
                res = r[h, rows, :]
                if update is not None:
                    alpha, beta = update
                    image = y[h, rows, :]
                    if beta is not None:
                        image = image + beta * s[h, rows, :]
                    s[h, rows, :] = image
                    res = res - alpha * image
                    r[h, rows, :] = res
                acc += res * res * w[h, rows, :]
                z[h, rows, :] = res * dinv[h, rows, :]
            store_split(xs.at[0], z, a)
        for j in range(4):
            g = product_first(128, 0, j)
            cross = cross_ref[pl.ds(16 * j, 16), :]
            for a, rows in enumerate(pair_rows[j]):
                for h in halves:
                    y[h, rows, :] = cross * g[a][h] + rm[h, rows, :] * z[h, rows, :]
        return total(acc)

    gamma = begin_sweep(None)
    alpha = beta = None
    for sweep in range(ITERS):
        acc = jnp.zeros((64, 128), F32)
        for group in SLAB_ORDER:
            slabs = {}
            for a in group:
                g = product(128 + 64 * min(a, 7 - a), 64, 0, a)
                slabs[a] = []
                for h in halves:
                    here = z[h, slab_rows[a], :]
                    image = y[h, slab_rows[a], :] + g[h]
                    acc += image * here
                    slabs[a].append(image)
            settle(y, slabs, lanes, "sum")
        delta = total(acc)
        if sweep:
            beta = gamma / gamma_before
            alpha = gamma / (delta - beta * gamma / alpha)
        else:
            alpha = gamma / delta
        for rows in slab_rows:
            search = z[0, rows, :]
            if sweep:
                search = search + beta * p[rows, :]
            p[rows, :] = search
            x[rows, :] = x[rows, :] + alpha * search if sweep else alpha * search
        if sweep < ITERS - 1:
            gamma_before, gamma = gamma, begin_sweep((alpha, beta))
    for rows in slab_rows:
        r[0, rows, :] -= alpha * (y[0, rows, :] + beta * s[0, rows, :])

    own_block(x[...], pre_own)
    send_pressure = pltpu.make_async_copy(pre_own, pre_out, sems.at[1])
    send_pressure.start()
    own_block(r[0], res_own)
    send_residual = pltpu.make_async_copy(res_own, res_out, sems.at[2])
    send_residual.start()
    send_velocity.wait()
    send_pressure.wait()
    send_residual.wait()


def whole_body(devices, velocity, reaction):
    fields = velocity.shape[0]
    lanes = int(np.prod(devices)) * 8
    weights, derivative = host_tables()
    eye = np.eye(8)
    stiffness = derivative.T @ (weights[:, None] * derivative)
    stiff_sum = np.sum(weights[:, None] * derivative * derivative, axis=0)
    across = np.kron(stiffness, np.diag(weights)) + np.kron(np.diag(weights), stiffness)
    matrices = np.concatenate(
        [
            split_matrix(step_size * np.kron(derivative, eye)),
            split_matrix(step_size * np.kron(eye, derivative)),
        ]
        + [split_matrix(weights[a] * across) for a in range(4)]
    )
    along = [step_size * derivative, stiffness]
    pairs = np.concatenate([split_matrix(np.kron(m, np.eye(16))) for m in along])
    cross = np.outer(weights, weights).reshape(-1)
    sides = np.outer(stiff_sum, weights).reshape(-1) + np.outer(weights, stiff_sum).reshape(-1)
    cross = np.broadcast_to(np.concatenate([cross, sides])[:, None], (128, 128))

    vmem = pl.BlockSpec(memory_space=pltpu.VMEM)
    hbm = pl.BlockSpec(memory_space=pltpu.HBM)
    def swapped(block, axis, mask):
        count = lax.axis_size(axis)
        return lax.ppermute(block, axis, [(i, i ^ mask) for i in range(count)])

    block = jnp.concatenate([velocity, reaction[None]], axis=0)
    column = jax.ShapeDtypeStruct((devices[1], 2, 8, 512), F32)
    first, second = pl.pallas_call(
        column_kernel,
        out_shape=[column, column],
        in_specs=[vmem] * devices[1],
        out_specs=[vmem, vmem],
        compiler_params=SMALL,
    )(block, *(swapped(block, "gy", mask) for mask in range(1, devices[1])))
    first_x, second_y = swapped(first, "gx", 1), swapped(second, "gx", 2)
    first_y, second_x = swapped(first, "gx", 2), swapped(second, "gx", 1)
    first_diagonal, second_diagonal = swapped(first_x, "gx", 2), swapped(second_y, "gx", 1)
    near = [paired(first, first_x), paired(second, second_y)]
    far = [paired(first_y, first_diagonal), paired(second_x, second_diagonal)]
    others = [swapped(pair, "gz", 1) for pair in (*near, *far)]

    field = pltpu.VMEM((lanes // 128, 512, 128), F32)
    three = pltpu.VMEM((fields, lanes // 128, 512, 128), F32)
    one_half = pltpu.VMEM((512, 128), F32)
    own = pltpu.VMEM(reaction.shape, F32)
    return pl.pallas_call(
        functools.partial(whole_kernel, devices, weights, derivative),
        out_shape=(
            jax.ShapeDtypeStruct(velocity.shape, F32),
            jax.ShapeDtypeStruct(reaction.shape, F32),
            jax.ShapeDtypeStruct(reaction.shape, F32),
        ),
        in_specs=[vmem] * 11,
        out_specs=(hbm, hbm, hbm),
        scratch_shapes=[three, three, pltpu.VMEM((fields, 2, 512, lanes), BF16)]
        + [field] * 7
        + [one_half] * 2
        + [
            pltpu.VMEM((128, 512), F32),
            pltpu.VMEM(velocity.shape, F32),
            own,
            own,
            pltpu.SemaphoreType.DMA((3,)),
        ],
        compiler_params=pltpu.CompilerParams(vmem_limit_bytes=40 << 20),
    )(
        *near, *far, *others, jnp.asarray(cross, F32), jnp.asarray(matrices), jnp.asarray(pairs),
    )


def extended(block, sides, width, periodic):
    for axis, dim in sides:
        count = lax.axis_size(axis)
        forward = [(i, i + 1) for i in range(count - 1)]
        if periodic:
            forward.append((count - 1, 0))
        backward = [(target, source) for source, target in forward]
        low = lax.ppermute(
            lax.slice_in_dim(block, block.shape[dim] - width, None, axis=dim), axis, forward
        )
        high = lax.ppermute(lax.slice_in_dim(block, 0, width, axis=dim), axis, backward)
        block = jnp.concatenate([low, block, high], axis=dim)
    return block


def derive(values, derivative, along_dim, transposed):
    layout = values.shape
    matrix = derivative.T if transposed else derivative
    blocks = values.reshape(-1, 8, 8, 8)
    patterns = ("aq,nqbc->nabc", "bq,naqc->nabc", "cq,nabq->nabc")
    result = jnp.einsum(patterns[along_dim], matrix, blocks, precision=lax.Precision.HIGHEST)
    return result.reshape(layout)


def place_face(values, target_axis, position, update):
    selector = tuple(
        (position if place == target_axis else slice(None) for place in range(values.ndim))
    )
    return values.at[selector].set(update)


def faces_along_x(sequence):
    return extended(sequence, (("gx", 0),), 1, True)


def faces_along_y(sequence):
    return extended(sequence, (("gy", 0),), 1, False)


def faces_along_z(sequence):
    return extended(sequence, (("gz", 0),), 1, False)


def join_faces(values, along_dim, exchanger):
    lower_face = jnp.moveaxis(jnp.take(values, 0, axis=4 + along_dim), 1 + along_dim, 0)
    upper_face = jnp.moveaxis(jnp.take(values, 7, axis=4 + along_dim), 1 + along_dim, 0)
    elements = lower_face.shape[0]
    face_shape = lower_face.shape
    sequence = jnp.stack([lower_face, upper_face], axis=1).reshape(2 * elements, -1)
    padded = exchanger(sequence)
    paired = padded.reshape(elements + 1, 2, -1)
    totals = paired[:, 0] + paired[:, 1]
    new_lower = jnp.moveaxis(totals[:-1].reshape(face_shape), 0, 1 + along_dim)
    new_upper = jnp.moveaxis(totals[1:].reshape(face_shape), 0, 1 + along_dim)
    values = place_face(values, 4 + along_dim, 0, new_lower)
    return place_face(values, 4 + along_dim, 7, new_upper)


def assemble(values):
    exchangers = (faces_along_x, faces_along_y, faces_along_z)
    dim_order = (0, 1, 2)
    for along_dim in dim_order:
        values = join_faces(values, along_dim, exchangers[along_dim])
    return values


def dim_factors(local_count, offset, total_count, bounded_by_walls):
    element_ids = offset + jnp.arange(local_count)
    node_ids = jnp.arange(8)
    at_end = (node_ids[None, :] == 0) | (node_ids[None, :] == 7)
    low_wall = (element_ids[:, None] == 0) & (node_ids[None, :] == 0)
    high_wall = (element_ids[:, None] == total_count - 1) & (node_ids[None, :] == 7)
    on_wall = (low_wall | high_wall) & bounded_by_walls
    shared = at_end & jnp.logical_not(on_wall)
    return (jnp.where(shared, 2.0, 1.0).astype(jnp.float32), on_wall.astype(jnp.float32))


def spread_body(velocity, reaction):
    weights, derivative = tables()
    count_x, count_y, count_z = (reaction.shape[0], reaction.shape[1], reaction.shape[2])
    speed = velocity.reshape(3, count_x, count_y, count_z, 8, 8, 8)
    react = reaction.reshape(1, count_x, count_y, count_z, 8, 8, 8)
    mass_matrix = weights[:, None, None] * weights[None, :, None] * weights[None, None, :]
    factor_x, wall_x = dim_factors(
        count_x, lax.axis_index("gx") * count_x, lax.axis_size("gx") * count_x, False
    )
    factor_y, wall_y = dim_factors(
        count_y, lax.axis_index("gy") * count_y, lax.axis_size("gy") * count_y, True
    )
    factor_z, wall_z = dim_factors(
        count_z, lax.axis_index("gz") * count_z, lax.axis_size("gz") * count_z, True
    )
    multiplicity = (
        factor_x[None, :, None, None, :, None, None]
        * factor_y[None, None, :, None, None, :, None]
        * factor_z[None, None, None, :, None, None, :]
    )
    interior = (1.0 - wall_y[None, None, :, None, None, :, None]) * (
        1.0 - wall_z[None, None, None, :, None, None, :]
    )
    stiff_sum = jnp.sum(weights[:, None] * derivative * derivative, axis=0)
    diag_local = (
        stiff_sum[:, None, None] * weights[None, :, None] * weights[None, None, :]
        + weights[:, None, None] * stiff_sum[None, :, None] * weights[None, None, :]
        + weights[:, None, None] * weights[None, :, None] * stiff_sum[None, None, :]
    )
    diag_terms = diag_local + react * mass_matrix
    speed = assemble(speed) / multiplicity
    diagonal = None
    for substep in range(SUBSTEPS):
        gradient_fields = [derive(speed, derivative, along_dim, False) for along_dim in range(3)]
        transport = (
            speed[0:1] * gradient_fields[0]
            + speed[1:2] * gradient_fields[1]
            + speed[2:3] * gradient_fields[2]
        )
        tendency = assemble(mass_matrix * transport) / (mass_matrix * multiplicity)
        speed = interior * (speed - step_size * tendency)
    spread = (
        derive(speed[0:1], derivative, 0, False)
        + derive(speed[1:2], derivative, 1, False)
        + derive(speed[2:3], derivative, 2, False)
    )
    source = -assemble(mass_matrix * spread)
    diagonal = assemble(diag_terms)

    def local_inner(first, second):
        return jnp.sum(first * second / multiplicity)

    def norm_weighted_mass(residual_vec, precond_vec):
        return lax.psum(local_inner(residual_vec, precond_vec), ("gx", "gy", "gz"))

    pressure = jnp.zeros_like(source)
    residual = source
    precond = residual / diagonal
    search = precond
    progress = norm_weighted_mass(residual, precond)
    for sweep_index in range(ITERS):
        local_sum = react * mass_matrix * search
        for apply_along_dim in range(3):
            local_sum = local_sum + derive(
                mass_matrix * derive(search, derivative, apply_along_dim, False),
                derivative,
                apply_along_dim,
                True,
            )
        applied = assemble(local_sum)
        step_length = progress / lax.psum(local_inner(search, applied), ("gx", "gy", "gz"))
        pressure = pressure + step_length * search
        residual = residual - step_length * applied
        precond = residual / diagonal
        progress_next = norm_weighted_mass(residual, precond)
        search = precond + progress_next / progress * search
        progress = progress_next
    return (
        speed.reshape(3, count_x, count_y, count_z, 512),
        pressure.reshape(count_x, count_y, count_z, 512),
        residual.reshape(count_x, count_y, count_z, 512),
    )


def solution(mesh):
    in_specs = (P(None, "gx", "gy", "gz", None), P("gx", "gy", "gz", None))
    out_specs = (
        P(None, "gx", "gy", "gz", None),
        P("gx", "gy", "gz", None),
        P("gx", "gy", "gz", None),
    )
    devices = tuple(mesh.shape[axis] for axis in ("gx", "gy", "gz"))

    def body(velocity, reaction):
        if devices == (4, 4, 2) and reaction.shape[:3] == (2, 1, 4):
            return whole_body(devices, velocity, reaction)
        return spread_body(velocity, reaction)

    return jax.shard_map(body, mesh=mesh, in_specs=in_specs, out_specs=out_specs, check_vma=False)
```

```python
import functools

import jax
import jax.numpy as jnp
import numpy as np
from jax import lax
from jax.experimental import pallas as pl
from jax.experimental.pallas import tpu as pltpu
from jax.sharding import PartitionSpec as P

SUBSTEPS = 2
ITERS = 4
step_size = 0.02

F32 = jnp.float32
BF16 = jnp.bfloat16


def legendre_seven(points):
    earlier = points * 0.0 + 1.0
    current = points
    for degree in range(1, 7):
        earlier, current = (
            current,
            ((2 * degree + 1) * points * current - degree * earlier) / (degree + 1),
        )
    return current


def host_tables():
    half = np.array([0.20929921790247888, 0.5917001814331423, 0.8717401485096066, 1.0])
    points = np.concatenate([-half[::-1], half])
    legendre = legendre_seven(points)
    weights = 2.0 / (56.0 * legendre**2)
    spacing = points[:, None] - points[None, :] + np.eye(8)
    derivative = legendre[:, None] / legendre[None, :] / spacing * (1.0 - np.eye(8))
    derivative[0, 0] = -14.0
    derivative[7, 7] = 14.0
    return weights, derivative


def tables():
    weights, derivative = host_tables()
    return (jnp.asarray(weights, F32), jnp.asarray(derivative, F32))


def split_matrix(matrix):
    matrix = matrix.astype(np.float32)
    high = matrix.astype(jnp.bfloat16)
    low = (matrix - high.astype(np.float32)).astype(jnp.bfloat16)
    return np.concatenate([high, high, low], axis=1)


def split_parts(values):
    high = values.astype(BF16)
    return high, (values - high.astype(F32)).astype(BF16)


def roll_lanes(parts, shift):
    turned = [pltpu.roll(part, shift, 1) for part in parts]
    lane = lax.broadcasted_iota(jnp.int32, parts[0].shape, 1)
    return [jnp.where(lane < shift, turned[i - 1], turned[i]) for i in range(len(parts))]


def roll_lanes_back(parts, shift):
    turned = [pltpu.roll(part, 128 - shift, 1) for part in parts]
    lane = lax.broadcasted_iota(jnp.int32, parts[0].shape, 1)
    count = len(parts)
    return [
        jnp.where(lane < 128 - shift, turned[i], turned[(i + 1) % count]) for i in range(count)
    ]


class Lanes:
    def __init__(self, counts):
        self.strides = (counts[1] * counts[2], counts[2], 1)
        lane = lax.broadcasted_iota(jnp.int32, (1, 128), 1)
        place = {1: (lane // counts[2]) % counts[1], 2: lane % counts[2]}
        self.has_next = {d: place[d] < counts[d] - 1 for d in (1, 2)}
        self.has_prev = {d: place[d] > 0 for d in (1, 2)}

    def factors(self, direction, mode):
        n, p = self.has_next[direction], self.has_prev[direction]
        if mode == "sum":
            return None, None, jnp.where(n, 1.0, 0.0), jnp.where(p, 1.0, 0.0)
        alone = 1.0 if mode == "avg" else 0.0
        return (
            jnp.where(n, 0.5, alone),
            jnp.where(p, 0.5, alone),
            jnp.where(n, 0.5, 0.0),
            jnp.where(p, 0.5, 0.0),
        )


def settle(ref, slabs, lanes, mode, split=None):
    if 0 in slabs:
        lower, upper = slabs[0], slabs[7]
        stride = lanes.strides[0]
        new_upper = [a + b for a, b in zip(upper, roll_lanes_back(lower, stride))]
        new_lower = [a + b for a, b in zip(lower, roll_lanes(upper, stride))]
        if mode != "sum":
            new_upper = [0.5 * a for a in new_upper]
            new_lower = [0.5 * a for a in new_lower]
        slabs = {**slabs, 0: new_lower, 7: new_upper}

    def joined(lower, upper, direction):
        stride = lanes.strides[direction]
        own_up, own_low, from_next, from_prev = lanes.factors(direction, mode)
        following, previous = pltpu.roll(lower, 128 - stride, 1), pltpu.roll(upper, stride, 1)
        if mode == "sum":
            return lower + previous * from_prev, upper + following * from_next
        if mode == "wall":
            return (lower + previous) * from_prev, (upper + following) * from_next
        return lower * own_low + previous * from_prev, upper * own_up + following * from_next

    for a, parts in slabs.items():
        for h, part in enumerate(parts):
            lower, upper = joined(part[:8], part[56:], 1)
            ref[h, pl.ds(64 * a, 8), :] = lower
            ref[h, pl.ds(64 * a + 8, 48), :] = part[8:56]
            ref[h, pl.ds(64 * a + 56, 8), :] = upper
            first, last = pl.ds(64 * a, 8, stride=8), pl.ds(64 * a + 7, 8, stride=8)
            lower, upper = joined(ref[h, first, :], ref[h, last, :], 2)
            ref[h, first, :] = lower
            ref[h, last, :] = upper
        if split is not None:
            store_split(split, ref, a)


def store_split(split, ref, a):
    rows = pl.ds(64 * a, 64)
    values = jnp.concatenate([ref[h, rows, :] for h in range(ref.shape[0])], axis=1)
    split[0, rows, :], split[1, rows, :] = split_parts(values)


SLAB_ORDER = ((0, 7), (1,), (2,), (3,), (4,), (5,), (6,))


def column_kernel(*refs):
    blocks, outs = refs[:-2], refs[-2:]
    is_low = lax.axis_index("gz") == 0
    for j, block in enumerate(blocks):
        for k in range(block.shape[0]):
            low, high = block[k, 0, 0], block[k, 1, 0]
            straight = jnp.concatenate([low, high], axis=0)
            turned = jnp.concatenate([high, low], axis=0)
            outs[k // 2][j, k % 2] = jnp.where(is_low, straight, turned)


def pair_kernel(first, second, out):
    out[0] = first[...]
    out[1] = second[...]


SMALL = pltpu.CompilerParams(vmem_limit_bytes=1 << 20)


def paired(first, second):
    vmem = pl.BlockSpec(memory_space=pltpu.VMEM)
    return pl.pallas_call(
        pair_kernel,
        out_shape=jax.ShapeDtypeStruct((2,) + first.shape, F32),
        in_specs=[vmem] * 2,
        out_specs=vmem,
        compiler_params=SMALL,
    )(first, second)


def whole_kernel(devices, weights, derivative, *refs):
    (
        near, far, near_other, far_other, cross_ref, matrix_ref, pair_ref,
        vel_out, pre_out, res_out,
        u, v, xs, rm, w, dinv, z, r, y, s, p, x, flip, vel_own, pre_own, res_own, sems,
    ) = [refs[0:2], refs[2:4], refs[4:6], refs[6:8], *refs[8:]]
    my_y, my_z = lax.axis_index("gy"), lax.axis_index("gz")
    fields = u.shape[0]
    halves = range(u.shape[1])
    per_half = devices[0] // len(halves)
    lanes = Lanes((2 * devices[0], devices[1], 8))
    stiff_sum = np.sum(weights[:, None] * derivative * derivative, axis=0)
    slab_rows = [pl.ds(64 * a, 64) for a in range(8)]
    pair_rows = [[pl.ds(64 * a + 16 * j, 16) for a in range(8)] for j in range(4)]

    is_low = my_z == 0
    is_even = lax.axis_index("gx") % 2 == 0
    sublane = lax.broadcasted_iota(jnp.int32, (8, 128), 0)
    own_rows = (sublane < 4) == is_low
    entry = [my_y ^ j for j in range(devices[1])]

    def tile(near, far, k, ahead, at, cols):
        by_x = (near[0], 1) if k < 2 else (far[0], 1)
        diagonal = (far[1], k // 2)
        if ahead == 0:
            ref, i = near[k // 2], 0
        elif ahead == 2:
            ref, i = (far[0], 0) if k < 2 else (near[1], 1)
        else:
            first, second = (by_x, diagonal) if ahead == 1 else (diagonal, by_x)
            first, second = (ref[i, at, k % 2, :, cols] for ref, i in (first, second))
            return jnp.where(is_even, first, second)
        return ref[i, at, k % 2, :, cols]

    def to_lanes(k, chunk):
        cols = pl.ds(128 * chunk, 128)
        parts = []
        for half in halves:
            tiles = []
            for i in range(per_half):
                first, second = [], []
                for at in entry:
                    here = tile(near, far, k, half * per_half + i, at, cols)
                    there = tile(near_other, far_other, k, half * per_half + i, at, cols)
                    first.append(jnp.where(own_rows, here, there))
                    second.append(pltpu.roll(jnp.where(own_rows, there, here), 4, 0))
                tiles += first + second
            parts.append(jnp.concatenate(tiles, axis=0).T)
        return parts

    def halves_of(parts, chunk):
        return {2 * chunk + i: [part[64 * i : 64 * i + 64] for part in parts] for i in range(2)}

    for k in range(fields):
        for chunks in ((0, 3), (1,), (2,)):
            slabs = {}
            for chunk in chunks:
                slabs.update(halves_of(to_lanes(k, chunk), chunk))
            settle(u.at[k], slabs, lanes, "avg", xs.at[k])

    for chunks in ((0, 3), (1,), (2,)):
        slabs = {}
        for chunk in chunks:
            for a, react in halves_of(to_lanes(fields, chunk), chunk).items():
                mass = cross_ref[pl.ds(0, 64), :] * float(weights[a])
                diag = cross_ref[pl.ds(0, 64), :] * float(stiff_sum[a])
                diag += cross_ref[pl.ds(64, 64), :] * float(weights[a])
                react = [part * mass for part in react]
                for h in halves:
                    rm[h, slab_rows[a], :] = react[h]
                slabs[a] = [part + diag for part in react]
        settle(dinv, slabs, lanes, "sum")

    up, low, _, _ = lanes.factors(2, "avg")
    share_z = jnp.where(sublane == 7, up, jnp.where(sublane == 0, low, 1.0))
    up, low, _, _ = lanes.factors(1, "avg")
    for b in range(8):
        share = share_z * (low if b == 0 else up) if b in (0, 7) else share_z
        for a in range(8):
            for h in halves:
                rows = pl.ds(64 * a + 8 * b, 8)
                inverse = 1.0 / dinv[h, rows, :]
                dinv[h, rows, :] = inverse
                w[h, rows, :] = inverse * (share * 0.5 if a in (0, 7) else share)

    def in_halves(g):
        return [g[:, 128 * h : 128 * (h + 1)] for h in halves]

    def product(row, count, k, a):
        high, low = xs[k, 0, slab_rows[a], :], xs[k, 1, slab_rows[a], :]
        parts = jnp.concatenate([high, low, high], axis=0)
        return in_halves(
            jnp.dot(matrix_ref[pl.ds(row, count), :], parts, preferred_element_type=F32)
        )

    def product_first(row, k, j):
        high, low = (
            jnp.concatenate([xs[k, i, pair_rows[j][a], :] for a in range(8)], axis=0)
            for i in range(2)
        )
        parts = jnp.concatenate([high, low, high], axis=0)
        g = in_halves(
            jnp.dot(pair_ref[pl.ds(row, 128), :], parts, preferred_element_type=F32)
        )
        return [[part[16 * a : 16 * a + 16] for part in g] for a in range(8)]

    now, after = u, v
    for _ in range(SUBSTEPS):
        for k in range(fields):
            for j in range(4):
                g = product_first(0, k, j)
                for a, rows in enumerate(pair_rows[j]):
                    for h in halves:
                        after[k, h, rows, :] = now[k, h, rows, :] - now[0, h, rows, :] * g[a][h]
            for group in SLAB_ORDER:
                slabs = {}
                for a in group:
                    g = product(0, 128, k, a)
                    slabs[a] = [
                        after[k, h, slab_rows[a], :]
                        - now[1, h, slab_rows[a], :] * g[h][:64]
                        - now[2, h, slab_rows[a], :] * g[h][64:]
                        for h in halves
                    ]
                settle(after.at[k], slabs, lanes, "wall", xs.at[k])
        now, after = after, now

    def own_block(source, own):
        flip[...] = source.T
        size = own.shape[2]
        for i in range(own.shape[0]):
            start = i * lanes.strides[0] + my_y * lanes.strides[1]
            block = flip[pl.ds(pl.multiple_of(start, 8), 8), :]
            own[i, 0] = jnp.where(is_low, block[:size], block[size:])

    for j in range(4):
        g = product_first(0, 0, j)
        for a, rows in enumerate(pair_rows[j]):
            for h in halves:
                r[h, rows, :] = g[a][h]
    for group in SLAB_ORDER:
        slabs = {}
        for a in group:
            second, third = product(0, 64, 1, a), product(64, 64, 2, a)
            mass = cross_ref[pl.ds(0, 64), :] * float(-weights[a] / step_size)
            slabs[a] = [
                mass * (r[h, slab_rows[a], :] + second[h] + third[h]) for h in halves
            ]
        settle(r, slabs, lanes, "sum")

    for k in range(fields):
        own_block(now[k, 0], vel_own.at[k])
    send_velocity = pltpu.make_async_copy(vel_own, vel_out, sems.at[0])
    send_velocity.start()

    def total(acc):
        return jnp.sum(jnp.sum(acc, axis=0, keepdims=True), axis=1, keepdims=True)

    def begin_sweep(update):
        acc = jnp.zeros((64, 128), F32)
        for a, rows in enumerate(slab_rows):
            for h in halves:
                res = r[h, rows, :]
                if update is not None:
                    alpha, beta = update
                    image = y[h, rows, :]
                    if beta is not None:
                        image = image + beta * s[h, rows, :]
                    s[h, rows, :] = image
                    res = res - alpha * image
                    r[h, rows, :] = res
                acc += res * res * w[h, rows, :]
                z[h, rows, :] = res * dinv[h, rows, :]
            store_split(xs.at[0], z, a)
        for j in range(4):
            g = product_first(128, 0, j)
            cross = cross_ref[pl.ds(16 * j, 16), :]
            for a, rows in enumerate(pair_rows[j]):
                for h in halves:
                    y[h, rows, :] = cross * g[a][h] + rm[h, rows, :] * z[h, rows, :]
        return total(acc)

    gamma = begin_sweep(None)
    alpha = beta = None
    for sweep in range(ITERS):
        acc = jnp.zeros((64, 128), F32)
        for group in SLAB_ORDER:
            slabs = {}
            for a in group:
                g = product(128 + 64 * min(a, 7 - a), 64, 0, a)
                slabs[a] = []
                for h in halves:
                    here = z[h, slab_rows[a], :]
                    image = y[h, slab_rows[a], :] + g[h]
                    acc += image * here
                    slabs[a].append(image)
            settle(y, slabs, lanes, "sum")
        delta = total(acc)
        if sweep:
            beta = gamma / gamma_before
            alpha = gamma / (delta - beta * gamma / alpha)
        else:
            alpha = gamma / delta
        for rows in slab_rows:
            search = z[0, rows, :]
            if sweep:
                search = search + beta * p[rows, :]
            p[rows, :] = search
            x[rows, :] = x[rows, :] + alpha * search if sweep else alpha * search
        if sweep < ITERS - 1:
            gamma_before, gamma = gamma, begin_sweep((alpha, beta))
    for rows in slab_rows:
        r[0, rows, :] -= alpha * (y[0, rows, :] + beta * s[0, rows, :])

    own_block(x[...], pre_own)
    send_pressure = pltpu.make_async_copy(pre_own, pre_out, sems.at[1])
    send_pressure.start()
    own_block(r[0], res_own)
    send_residual = pltpu.make_async_copy(res_own, res_out, sems.at[2])
    send_residual.start()
    send_velocity.wait()
    send_pressure.wait()
    send_residual.wait()


def whole_body(devices, velocity, reaction):
    fields = velocity.shape[0]
    lanes = int(np.prod(devices)) * 8
    weights, derivative = host_tables()
    eye = np.eye(8)
    stiffness = derivative.T @ (weights[:, None] * derivative)
    stiff_sum = np.sum(weights[:, None] * derivative * derivative, axis=0)
    across = np.kron(stiffness, np.diag(weights)) + np.kron(np.diag(weights), stiffness)
    matrices = np.concatenate(
        [
            split_matrix(step_size * np.kron(derivative, eye)),
            split_matrix(step_size * np.kron(eye, derivative)),
        ]
        + [split_matrix(weights[a] * across) for a in range(4)]
    )
    along = [step_size * derivative, stiffness]
    pairs = np.concatenate([split_matrix(np.kron(m, np.eye(16))) for m in along])
    cross = np.outer(weights, weights).reshape(-1)
    sides = np.outer(stiff_sum, weights).reshape(-1) + np.outer(weights, stiff_sum).reshape(-1)
    cross = np.broadcast_to(np.concatenate([cross, sides])[:, None], (128, 128))

    vmem = pl.BlockSpec(memory_space=pltpu.VMEM)
    hbm = pl.BlockSpec(memory_space=pltpu.HBM)
    def swapped(block, axis, mask):
        count = lax.axis_size(axis)
        return lax.ppermute(block, axis, [(i, i ^ mask) for i in range(count)])

    block = jnp.concatenate([velocity, reaction[None]], axis=0)
    column = jax.ShapeDtypeStruct((devices[1], 2, 8, 512), F32)
    first, second = pl.pallas_call(
        column_kernel,
        out_shape=[column, column],
        in_specs=[vmem] * devices[1],
        out_specs=[vmem, vmem],
        compiler_params=SMALL,
    )(block, *(swapped(block, "gy", mask) for mask in range(1, devices[1])))
    first_x, second_y = swapped(first, "gx", 1), swapped(second, "gx", 2)
    first_y, second_x = swapped(first, "gx", 2), swapped(second, "gx", 1)
    first_diagonal, second_diagonal = swapped(first_x, "gx", 2), swapped(second_y, "gx", 1)
    near = [paired(first, first_x), paired(second, second_y)]
    far = [paired(first_y, second_x), paired(first_diagonal, second_diagonal)]
    others = [swapped(pair, "gz", 1) for pair in (*near, *far)]

    field = pltpu.VMEM((lanes // 128, 512, 128), F32)
    three = pltpu.VMEM((fields, lanes // 128, 512, 128), F32)
    one_half = pltpu.VMEM((512, 128), F32)
    own = pltpu.VMEM(reaction.shape, F32)
    return pl.pallas_call(
        functools.partial(whole_kernel, devices, weights, derivative),
        out_shape=(
            jax.ShapeDtypeStruct(velocity.shape, F32),
            jax.ShapeDtypeStruct(reaction.shape, F32),
            jax.ShapeDtypeStruct(reaction.shape, F32),
        ),
        in_specs=[vmem] * 11,
        out_specs=(hbm, hbm, hbm),
        scratch_shapes=[three, three, pltpu.VMEM((fields, 2, 512, lanes), BF16)]
        + [field] * 7
        + [one_half] * 2
        + [
            pltpu.VMEM((128, 512), F32),
            pltpu.VMEM(velocity.shape, F32),
            own,
            own,
            pltpu.SemaphoreType.DMA((3,)),
        ],
        compiler_params=pltpu.CompilerParams(vmem_limit_bytes=40 << 20),
    )(
        *near, *far, *others, jnp.asarray(cross, F32), jnp.asarray(matrices), jnp.asarray(pairs),
    )


def extended(block, sides, width, periodic):
    for axis, dim in sides:
        count = lax.axis_size(axis)
        forward = [(i, i + 1) for i in range(count - 1)]
        if periodic:
            forward.append((count - 1, 0))
        backward = [(target, source) for source, target in forward]
        low = lax.ppermute(
            lax.slice_in_dim(block, block.shape[dim] - width, None, axis=dim), axis, forward
        )
        high = lax.ppermute(lax.slice_in_dim(block, 0, width, axis=dim), axis, backward)
        block = jnp.concatenate([low, block, high], axis=dim)
    return block


def derive(values, derivative, along_dim, transposed):
    layout = values.shape
    matrix = derivative.T if transposed else derivative
    blocks = values.reshape(-1, 8, 8, 8)
    patterns = ("aq,nqbc->nabc", "bq,naqc->nabc", "cq,nabq->nabc")
    result = jnp.einsum(patterns[along_dim], matrix, blocks, precision=lax.Precision.HIGHEST)
    return result.reshape(layout)


def place_face(values, target_axis, position, update):
    selector = tuple(
        (position if place == target_axis else slice(None) for place in range(values.ndim))
    )
    return values.at[selector].set(update)


def faces_along_x(sequence):
    return extended(sequence, (("gx", 0),), 1, True)


def faces_along_y(sequence):
    return extended(sequence, (("gy", 0),), 1, False)


def faces_along_z(sequence):
    return extended(sequence, (("gz", 0),), 1, False)


def join_faces(values, along_dim, exchanger):
    lower_face = jnp.moveaxis(jnp.take(values, 0, axis=4 + along_dim), 1 + along_dim, 0)
    upper_face = jnp.moveaxis(jnp.take(values, 7, axis=4 + along_dim), 1 + along_dim, 0)
    elements = lower_face.shape[0]
    face_shape = lower_face.shape
    sequence = jnp.stack([lower_face, upper_face], axis=1).reshape(2 * elements, -1)
    padded = exchanger(sequence)
    paired = padded.reshape(elements + 1, 2, -1)
    totals = paired[:, 0] + paired[:, 1]
    new_lower = jnp.moveaxis(totals[:-1].reshape(face_shape), 0, 1 + along_dim)
    new_upper = jnp.moveaxis(totals[1:].reshape(face_shape), 0, 1 + along_dim)
    values = place_face(values, 4 + along_dim, 0, new_lower)
    return place_face(values, 4 + along_dim, 7, new_upper)


def assemble(values):
    exchangers = (faces_along_x, faces_along_y, faces_along_z)
    dim_order = (0, 1, 2)
    for along_dim in dim_order:
        values = join_faces(values, along_dim, exchangers[along_dim])
    return values


def dim_factors(local_count, offset, total_count, bounded_by_walls):
    element_ids = offset + jnp.arange(local_count)
    node_ids = jnp.arange(8)
    at_end = (node_ids[None, :] == 0) | (node_ids[None, :] == 7)
    low_wall = (element_ids[:, None] == 0) & (node_ids[None, :] == 0)
    high_wall = (element_ids[:, None] == total_count - 1) & (node_ids[None, :] == 7)
    on_wall = (low_wall | high_wall) & bounded_by_walls
    shared = at_end & jnp.logical_not(on_wall)
    return (jnp.where(shared, 2.0, 1.0).astype(jnp.float32), on_wall.astype(jnp.float32))


def spread_body(velocity, reaction):
    weights, derivative = tables()
    count_x, count_y, count_z = (reaction.shape[0], reaction.shape[1], reaction.shape[2])
    speed = velocity.reshape(3, count_x, count_y, count_z, 8, 8, 8)
    react = reaction.reshape(1, count_x, count_y, count_z, 8, 8, 8)
    mass_matrix = weights[:, None, None] * weights[None, :, None] * weights[None, None, :]
    factor_x, wall_x = dim_factors(
        count_x, lax.axis_index("gx") * count_x, lax.axis_size("gx") * count_x, False
    )
    factor_y, wall_y = dim_factors(
        count_y, lax.axis_index("gy") * count_y, lax.axis_size("gy") * count_y, True
    )
    factor_z, wall_z = dim_factors(
        count_z, lax.axis_index("gz") * count_z, lax.axis_size("gz") * count_z, True
    )
    multiplicity = (
        factor_x[None, :, None, None, :, None, None]
        * factor_y[None, None, :, None, None, :, None]
        * factor_z[None, None, None, :, None, None, :]
    )
    interior = (1.0 - wall_y[None, None, :, None, None, :, None]) * (
        1.0 - wall_z[None, None, None, :, None, None, :]
    )
    stiff_sum = jnp.sum(weights[:, None] * derivative * derivative, axis=0)
    diag_local = (
        stiff_sum[:, None, None] * weights[None, :, None] * weights[None, None, :]
        + weights[:, None, None] * stiff_sum[None, :, None] * weights[None, None, :]
        + weights[:, None, None] * weights[None, :, None] * stiff_sum[None, None, :]
    )
    diag_terms = diag_local + react * mass_matrix
    speed = assemble(speed) / multiplicity
    diagonal = None
    for substep in range(SUBSTEPS):
        gradient_fields = [derive(speed, derivative, along_dim, False) for along_dim in range(3)]
        transport = (
            speed[0:1] * gradient_fields[0]
            + speed[1:2] * gradient_fields[1]
            + speed[2:3] * gradient_fields[2]
        )
        tendency = assemble(mass_matrix * transport) / (mass_matrix * multiplicity)
        speed = interior * (speed - step_size * tendency)
    spread = (
        derive(speed[0:1], derivative, 0, False)
        + derive(speed[1:2], derivative, 1, False)
        + derive(speed[2:3], derivative, 2, False)
    )
    source = -assemble(mass_matrix * spread)
    diagonal = assemble(diag_terms)

    def local_inner(first, second):
        return jnp.sum(first * second / multiplicity)

    def norm_weighted_mass(residual_vec, precond_vec):
        return lax.psum(local_inner(residual_vec, precond_vec), ("gx", "gy", "gz"))

    pressure = jnp.zeros_like(source)
    residual = source
    precond = residual / diagonal
    search = precond
    progress = norm_weighted_mass(residual, precond)
    for sweep_index in range(ITERS):
        local_sum = react * mass_matrix * search
        for apply_along_dim in range(3):
            local_sum = local_sum + derive(
                mass_matrix * derive(search, derivative, apply_along_dim, False),
                derivative,
                apply_along_dim,
                True,
            )
        applied = assemble(local_sum)
        step_length = progress / lax.psum(local_inner(search, applied), ("gx", "gy", "gz"))
        pressure = pressure + step_length * search
        residual = residual - step_length * applied
        precond = residual / diagonal
        progress_next = norm_weighted_mass(residual, precond)
        search = precond + progress_next / progress * search
        progress = progress_next
    return (
        speed.reshape(3, count_x, count_y, count_z, 512),
        pressure.reshape(count_x, count_y, count_z, 512),
        residual.reshape(count_x, count_y, count_z, 512),
    )


def solution(mesh):
    in_specs = (P(None, "gx", "gy", "gz", None), P("gx", "gy", "gz", None))
    out_specs = (
        P(None, "gx", "gy", "gz", None),
        P("gx", "gy", "gz", None),
        P("gx", "gy", "gz", None),
    )
    devices = tuple(mesh.shape[axis] for axis in ("gx", "gy", "gz"))

    def body(velocity, reaction):
        if devices == (4, 4, 2) and reaction.shape[:3] == (2, 1, 4):
            return whole_body(devices, velocity, reaction)
        return spread_body(velocity, reaction)

    return jax.shard_map(body, mesh=mesh, in_specs=in_specs, out_specs=out_specs, check_vma=False)
```

```python
import functools

import jax
import jax.numpy as jnp
import numpy as np
from jax import lax
from jax.experimental import pallas as pl
from jax.experimental.pallas import tpu as pltpu
from jax.sharding import PartitionSpec as P

SUBSTEPS = 2
ITERS = 4
step_size = 0.02

F32 = jnp.float32
BF16 = jnp.bfloat16


def legendre_seven(points):
    earlier = points * 0.0 + 1.0
    current = points
    for degree in range(1, 7):
        earlier, current = (
            current,
            ((2 * degree + 1) * points * current - degree * earlier) / (degree + 1),
        )
    return current


def host_tables():
    half = np.array([0.20929921790247888, 0.5917001814331423, 0.8717401485096066, 1.0])
    points = np.concatenate([-half[::-1], half])
    legendre = legendre_seven(points)
    weights = 2.0 / (56.0 * legendre**2)
    spacing = points[:, None] - points[None, :] + np.eye(8)
    derivative = legendre[:, None] / legendre[None, :] / spacing * (1.0 - np.eye(8))
    derivative[0, 0] = -14.0
    derivative[7, 7] = 14.0
    return weights, derivative


def tables():
    weights, derivative = host_tables()
    return (jnp.asarray(weights, F32), jnp.asarray(derivative, F32))


def split_matrix(matrix):
    matrix = matrix.astype(np.float32)
    high = matrix.astype(jnp.bfloat16)
    low = (matrix - high.astype(np.float32)).astype(jnp.bfloat16)
    return np.concatenate([high, high, low], axis=1)


def split_parts(values):
    high = values.astype(BF16)
    return high, (values - high.astype(F32)).astype(BF16)


def roll_lanes(parts, shift):
    turned = [pltpu.roll(part, shift, 1) for part in parts]
    lane = lax.broadcasted_iota(jnp.int32, parts[0].shape, 1)
    return [jnp.where(lane < shift, turned[i - 1], turned[i]) for i in range(len(parts))]


def roll_lanes_back(parts, shift):
    turned = [pltpu.roll(part, 128 - shift, 1) for part in parts]
    lane = lax.broadcasted_iota(jnp.int32, parts[0].shape, 1)
    count = len(parts)
    return [
        jnp.where(lane < 128 - shift, turned[i], turned[(i + 1) % count]) for i in range(count)
    ]


class Lanes:
    def __init__(self, counts):
        self.strides = (counts[1] * counts[2], counts[2], 1)
        lane = lax.broadcasted_iota(jnp.int32, (1, 128), 1)
        place = {1: (lane // counts[2]) % counts[1], 2: lane % counts[2]}
        self.has_next = {d: place[d] < counts[d] - 1 for d in (1, 2)}
        self.has_prev = {d: place[d] > 0 for d in (1, 2)}

    def factors(self, direction, mode):
        n, p = self.has_next[direction], self.has_prev[direction]
        if mode == "sum":
            return None, None, jnp.where(n, 1.0, 0.0), jnp.where(p, 1.0, 0.0)
        alone = 1.0 if mode == "avg" else 0.0
        return (
            jnp.where(n, 0.5, alone),
            jnp.where(p, 0.5, alone),
            jnp.where(n, 0.5, 0.0),
            jnp.where(p, 0.5, 0.0),
        )


def settle(ref, slabs, lanes, mode, split=None):
    if 0 in slabs:
        lower, upper = slabs[0], slabs[7]
        stride = lanes.strides[0]
        new_upper = [a + b for a, b in zip(upper, roll_lanes_back(lower, stride))]
        new_lower = [a + b for a, b in zip(lower, roll_lanes(upper, stride))]
        if mode != "sum":
            new_upper = [0.5 * a for a in new_upper]
            new_lower = [0.5 * a for a in new_lower]
        slabs = {**slabs, 0: new_lower, 7: new_upper}

    def joined(lower, upper, direction):
        stride = lanes.strides[direction]
        own_up, own_low, from_next, from_prev = lanes.factors(direction, mode)
        following, previous = pltpu.roll(lower, 128 - stride, 1), pltpu.roll(upper, stride, 1)
        if mode == "sum":
            return lower + previous * from_prev, upper + following * from_next
        if mode == "wall":
            return (lower + previous) * from_prev, (upper + following) * from_next
        return lower * own_low + previous * from_prev, upper * own_up + following * from_next

    for a, parts in slabs.items():
        for h, part in enumerate(parts):
            lower, upper = joined(part[:8], part[56:], 1)
            ref[h, pl.ds(64 * a, 8), :] = lower
            ref[h, pl.ds(64 * a + 8, 48), :] = part[8:56]
            ref[h, pl.ds(64 * a + 56, 8), :] = upper
            first, last = pl.ds(64 * a, 8, stride=8), pl.ds(64 * a + 7, 8, stride=8)
            lower, upper = joined(ref[h, first, :], ref[h, last, :], 2)
            ref[h, first, :] = lower
            ref[h, last, :] = upper
        if split is not None:
            store_split(split, ref, a)


def store_split(split, ref, a):
    rows = pl.ds(64 * a, 64)
    values = jnp.concatenate([ref[h, rows, :] for h in range(ref.shape[0])], axis=1)
    split[0, rows, :], split[1, rows, :] = split_parts(values)


SLAB_ORDER = ((0, 7), (1,), (2,), (3,), (4,), (5,), (6,))


def column_kernel(*refs):
    blocks, outs = refs[:-2], refs[-2:]
    is_low = lax.axis_index("gz") == 0
    for j, block in enumerate(blocks):
        for k in range(block.shape[0]):
            low, high = block[k, 0, 0], block[k, 1, 0]
            straight = jnp.concatenate([low, high], axis=0)
            turned = jnp.concatenate([high, low], axis=0)
            outs[k // 2][j, k % 2] = jnp.where(is_low, straight, turned)


def pair_kernel(first, second, out):
    out[0] = first[...]
    out[1] = second[...]


SMALL = pltpu.CompilerParams(vmem_limit_bytes=1 << 20)


def paired(first, second):
    vmem = pl.BlockSpec(memory_space=pltpu.VMEM)
    return pl.pallas_call(
        pair_kernel,
        out_shape=jax.ShapeDtypeStruct((2,) + first.shape, F32),
        in_specs=[vmem] * 2,
        out_specs=vmem,
        compiler_params=SMALL,
    )(first, second)


def whole_kernel(devices, weights, derivative, *refs):
    (
        near, far, near_other, far_other, cross_ref, matrix_ref, pair_ref,
        vel_out, pre_out, res_out,
        u, v, xs, rm, w, dinv, z, r, y, s, p, x, flip, vel_own, pre_own, res_own, sems,
    ) = [refs[0:2], refs[2:5], refs[5:7], refs[7:10], *refs[10:]]
    my_y, my_z = lax.axis_index("gy"), lax.axis_index("gz")
    fields = u.shape[0]
    halves = range(u.shape[1])
    per_half = devices[0] // len(halves)
    lanes = Lanes((2 * devices[0], devices[1], 8))
    stiff_sum = np.sum(weights[:, None] * derivative * derivative, axis=0)
    slab_rows = [pl.ds(64 * a, 64) for a in range(8)]
    pair_rows = [[pl.ds(64 * a + 16 * j, 16) for a in range(8)] for j in range(4)]

    is_low = my_z == 0
    is_even = lax.axis_index("gx") % 2 == 0
    sublane = lax.broadcasted_iota(jnp.int32, (8, 128), 0)
    own_rows = (sublane < 4) == is_low
    entry = [my_y ^ j for j in range(devices[1])]

    def tile(near, far, k, ahead, at, cols):
        if ahead == 0:
            return near[k // 2][0, at, k % 2, :, cols]
        if ahead == 2:
            ref, i = (far[0], 0) if k < 2 else (near[1], 1)
            return ref[i, at, k % 2, :, cols]
        ref = near[0] if k < 2 else far[0]
        by_x, diagonal = ref[1, at, k % 2, :, cols], far[1 + k // 2][at, k % 2, :, cols]
        if ahead == 1:
            return jnp.where(is_even, by_x, diagonal)
        return jnp.where(is_even, diagonal, by_x)

    def to_lanes(k, chunk):
        cols = pl.ds(128 * chunk, 128)
        parts = []
        for half in halves:
            tiles = []
            for i in range(per_half):
                first, second = [], []
                for at in entry:
                    here = tile(near, far, k, half * per_half + i, at, cols)
                    there = tile(near_other, far_other, k, half * per_half + i, at, cols)
                    first.append(jnp.where(own_rows, here, there))
                    second.append(pltpu.roll(jnp.where(own_rows, there, here), 4, 0))
                tiles += first + second
            parts.append(jnp.concatenate(tiles, axis=0).T)
        return parts

    def halves_of(parts, chunk):
        return {2 * chunk + i: [part[64 * i : 64 * i + 64] for part in parts] for i in range(2)}

    for k in range(fields):
        for chunks in ((0, 3), (1,), (2,)):
            slabs = {}
            for chunk in chunks:
                slabs.update(halves_of(to_lanes(k, chunk), chunk))
            settle(u.at[k], slabs, lanes, "avg", xs.at[k])

    for chunks in ((0, 3), (1,), (2,)):
        slabs = {}
        for chunk in chunks:
            for a, react in halves_of(to_lanes(fields, chunk), chunk).items():
                mass = cross_ref[pl.ds(0, 64), :] * float(weights[a])
                diag = cross_ref[pl.ds(0, 64), :] * float(stiff_sum[a])
                diag += cross_ref[pl.ds(64, 64), :] * float(weights[a])
                react = [part * mass for part in react]
                for h in halves:
                    rm[h, slab_rows[a], :] = react[h]
                slabs[a] = [part + diag for part in react]
        settle(dinv, slabs, lanes, "sum")

    up, low, _, _ = lanes.factors(2, "avg")
    share_z = jnp.where(sublane == 7, up, jnp.where(sublane == 0, low, 1.0))
    up, low, _, _ = lanes.factors(1, "avg")
    for b in range(8):
        share = share_z * (low if b == 0 else up) if b in (0, 7) else share_z
        for a in range(8):
            for h in halves:
                rows = pl.ds(64 * a + 8 * b, 8)
                inverse = 1.0 / dinv[h, rows, :]
                dinv[h, rows, :] = inverse
                w[h, rows, :] = inverse * (share * 0.5 if a in (0, 7) else share)

    def in_halves(g):
        return [g[:, 128 * h : 128 * (h + 1)] for h in halves]

    def product(row, count, k, a):
        high, low = xs[k, 0, slab_rows[a], :], xs[k, 1, slab_rows[a], :]
        parts = jnp.concatenate([high, low, high], axis=0)
        return in_halves(
            jnp.dot(matrix_ref[pl.ds(row, count), :], parts, preferred_element_type=F32)
        )

    def product_first(row, k, j):
        high, low = (
            jnp.concatenate([xs[k, i, pair_rows[j][a], :] for a in range(8)], axis=0)
            for i in range(2)
        )
        parts = jnp.concatenate([high, low, high], axis=0)
        g = in_halves(
            jnp.dot(pair_ref[pl.ds(row, 128), :], parts, preferred_element_type=F32)
        )
        return [[part[16 * a : 16 * a + 16] for part in g] for a in range(8)]

    now, after = u, v
    for _ in range(SUBSTEPS):
        for k in range(fields):
            for j in range(4):
                g = product_first(0, k, j)
                for a, rows in enumerate(pair_rows[j]):
                    for h in halves:
                        after[k, h, rows, :] = now[k, h, rows, :] - now[0, h, rows, :] * g[a][h]
            for group in SLAB_ORDER:
                slabs = {}
                for a in group:
                    g = product(0, 128, k, a)
                    slabs[a] = [
                        after[k, h, slab_rows[a], :]
                        - now[1, h, slab_rows[a], :] * g[h][:64]
                        - now[2, h, slab_rows[a], :] * g[h][64:]
                        for h in halves
                    ]
                settle(after.at[k], slabs, lanes, "wall", xs.at[k])
        now, after = after, now

    def own_block(source, own):
        flip[...] = source.T
        size = own.shape[2]
        for i in range(own.shape[0]):
            start = i * lanes.strides[0] + my_y * lanes.strides[1]
            block = flip[pl.ds(pl.multiple_of(start, 8), 8), :]
            own[i, 0] = jnp.where(is_low, block[:size], block[size:])

    for j in range(4):
        g = product_first(0, 0, j)
        for a, rows in enumerate(pair_rows[j]):
            for h in halves:
                r[h, rows, :] = g[a][h]
    for group in SLAB_ORDER:
        slabs = {}
        for a in group:
            second, third = product(0, 64, 1, a), product(64, 64, 2, a)
            mass = cross_ref[pl.ds(0, 64), :] * float(-weights[a] / step_size)
            slabs[a] = [
                mass * (r[h, slab_rows[a], :] + second[h] + third[h]) for h in halves
            ]
        settle(r, slabs, lanes, "sum")

    for k in range(fields):
        own_block(now[k, 0], vel_own.at[k])
    send_velocity = pltpu.make_async_copy(vel_own, vel_out, sems.at[0])
    send_velocity.start()

    def total(acc):
        return jnp.sum(jnp.sum(acc, axis=0, keepdims=True), axis=1, keepdims=True)

    def begin_sweep(update):
        acc = jnp.zeros((64, 128), F32)
        for a, rows in enumerate(slab_rows):
            for h in halves:
                res = r[h, rows, :]
                if update is not None:
                    alpha, beta = update
                    image = y[h, rows, :]
                    if beta is not None:
                        image = image + beta * s[h, rows, :]
                    s[h, rows, :] = image
                    res = res - alpha * image
                    r[h, rows, :] = res
                acc += res * res * w[h, rows, :]
                z[h, rows, :] = res * dinv[h, rows, :]
            store_split(xs.at[0], z, a)
        for j in range(4):
            g = product_first(128, 0, j)
            cross = cross_ref[pl.ds(16 * j, 16), :]
            for a, rows in enumerate(pair_rows[j]):
                for h in halves:
                    y[h, rows, :] = cross * g[a][h] + rm[h, rows, :] * z[h, rows, :]
        return total(acc)

    gamma = begin_sweep(None)
    alpha = beta = None
    for sweep in range(ITERS):
        acc = jnp.zeros((64, 128), F32)
        for group in SLAB_ORDER:
            slabs = {}
            for a in group:
                g = product(128 + 64 * min(a, 7 - a), 64, 0, a)
                slabs[a] = []
                for h in halves:
                    here = z[h, slab_rows[a], :]
                    image = y[h, slab_rows[a], :] + g[h]
                    acc += image * here
                    slabs[a].append(image)
            settle(y, slabs, lanes, "sum")
        delta = total(acc)
        if sweep:
            beta = gamma / gamma_before
            alpha = gamma / (delta - beta * gamma / alpha)
        else:
            alpha = gamma / delta
        for rows in slab_rows:
            search = z[0, rows, :]
            if sweep:
                search = search + beta * p[rows, :]
            p[rows, :] = search
            x[rows, :] = x[rows, :] + alpha * search if sweep else alpha * search
        if sweep < ITERS - 1:
            gamma_before, gamma = gamma, begin_sweep((alpha, beta))
    for rows in slab_rows:
        r[0, rows, :] -= alpha * (y[0, rows, :] + beta * s[0, rows, :])

    own_block(x[...], pre_own)
    send_pressure = pltpu.make_async_copy(pre_own, pre_out, sems.at[1])
    send_pressure.start()
    own_block(r[0], res_own)
    send_residual = pltpu.make_async_copy(res_own, res_out, sems.at[2])
    send_residual.start()
    send_velocity.wait()
    send_pressure.wait()
    send_residual.wait()


def whole_body(devices, velocity, reaction):
    fields = velocity.shape[0]
    lanes = int(np.prod(devices)) * 8
    weights, derivative = host_tables()
    eye = np.eye(8)
    stiffness = derivative.T @ (weights[:, None] * derivative)
    stiff_sum = np.sum(weights[:, None] * derivative * derivative, axis=0)
    across = np.kron(stiffness, np.diag(weights)) + np.kron(np.diag(weights), stiffness)
    matrices = np.concatenate(
        [
            split_matrix(step_size * np.kron(derivative, eye)),
            split_matrix(step_size * np.kron(eye, derivative)),
        ]
        + [split_matrix(weights[a] * across) for a in range(4)]
    )
    along = [step_size * derivative, stiffness]
    pairs = np.concatenate([split_matrix(np.kron(m, np.eye(16))) for m in along])
    cross = np.outer(weights, weights).reshape(-1)
    sides = np.outer(stiff_sum, weights).reshape(-1) + np.outer(weights, stiff_sum).reshape(-1)
    cross = np.broadcast_to(np.concatenate([cross, sides])[:, None], (128, 128))

    vmem = pl.BlockSpec(memory_space=pltpu.VMEM)
    hbm = pl.BlockSpec(memory_space=pltpu.HBM)
    def swapped(block, axis, mask):
        count = lax.axis_size(axis)
        return lax.ppermute(block, axis, [(i, i ^ mask) for i in range(count)])

    block = jnp.concatenate([velocity, reaction[None]], axis=0)
    column = jax.ShapeDtypeStruct((devices[1], 2, 8, 512), F32)
    first, second = pl.pallas_call(
        column_kernel,
        out_shape=[column, column],
        in_specs=[vmem] * devices[1],
        out_specs=[vmem, vmem],
        compiler_params=SMALL,
    )(block, *(swapped(block, "gy", mask) for mask in range(1, devices[1])))
    first_x, second_y = swapped(first, "gx", 1), swapped(second, "gx", 2)
    first_y, second_x = swapped(first, "gx", 2), swapped(second, "gx", 1)
    first_diagonal, second_diagonal = swapped(first_x, "gx", 2), swapped(second_y, "gx", 1)
    near = [paired(first, first_x), paired(second, second_y)]
    far = [paired(first_y, second_x), first_diagonal, second_diagonal]
    others = [swapped(pair, "gz", 1) for pair in (*near, *far)]

    field = pltpu.VMEM((lanes // 128, 512, 128), F32)
    three = pltpu.VMEM((fields, lanes // 128, 512, 128), F32)
    one_half = pltpu.VMEM((512, 128), F32)
    own = pltpu.VMEM(reaction.shape, F32)
    return pl.pallas_call(
        functools.partial(whole_kernel, devices, weights, derivative),
        out_shape=(
            jax.ShapeDtypeStruct(velocity.shape, F32),
            jax.ShapeDtypeStruct(reaction.shape, F32),
            jax.ShapeDtypeStruct(reaction.shape, F32),
        ),
        in_specs=[vmem] * 13,
        out_specs=(hbm, hbm, hbm),
        scratch_shapes=[three, three, pltpu.VMEM((fields, 2, 512, lanes), BF16)]
        + [field] * 7
        + [one_half] * 2
        + [
            pltpu.VMEM((128, 512), F32),
            pltpu.VMEM(velocity.shape, F32),
            own,
            own,
            pltpu.SemaphoreType.DMA((3,)),
        ],
        compiler_params=pltpu.CompilerParams(vmem_limit_bytes=40 << 20),
    )(
        *near, *far, *others, jnp.asarray(cross, F32), jnp.asarray(matrices), jnp.asarray(pairs),
    )


def extended(block, sides, width, periodic):
    for axis, dim in sides:
        count = lax.axis_size(axis)
        forward = [(i, i + 1) for i in range(count - 1)]
        if periodic:
            forward.append((count - 1, 0))
        backward = [(target, source) for source, target in forward]
        low = lax.ppermute(
            lax.slice_in_dim(block, block.shape[dim] - width, None, axis=dim), axis, forward
        )
        high = lax.ppermute(lax.slice_in_dim(block, 0, width, axis=dim), axis, backward)
        block = jnp.concatenate([low, block, high], axis=dim)
    return block


def derive(values, derivative, along_dim, transposed):
    layout = values.shape
    matrix = derivative.T if transposed else derivative
    blocks = values.reshape(-1, 8, 8, 8)
    patterns = ("aq,nqbc->nabc", "bq,naqc->nabc", "cq,nabq->nabc")
    result = jnp.einsum(patterns[along_dim], matrix, blocks, precision=lax.Precision.HIGHEST)
    return result.reshape(layout)


def place_face(values, target_axis, position, update):
    selector = tuple(
        (position if place == target_axis else slice(None) for place in range(values.ndim))
    )
    return values.at[selector].set(update)


def faces_along_x(sequence):
    return extended(sequence, (("gx", 0),), 1, True)


def faces_along_y(sequence):
    return extended(sequence, (("gy", 0),), 1, False)


def faces_along_z(sequence):
    return extended(sequence, (("gz", 0),), 1, False)


def join_faces(values, along_dim, exchanger):
    lower_face = jnp.moveaxis(jnp.take(values, 0, axis=4 + along_dim), 1 + along_dim, 0)
    upper_face = jnp.moveaxis(jnp.take(values, 7, axis=4 + along_dim), 1 + along_dim, 0)
    elements = lower_face.shape[0]
    face_shape = lower_face.shape
    sequence = jnp.stack([lower_face, upper_face], axis=1).reshape(2 * elements, -1)
    padded = exchanger(sequence)
    paired = padded.reshape(elements + 1, 2, -1)
    totals = paired[:, 0] + paired[:, 1]
    new_lower = jnp.moveaxis(totals[:-1].reshape(face_shape), 0, 1 + along_dim)
    new_upper = jnp.moveaxis(totals[1:].reshape(face_shape), 0, 1 + along_dim)
    values = place_face(values, 4 + along_dim, 0, new_lower)
    return place_face(values, 4 + along_dim, 7, new_upper)


def assemble(values):
    exchangers = (faces_along_x, faces_along_y, faces_along_z)
    dim_order = (0, 1, 2)
    for along_dim in dim_order:
        values = join_faces(values, along_dim, exchangers[along_dim])
    return values


def dim_factors(local_count, offset, total_count, bounded_by_walls):
    element_ids = offset + jnp.arange(local_count)
    node_ids = jnp.arange(8)
    at_end = (node_ids[None, :] == 0) | (node_ids[None, :] == 7)
    low_wall = (element_ids[:, None] == 0) & (node_ids[None, :] == 0)
    high_wall = (element_ids[:, None] == total_count - 1) & (node_ids[None, :] == 7)
    on_wall = (low_wall | high_wall) & bounded_by_walls
    shared = at_end & jnp.logical_not(on_wall)
    return (jnp.where(shared, 2.0, 1.0).astype(jnp.float32), on_wall.astype(jnp.float32))


def spread_body(velocity, reaction):
    weights, derivative = tables()
    count_x, count_y, count_z = (reaction.shape[0], reaction.shape[1], reaction.shape[2])
    speed = velocity.reshape(3, count_x, count_y, count_z, 8, 8, 8)
    react = reaction.reshape(1, count_x, count_y, count_z, 8, 8, 8)
    mass_matrix = weights[:, None, None] * weights[None, :, None] * weights[None, None, :]
    factor_x, wall_x = dim_factors(
        count_x, lax.axis_index("gx") * count_x, lax.axis_size("gx") * count_x, False
    )
    factor_y, wall_y = dim_factors(
        count_y, lax.axis_index("gy") * count_y, lax.axis_size("gy") * count_y, True
    )
    factor_z, wall_z = dim_factors(
        count_z, lax.axis_index("gz") * count_z, lax.axis_size("gz") * count_z, True
    )
    multiplicity = (
        factor_x[None, :, None, None, :, None, None]
        * factor_y[None, None, :, None, None, :, None]
        * factor_z[None, None, None, :, None, None, :]
    )
    interior = (1.0 - wall_y[None, None, :, None, None, :, None]) * (
        1.0 - wall_z[None, None, None, :, None, None, :]
    )
    stiff_sum = jnp.sum(weights[:, None] * derivative * derivative, axis=0)
    diag_local = (
        stiff_sum[:, None, None] * weights[None, :, None] * weights[None, None, :]
        + weights[:, None, None] * stiff_sum[None, :, None] * weights[None, None, :]
        + weights[:, None, None] * weights[None, :, None] * stiff_sum[None, None, :]
    )
    diag_terms = diag_local + react * mass_matrix
    speed = assemble(speed) / multiplicity
    diagonal = None
    for substep in range(SUBSTEPS):
        gradient_fields = [derive(speed, derivative, along_dim, False) for along_dim in range(3)]
        transport = (
            speed[0:1] * gradient_fields[0]
            + speed[1:2] * gradient_fields[1]
            + speed[2:3] * gradient_fields[2]
        )
        tendency = assemble(mass_matrix * transport) / (mass_matrix * multiplicity)
        speed = interior * (speed - step_size * tendency)
    spread = (
        derive(speed[0:1], derivative, 0, False)
        + derive(speed[1:2], derivative, 1, False)
        + derive(speed[2:3], derivative, 2, False)
    )
    source = -assemble(mass_matrix * spread)
    diagonal = assemble(diag_terms)

    def local_inner(first, second):
        return jnp.sum(first * second / multiplicity)

    def norm_weighted_mass(residual_vec, precond_vec):
        return lax.psum(local_inner(residual_vec, precond_vec), ("gx", "gy", "gz"))

    pressure = jnp.zeros_like(source)
    residual = source
    precond = residual / diagonal
    search = precond
    progress = norm_weighted_mass(residual, precond)
    for sweep_index in range(ITERS):
        local_sum = react * mass_matrix * search
        for apply_along_dim in range(3):
            local_sum = local_sum + derive(
                mass_matrix * derive(search, derivative, apply_along_dim, False),
                derivative,
                apply_along_dim,
                True,
            )
        applied = assemble(local_sum)
        step_length = progress / lax.psum(local_inner(search, applied), ("gx", "gy", "gz"))
        pressure = pressure + step_length * search
        residual = residual - step_length * applied
        precond = residual / diagonal
        progress_next = norm_weighted_mass(residual, precond)
        search = precond + progress_next / progress * search
        progress = progress_next
    return (
        speed.reshape(3, count_x, count_y, count_z, 512),
        pressure.reshape(count_x, count_y, count_z, 512),
        residual.reshape(count_x, count_y, count_z, 512),
    )


def solution(mesh):
    in_specs = (P(None, "gx", "gy", "gz", None), P("gx", "gy", "gz", None))
    out_specs = (
        P(None, "gx", "gy", "gz", None),
        P("gx", "gy", "gz", None),
        P("gx", "gy", "gz", None),
    )
    devices = tuple(mesh.shape[axis] for axis in ("gx", "gy", "gz"))

    def body(velocity, reaction):
        if devices == (4, 4, 2) and reaction.shape[:3] == (2, 1, 4):
            return whole_body(devices, velocity, reaction)
        return spread_body(velocity, reaction)

    return jax.shard_map(body, mesh=mesh, in_specs=in_specs, out_specs=out_specs, check_vma=False)
```
